32 devices in a mesh: seq: 4 (over y, x), tok: 8 (over z, core).
Axes of the slice: x: 2, y: 2, z: 4, core: 2. Of those that a mesh axis runs over, the one named last changes fastest.
Arguments:
- tokens: bfloat16 [4, 2048, 2048], P('seq', 'tok'), may hold values from -6 to 6
- source_ids: int32 [4], P('seq'), may hold values from 0 to 7
- loss_weights: float32 [8], replicated, may hold values from 0.5 to 2
- grad_output: bfloat16 [4, 2048, 2048], P('seq', 'tok'), may hold values from -6 to 6
- first_gain: bfloat16 [2048], P(('seq', 'tok')), may hold values from 0.5 to 1.5
- input_weight: bfloat16 [2048, 2560], P(('seq', 'tok')), may hold values from -0.125 to 0.125
- gelu_weight: bfloat16 [2048, 2560], P(('seq', 'tok')), may hold values from -0.125 to 0.125
- conv_weight: bfloat16 [2560, 4], P(('seq', 'tok')), may hold values from -3 to 3
- conv_bias: bfloat16 [2560], P(('seq', 'tok')), may hold values from -3 to 3
- decay_gate: bfloat16 [2560, 256], P(('seq', 'tok')), may hold values from -0.375 to 0.375
- decay_bias: bfloat16 [2560], P(('seq', 'tok')), may hold values from -3 to 3
- input_gate: bfloat16 [2560, 256], P(('seq', 'tok')), may hold values from -0.375 to 0.375
- input_bias: bfloat16 [2560], P(('seq', 'tok')), may hold values from -3 to 3
- decay_param: bfloat16 [2560], P(('seq', 'tok')), may hold values from -13 to -4
- output_weight: bfloat16 [2560, 2048], P(('seq', 'tok')), may hold values from -0.3125 to 0.3125
- second_gain: bfloat16 [2048], P(('seq', 'tok')), may hold values from 0.5 to 1.5
- gate_weight: bfloat16 [2048, 6144], P(('seq', 'tok')), may hold values from -0.125 to 0.125
- up_weight: bfloat16 [2048, 6144], P(('seq', 'tok')), may hold values from -0.125 to 0.125
- down_weight: bfloat16 [6144, 2048], P(('seq', 'tok')), may hold values from -0.15625 to 0.15625
Outputs:
- block_out: bfloat16 [4, 2048, 2048], P('seq', 'tok')
- grad_tokens: float32 [4, 2048, 2048], P('seq', 'tok')
- grad_first_gain: float32 [2048], P(('seq', 'tok'))
- grad_input_weight: float32 [2048, 2560], P(('seq', 'tok'))
- grad_gelu_weight: float32 [2048, 2560], P(('seq', 'tok'))
- grad_conv_weight: float32 [2560, 4], P(('seq', 'tok'))
- grad_conv_bias: float32 [2560], P(('seq', 'tok'))
- grad_decay_gate: float32 [2560, 256], P(('seq', 'tok'))
- grad_decay_bias: float32 [2560], P(('seq', 'tok'))
- grad_input_gate: float32 [2560, 256], P(('seq', 'tok'))
- grad_input_bias: float32 [2560], P(('seq', 'tok'))
- grad_decay_param: float32 [2560], P(('seq', 'tok'))
- grad_output_weight: float32 [2560, 2048], P(('seq', 'tok'))
- grad_second_gain: float32 [2048], P(('seq', 'tok'))
- grad_gate_weight: float32 [2048, 6144], P(('seq', 'tok'))
- grad_up_weight: float32 [2048, 6144], P(('seq', 'tok'))
- grad_down_weight: float32 [6144, 2048], P(('seq', 'tok'))
The draws below stay inside these ranges and needn't reach their ends.
Inputs may be any that keep to these rules, and one draw needn't show every extreme that they name: `source_ids`: each sequence's source, which selects its entry of loss_weights.
All inputs are finite; a program needn't handle non-finite values.
Results may differ from the reference program's by a relative error of at most 0.0094.
Values may be sent and summed in bfloat16 or wider, within the bound.
A program may use at most 448 MiB of HBM per device.

```python
import math
import jax
import jax.numpy as jnp
from jax import lax

D = 2048
R = 2560
FF = 6144
BW = 256
CONV = 4
SOURCES = 8
HEADS = 10
LENGTH = 2048
SEQS = 4


def draw_decay_param(key, part):
    key = jax.random.fold_in(key, 11)
    floor_log = jnp.log(0.05 / LENGTH)
    ceiling_log = jnp.log(0.008)
    rates = jnp.exp(jax.random.uniform(key, (R,), jnp.float32, floor_log, ceiling_log))
    return jnp.log(jnp.expm1(rates)).astype(jnp.bfloat16)


def touch_ends(array, rng, low, largest):
    dims = array.shape
    index_at = [jax.random.randint(jax.random.fold_in(rng, axis), (), 0, dims[axis]) for axis in range(len(dims))]
    array = array.at[tuple(index_at)].set(low)
    longest = dims.index(max(dims))
    index_at[longest] = (index_at[longest] + 1) % dims[longest]
    return array.at[tuple(index_at)].set(largest)


def block_scale(own_key, dims, shards, least, top_value):
    loudness, own = 1.0, jax.random.fold_in(own_key, 6)
    for position, blocks in shards:
        heights = jnp.exp(jax.random.uniform(jax.random.fold_in(own, position), (blocks,), jnp.float32, least / len(shards), top_value / len(shards)))
        loudness = loudness * jnp.repeat(heights, dims[position] // blocks).reshape([-1 if axis == position else 1 for axis in range(len(dims))])
    return loudness


def gaussian(rng, extent, width, most, shards=(), kind=jnp.bfloat16):
    drawn = jax.random.normal(rng, extent, jnp.float32) * width
    if len(shards) > 0:
        drawn = block_scale(rng, extent, shards, -0.22, 0.18) * drawn
    return jnp.clip(drawn, min=-most, max=most).astype(kind)


def setup_inputs(seed: int = 0) -> dict:
    arg_keys = jax.random.split(jax.random.key(seed), 20)
    tokens = gaussian(arg_keys[0], (SEQS, LENGTH, D), 1.0, 6.0, ((0, 4), (1, 8)))
    source_ids = touch_ends(jax.random.randint(arg_keys[1], (SEQS,), 0, SOURCES), jax.random.fold_in(arg_keys[1], 1), 0, SOURCES - 1).astype(jnp.int32)
    loss_weights = jnp.clip(jnp.exp(jax.random.uniform(arg_keys[2], (SOURCES,), jnp.float32, math.log(0.5), math.log(2.0))), 0.5, 2.0)
    grad_output = gaussian(arg_keys[3], (SEQS, LENGTH, D), 1.0, 6.0, ((0, 4), (1, 8)))
    first_gain = jnp.clip(1.0 + 0.1 * jax.random.normal(arg_keys[4], (D,), jnp.float32), 0.5, 1.5).astype(jnp.bfloat16)
    input_weight = gaussian(arg_keys[5], (D, R), D ** -0.5, 0.125, ((0, 32),))
    gelu_weight = gaussian(arg_keys[6], (D, R), D ** -0.5, 0.125, ((0, 32),))
    conv_weight = gaussian(arg_keys[7], (R, CONV), CONV ** -0.5, 3.0, ((0, 32),))
    conv_bias = gaussian(arg_keys[8], (R,), 0.5, 3.0, ((0, 32),))
    decay_gate = gaussian(arg_keys[9], (R, BW), BW ** -0.5, 0.375, ((0, 32),))
    decay_bias = gaussian(arg_keys[10], (R,), 0.5, 3.0, ((0, 32),))
    input_gate = gaussian(arg_keys[11], (R, BW), BW ** -0.5, 0.375, ((0, 32),))
    input_bias = gaussian(arg_keys[12], (R,), 0.5, 3.0, ((0, 32),))
    decay_param = draw_decay_param(jax.random.fold_in(arg_keys[19], 71), 0)
    output_weight = gaussian(arg_keys[14], (R, D), (R // 8) ** -0.5, 0.3125, ((0, 32),))
    second_gain = jnp.clip(1.0 + 0.1 * jax.random.normal(arg_keys[15], (D,), jnp.float32), 0.5, 1.5).astype(jnp.bfloat16)
    gate_weight = gaussian(arg_keys[16], (D, FF), D ** -0.5, 0.125, ((0, 32),))
    up_weight = gaussian(arg_keys[17], (D, FF), D ** -0.5, 0.125, ((0, 32),))
    down_weight = gaussian(arg_keys[18], (FF, D), (FF // 4) ** -0.5, 0.15625, ((0, 32),))
    return dict(tokens=tokens, source_ids=source_ids, loss_weights=loss_weights, grad_output=grad_output, first_gain=first_gain, input_weight=input_weight, gelu_weight=gelu_weight, conv_weight=conv_weight, conv_bias=conv_bias, decay_gate=decay_gate, decay_bias=decay_bias, input_gate=input_gate, input_bias=input_bias, decay_param=decay_param, output_weight=output_weight, second_gain=second_gain, gate_weight=gate_weight, up_weight=up_weight, down_weight=down_weight)


@jax.custom_vjp
def low(v):
    return lax.optimization_barrier(v.astype(jnp.bfloat16)).astype(jnp.float32)

@jax.custom_vjp
def low_back(v):
    return v

def low_keep(v):
    return (low(v), None)

def low_pass(kept, grad):
    return (grad,)

def back_keep(v):
    return (v, None)

def back_low(kept, grad):
    return (low(grad),)
low.defvjp(low_keep, low_pass)
low_back.defvjp(back_keep, back_low)
highest = lax.Precision.HIGHEST
eps = 1e-06

def rms_scale(value, gain):
    return value * lax.rsqrt(lax.optimization_barrier(jnp.mean(value * value, axis=-1, keepdims=True)) + eps) * gain

def gelu(value):
    return jax.nn.gelu(value, approximate=True)

def matmul(left, right):
    return jnp.einsum('std,de->ste', left, right, precision=highest)

def combine(earlier, later):
    return (earlier[0] * later[0], later[0] * earlier[1] + later[1])

def block_gate(conv_low, weights, bias):
    seqs, length = (conv_low.shape[0], conv_low.shape[1])
    shaped = conv_low.reshape(seqs, length, HEADS, BW)
    result = jnp.einsum('sthi,hij->sthj', shaped, weights.reshape(HEADS, BW, BW), precision=highest)
    return result.reshape(seqs, length, R) + bias

def forward(inputs, first_gain, input_weight, gelu_weight, conv_weight, conv_bias, decay_gate, decay_bias, input_gate, input_bias, decay_param, output_weight, second_gain, gate_weight, up_weight, down_weight):
    length = inputs.shape[1]
    normed = low(rms_scale(inputs, first_gain))
    branch_x = low_back(low(matmul(normed, input_weight)))
    branch_y = low_back(matmul(normed, gelu_weight))
    padded = jnp.pad(branch_x, ((0, 0), (CONV - 1, 0), (0, 0)))
    conv_out = conv_bias + jnp.zeros_like(branch_x)
    for offset in range(CONV):
        conv_out = conv_out + padded[:, offset:offset + length, :] * conv_weight[:, offset]
    conv_low = low(conv_out)
    gate_pre = low_back(block_gate(conv_low, decay_gate, decay_bias))
    input_pre = low_back(block_gate(conv_low, input_gate, input_bias))
    decay_log = -8.0 * jax.nn.sigmoid(gate_pre) * jax.nn.softplus(decay_param)
    inject = jnp.sqrt(-jnp.expm1(2.0 * decay_log)) * jax.nn.sigmoid(input_pre) * conv_low
    states = lax.associative_scan(combine, (jnp.exp(decay_log), inject), axis=1)[1]
    mixed = low(states * gelu(branch_y))
    resid = inputs + low_back(matmul(mixed, output_weight))
    second_normed = low(rms_scale(resid, second_gain))
    gate_val = low_back(matmul(second_normed, gate_weight))
    up_val = low_back(matmul(second_normed, up_weight))
    hidden = low(gelu(gate_val) * up_val)
    return resid + low_back(matmul(hidden, down_weight))

def reference(tokens, source_ids, loss_weights, grad_output, first_gain, input_weight, gelu_weight, conv_weight, conv_bias, decay_gate, decay_bias, input_gate, input_bias, decay_param, output_weight, second_gain, gate_weight, up_weight, down_weight):
    params = [weight.astype(jnp.float32) for weight in (first_gain, input_weight, gelu_weight, conv_weight, conv_bias, decay_gate, decay_bias, input_gate, input_bias, decay_param, output_weight, second_gain, gate_weight, up_weight, down_weight)]
    inputs = tokens.astype(jnp.float32)
    result, pullback = jax.vjp(forward, inputs, *params)
    sources = jnp.arange(SOURCES, dtype=jnp.int32)
    picked = lax.optimization_barrier(jnp.sum(jnp.where(source_ids[:, None] == sources[None, :], loss_weights[None, :], 0.0), axis=1))
    cotangent = grad_output.astype(jnp.float32) * picked[:, None, None]
    grad_tokens, grad_first_gain, grad_input_weight, grad_gelu_weight, grad_conv_weight, grad_conv_bias, grad_decay_gate, grad_decay_bias, grad_input_gate, grad_input_bias, grad_decay_param, grad_output_weight, grad_second_gain, grad_gate_weight, grad_up_weight, grad_down_weight = pullback(cotangent)
    return (result.astype(jnp.bfloat16), grad_tokens, grad_first_gain, grad_input_weight, grad_gelu_weight, grad_conv_weight, grad_conv_bias, grad_decay_gate, grad_decay_bias, grad_input_gate, grad_input_bias, grad_decay_param, grad_output_weight, grad_second_gain, grad_gate_weight, grad_up_weight, grad_down_weight)
```

```python
import jax
import jax.numpy as jnp
from jax import lax
from jax.sharding import PartitionSpec as P

BW = 256
CONV = 4
SMALL = 128
BF = jnp.bfloat16
F32 = jnp.float32
eps = 1e-06


def from_behind(block, axis, distance):
    devices = range(lax.axis_size(axis))
    route = [(i - distance, i) for i in devices if i - distance in devices]
    return lax.ppermute(block, axis, route)


def entering(value, axis, join, neutral, backward):
    count, mine = (lax.axis_size(axis), lax.axis_index(axis))
    pieces = jax.tree.map(lambda part: lax.all_gather(part, axis), value)
    if backward:
        pieces = jax.tree.map(lambda part: part[::-1], pieces)
        mine = count - 1 - mine
    total = jax.tree.map(
        lambda part, zero: jnp.full_like(part, 0) + jnp.asarray(zero, part.dtype), value, neutral
    )

    def turn(position, total):
        longer = join(total, jax.tree.map(lambda part: part[position], pieces))
        return jax.tree.map(lambda new, old: jnp.where(position < mine, new, old), longer, total)

    return lax.fori_loop(0, count - 1, turn, total)


def gelu(value):
    return jax.nn.gelu(value, approximate=True)


def rms_scale(value, gain):
    return value * lax.rsqrt(jnp.mean(value * value, axis=-1, keepdims=True) + eps) * gain


def combine(earlier, later):
    return (earlier[0] * later[0], later[0] * earlier[1] + later[1])


def gelu_product(gate_val, up_val):
    return gelu(gate_val) * up_val


def recur_inputs(gate_pre, input_pre, conv_vals, decay_param):
    decay_log = -8.0 * jax.nn.sigmoid(gate_pre) * jax.nn.softplus(decay_param)
    inject = jnp.sqrt(-jnp.expm1(2.0 * decay_log)) * jax.nn.sigmoid(input_pre) * conv_vals
    return (jnp.exp(decay_log), inject)


def forward_product(left, weight):
    return jnp.dot(left, weight, preferred_element_type=F32)


def back_product(grad, weight):
    return lax.dot_general(grad, weight, (((2,), (1,)), ((), ())), preferred_element_type=F32)


def token_product(left, grad):
    return lax.dot_general(left, grad, (((0, 1), (0, 1)), ((), ())), preferred_element_type=F32)


def split_blocks(value):
    return value.reshape(value.shape[:-1] + (value.shape[-1] // BW, BW))


def block_gate(conv_low, weights, bias):
    result = jnp.einsum(
        "sthi,hij->sthj", split_blocks(conv_low), weights.reshape(-1, BW, BW), preferred_element_type=F32
    )
    return result.reshape(conv_low.shape) + bias


def block_gate_back(grad_low, weights):
    result = jnp.einsum(
        "sthj,hij->sthi", split_blocks(grad_low), weights.reshape(-1, BW, BW), preferred_element_type=F32
    )
    return result.reshape(grad_low.shape)


def block_gate_weight(conv_low, grad_low):
    result = jnp.einsum(
        "sthi,sthj->hij", split_blocks(conv_low), split_blocks(grad_low), preferred_element_type=F32
    )
    return result.reshape(-1, BW)


def to_seq(parts):
    return lax.all_to_all(parts, "seq", split_axis=0, concat_axis=0, tiled=True)


def gather(value, axis):
    return lax.all_gather(value, axis, axis=0, tiled=True)


def scatter(value, axis):
    return lax.psum_scatter(value.astype(BF), axis, scatter_dimension=0, tiled=True)


def body(
    tokens,
    source_ids,
    loss_weights,
    grad_output,
    first_gain,
    input_weight,
    gelu_weight,
    conv_weight,
    conv_bias,
    decay_gate,
    decay_bias,
    input_gate,
    input_bias,
    decay_param,
    output_weight,
    second_gain,
    gate_weight,
    up_weight,
    down_weight,
):
    S, T = lax.axis_size("seq"), lax.axis_size("tok")
    me = lax.axis_index("seq")
    length, D = tokens.shape[1:]
    ds, R = input_weight.shape
    rs = output_weight.shape[0]
    F = gate_weight.shape[1]
    FQ = F // S
    heads = R // BW
    starts = [-(-i * heads // S) for i in range(S + 1)]
    C = max(starts[i + 1] - starts[i] for i in range(S)) * BW
    quarter = R // S
    offs = [starts[i] * BW - i * quarter for i in range(S)] + [0]
    most = max(offs)
    off = sum(jnp.where(me == i, offs[i], 0) for i in range(S))
    own = sum(jnp.where(me == i, (starts[i + 1] - starts[i]) * BW, 0) for i in range(S))

    def cols_for(w):
        parts = [w[:, starts[i] * BW : starts[i + 1] * BW] for i in range(S)]
        return jnp.stack([jnp.pad(p, ((0, 0), (0, C - p.shape[1]))) for p in parts])

    def d_rows(w):
        w = gather(w[None], "tok")
        return jnp.swapaxes(w, 0, 1).reshape((D, w.shape[-1]))

    gains = jnp.pad(jnp.stack([first_gain, second_gain], axis=1), ((0, 0), (0, SMALL - 2)))
    pack_in = jnp.concatenate(
        [cols_for(input_weight), cols_for(gelu_weight), jnp.broadcast_to(gains, (S,) + gains.shape)], axis=2
    )
    pack_in = d_rows(to_seq(pack_in))
    weight_in, weight_gelu = pack_in[:, :C], pack_in[:, C : 2 * C]
    gain_one, gain_two = pack_in[:, 2 * C].astype(F32), pack_in[:, 2 * C + 1].astype(F32)
    small = jnp.concatenate(
        [conv_weight, jnp.stack([conv_bias, decay_bias, input_bias, decay_param], axis=1)], axis=1
    )
    small = jnp.pad(small, ((0, 0), (0, SMALL - small.shape[1])))
    pack_r = gather(jnp.concatenate([output_weight, decay_gate, input_gate, small], axis=1), "tok")
    lent = from_behind(pack_r[:most], "seq", -1)
    pack_r = jnp.concatenate([pack_r, lent, jnp.zeros_like(lent)], axis=0)
    pack_r = lax.dynamic_slice_in_dim(pack_r, off, C, axis=0)
    pack_r = jnp.where(lax.broadcasted_iota(jnp.int32, pack_r.shape, 0) < own, pack_r, 0)
    weight_out = pack_r[:, :D]
    weight_decay, weight_input = pack_r[:, D : D + BW], pack_r[:, D + BW : D + 2 * BW]
    rows = pack_r[:, D + 2 * BW :].T.astype(F32)
    conv_float, bias_conv, bias_decay, bias_input, param = rows[:CONV], rows[4], rows[5], rows[6], rows[7]

    pack_f = jnp.stack([w.reshape(ds, S, FQ).swapaxes(0, 1) for w in (gate_weight, up_weight)])
    pack_f = lax.all_to_all(pack_f, "seq", split_axis=1, concat_axis=1, tiled=True)
    pack_f = gather(pack_f[None], "tok")
    pack_f = pack_f.transpose(1, 2, 0, 3, 4).reshape(2, D, FQ)
    weight_gate, weight_up = pack_f[0], pack_f[1]
    weight_down = gather(down_weight, "tok")

    inputs = tokens.astype(F32)
    everyone = gather(tokens, "seq").astype(F32)
    normed = rms_scale(everyone, gain_one).astype(BF)
    branch_x = forward_product(normed, weight_in).astype(BF)
    branch_y = forward_product(normed, weight_gelu)
    previous = from_behind(branch_x[:, length - (CONV - 1) :, :], "tok", 1)
    extended = jnp.concatenate([previous, branch_x], axis=1)
    conv_out = bias_conv + jnp.zeros(branch_x.shape, F32)
    for k in range(CONV):
        conv_out = conv_out + extended[:, k : k + length, :].astype(F32) * conv_float[k]
    conv_low = conv_out.astype(BF)
    conv_vals = conv_low.astype(F32)
    gate_pre = block_gate(conv_low, weight_decay, bias_decay)
    input_pre = block_gate(conv_low, weight_input, bias_input)
    decays, inject = recur_inputs(gate_pre, input_pre, conv_vals, param)
    cum_decay, local_state = lax.associative_scan(combine, (decays, inject), axis=1)
    ones, zeros = jnp.ones((S, C), F32), jnp.zeros((S, C), F32)
    incoming = entering(
        (cum_decay[:, -1, :], local_state[:, -1, :]), "tok", combine, (ones, zeros), False
    )[1]
    states = local_state + cum_decay * incoming[:, None, :]
    gated = gelu(branch_y)
    mixed = (states * gated).astype(BF)
    resid = inputs + scatter(forward_product(mixed, weight_out), "seq").astype(F32)
    second_own = rms_scale(resid, gain_two).astype(BF)
    second_normed = gather(second_own, "seq")
    sources = lax.broadcasted_iota(jnp.int32, (1, loss_weights.shape[0]), 1)
    picked = jnp.sum(jnp.where(source_ids[:, None] == sources, loss_weights[None, :], 0.0), axis=1)
    cotangent = grad_output.astype(F32) * picked[:, None, None]
    cot_low = gather(cotangent.astype(BF), "seq")

    gate_val = forward_product(second_normed, weight_gate)
    up_val = forward_product(second_normed, weight_up)
    hidden = gelu_product(gate_val, up_val).astype(BF)
    block_out = (resid + scatter(forward_product(hidden, weight_down), "seq").astype(F32)).astype(BF)

    grad_hidden = back_product(cot_low, weight_down)
    _, hidden_pull = jax.vjp(gelu_product, gate_val, up_val)
    grad_gate_val, grad_up_val = hidden_pull(grad_hidden)
    grad_gate_low, grad_up_low = grad_gate_val.astype(BF), grad_up_val.astype(BF)
    grad_second = back_product(grad_gate_low, weight_gate) + back_product(grad_up_low, weight_up)
    grad_second = scatter(grad_second, "seq").astype(F32)
    grad_down = scatter(token_product(hidden, cot_low), "tok").astype(F32)

    def d_scatter(g):
        cols = g.shape[-1]
        g = g.reshape((S, T, ds, cols)).swapaxes(0, 1).astype(BF).reshape(D, cols)
        return to_seq(scatter(g, "tok").reshape(S, ds, cols))

    def whole_rows(parts):
        return parts.swapaxes(0, 1).reshape(ds, F).astype(F32)

    grad_gate_w = whole_rows(d_scatter(token_product(second_normed, grad_gate_low)))
    grad_up_w = whole_rows(d_scatter(token_product(second_normed, grad_up_low)))

    _, second_pull = jax.vjp(rms_scale, resid, gain_two)
    grad_resid_norm, grad_gain_two = second_pull(grad_second)
    grad_resid = cotangent + grad_resid_norm
    resid_low = gather(grad_resid.astype(BF), "seq")

    grad_out_w = token_product(mixed, resid_low)
    grad_mixed = back_product(resid_low, weight_out)
    grad_local = grad_mixed * gated
    _, gelu_pull = jax.vjp(gelu, branch_y)
    grad_y_low = gelu_pull(grad_mixed * states)[0].astype(BF)
    next_decay = jnp.concatenate([decays[:, 1:, :], jnp.ones((S, 1, C), F32)], axis=1)
    reach, local_adjoint = lax.associative_scan(combine, (next_decay, grad_local), axis=1, reverse=True)
    first_adjoint = decays[:, 0, :] * local_adjoint[:, 0, :]
    carry_in = entering((cum_decay[:, -1, :], first_adjoint), "tok", combine, (ones, zeros), True)[1]
    grad_states = local_adjoint + reach * carry_in[:, None, :]
    prev_states = jnp.concatenate([incoming[:, None, :], states[:, :-1, :]], axis=1)
    _, recur_pull = jax.vjp(recur_inputs, gate_pre, input_pre, conv_vals, param)
    grad_gate_pre, grad_input_pre, grad_conv, grad_param = recur_pull((grad_states * prev_states, grad_states))
    gate_low, input_low = grad_gate_pre.astype(BF), grad_input_pre.astype(BF)
    grad_decay_b = jnp.sum(gate_low.astype(F32), axis=(0, 1))
    grad_input_b = jnp.sum(input_low.astype(F32), axis=(0, 1))
    grad_decay_w = block_gate_weight(conv_low, gate_low)
    grad_input_w = block_gate_weight(conv_low, input_low)
    grad_conv = grad_conv + block_gate_back(gate_low, weight_decay) + block_gate_back(input_low, weight_input)
    grad_conv_b = jnp.sum(grad_conv, axis=(0, 1))
    taps = []
    grad_extended = jnp.zeros((S, length + CONV - 1, C), F32)
    for k in range(CONV):
        taps.append(jnp.sum(grad_conv * extended[:, k : k + length, :].astype(F32), axis=(0, 1)))
        grad_extended = grad_extended + jnp.pad(
            grad_conv * conv_float[k], ((0, 0), (k, CONV - 1 - k), (0, 0))
        )
    rim = from_behind(grad_extended[:, : CONV - 1, :], "tok", -1)
    grad_branch_x = grad_extended[:, CONV - 1 :, :] + jnp.pad(rim, ((0, 0), (length - (CONV - 1), 0), (0, 0)))
    grad_x_low = grad_branch_x.astype(BF)
    grad_in_w = token_product(normed, grad_x_low)
    grad_gelu_w = token_product(normed, grad_y_low)
    grad_normed = back_product(grad_x_low, weight_in) + back_product(grad_y_low, weight_gelu)
    grad_normed = scatter(grad_normed, "seq").astype(F32)
    _, first_pull = jax.vjp(rms_scale, inputs, gain_one)
    grad_inputs_norm, grad_gain_one = first_pull(grad_normed)
    grad_tokens = grad_resid + grad_inputs_norm

    smalls = jnp.stack(taps + [grad_conv_b, grad_decay_b, grad_input_b, grad_param], axis=1)
    smalls = jnp.pad(smalls, ((0, 0), (0, SMALL - smalls.shape[1])))
    grad_r = jnp.concatenate([grad_out_w, grad_decay_w, grad_input_w, smalls], axis=1).astype(BF)
    grad_r = lax.dynamic_update_slice_in_dim(
        jnp.zeros((quarter + 2 * most, grad_r.shape[1]), BF), grad_r, off, axis=0
    )
    back = from_behind(grad_r[quarter : quarter + most], "seq", 1)
    keep = lax.broadcasted_iota(jnp.int32, (quarter, 1), 0) < off
    grad_r = jnp.where(keep, jnp.pad(back, ((0, quarter - most), (0, 0))), grad_r[:quarter])
    grad_r = scatter(grad_r, "tok").astype(F32)
    gain_grads = jnp.pad(jnp.stack([grad_gain_one, grad_gain_two], axis=1), ((0, 0), (0, SMALL - 2)))
    grad_i = d_scatter(jnp.concatenate([grad_in_w, grad_gelu_w, gain_grads], axis=1)).astype(F32)
    gain_grads = jnp.sum(grad_i[:, :, 2 * C :], axis=0)

    def columns(at):
        return jnp.concatenate(
            [grad_i[i, :, at : at + (starts[i + 1] - starts[i]) * BW] for i in range(S)], axis=1
        )

    smalls = grad_r[:, D + 2 * BW :]
    return (
        block_out,
        grad_tokens,
        gain_grads[:, 0],
        columns(0),
        columns(C),
        smalls[:, :CONV],
        smalls[:, 4],
        grad_r[:, D : D + BW],
        smalls[:, 5],
        grad_r[:, D + BW : D + 2 * BW],
        smalls[:, 6],
        smalls[:, 7],
        grad_r[:, :D],
        gain_grads[:, 1],
        grad_gate_w,
        grad_up_w,
        grad_down,
    )


def solution(mesh):
    one, two = P(("seq", "tok")), P(("seq", "tok"), None)
    data = P("seq", "tok", None)
    return jax.shard_map(
        body,
        mesh=mesh,
        in_specs=(data, P("seq"), P(), data, one, two, two, two, one, two, one, two, one, one, two, one, two, two, two),
        out_specs=(data, data, one, two, two, two, one, two, one, two, one, one, two, one, two, two, two),
        check_vma=False,
    )
```

```python
import functools

import jax
import jax.numpy as jnp
from jax import lax
from jax.experimental import pallas as pl
from jax.experimental.pallas import tpu as pltpu
from jax.sharding import PartitionSpec as P

BW = 256
CONV = 4
SMALL = 128
BF = jnp.bfloat16
F32 = jnp.float32
eps = 1e-06


def from_behind(block, axis, distance):
    devices = range(lax.axis_size(axis))
    route = [(i - distance, i) for i in devices if i - distance in devices]
    return lax.ppermute(block, axis, route)


def gelu(value):
    return jax.nn.gelu(value, approximate=True)


def rms_scale(value, gain):
    return value * lax.rsqrt(jnp.mean(value * value, axis=-1, keepdims=True) + eps) * gain


def gelu_product(gate_val, up_val):
    return gelu(gate_val) * up_val


def forward_product(left, weight):
    return jnp.dot(left, weight, preferred_element_type=F32)


def back_product(grad, weight):
    return lax.dot_general(grad, weight, (((2,), (1,)), ((), ())), preferred_element_type=F32)


def token_product(left, grad):
    return lax.dot_general(left, grad, (((0, 1), (0, 1)), ((), ())), preferred_element_type=F32)


def to_seq(parts):
    return lax.all_to_all(parts, "seq", split_axis=0, concat_axis=0, tiled=True)


def gather(value, axis):
    return lax.all_gather(value, axis, axis=0, tiled=True)


def scatter(value, axis):
    return lax.psum_scatter(value.astype(BF), axis, scatter_dimension=0, tiled=True)


MESH = pl.DeviceIdType.MESH
TILE = 128
LAP = 16


def greet(axis, count, mine):
    barrier = pltpu.get_barrier_semaphore()
    for d in range(1, count):
        pl.semaphore_signal(
            barrier, inc=1, device_id={axis: lax.rem(mine + d, count)}, device_id_type=MESH
        )
    pl.semaphore_wait(barrier, count - 1)


def remote(src, dst, send, recv, axis, to):
    return pltpu.make_async_remote_copy(
        src_ref=src, dst_ref=dst, send_sem=send, recv_sem=recv, device_id={axis: to}, device_id_type=MESH
    )


def minus_expm1(x, whole):
    series = 1.0 + x * (1.0 / 7)
    for n in (6, 5, 4, 3, 2):
        series = 1.0 + x * (1.0 / n) * series
    return jnp.where(x > -0.5, -x * series, 1.0 - whole)


def gelu_parts(v):
    inner = 0.7978845608028654 * (v + 0.044715 * (v * v * v))
    th = jnp.tanh(inner)
    value = 0.5 * v * (1.0 + th)
    slope = 0.5 * (1.0 + th) + 0.5 * v * (1.0 - th * th) * 0.7978845608028654 * (
        1.0 + 3 * 0.044715 * (v * v)
    )
    return value, slope


def dot(a, b, dims=((1,), (0,))):
    return lax.dot_general(a, b, (dims, ((), ())), preferred_element_type=F32)


LANE = 128


def wide(ref, rows, col):
    return jnp.concatenate([ref[c, rows, :] for c in range(col // LANE, (col + BW) // LANE)], axis=1)


def put_wide(ref, rows, col, value):
    for c in range(BW // LANE):
        ref[col // LANE + c, rows, :] = value[:, c * LANE : (c + 1) * LANE]


def over_tiles(S, L, C, step):
    per = L // TILE

    @pl.loop(0, S * per)
    def _(i):
        for col in range(0, C, BW):
            step(i // per, pl.multiple_of(lax.rem(i, per) * TILE, TILE), col)


def recur_forward(
    T, S, L, C, xy_ref, rows_ref, wd_ref, wi_ref,
    mixed_ref, states_ref, conv_ref, x_ref, halo_ref, inc_ref,
    a_s, b_s, ext_s, fin_s, got_s, halo_send, halo_recv, send_sem, recv_sem,
):
    t = lax.axis_index("tok")
    SL = S * L // 8
    half = 8 // S
    greet("tok", T, t)
    for q in range(S):
        x_ref[q, L - LAP : L, :] = xy_ref[q, L - LAP : L, 0:C].astype(BF)
    lap = remote(x_ref.at[:, pl.ds(L - LAP, LAP), :], halo_ref, halo_send, halo_recv, "tok", lax.rem(t + 1, T))

    @pl.when(t < T - 1)
    def _():
        lap.start()

    @pl.when(t > 0)
    def _():
        lap.wait_recv()

    @pl.when(t == 0)
    def _():
        halo_ref[...] = jnp.zeros_like(halo_ref)

    def make(q, r0, col):
        cs = pl.ds(col, BW)

        @pl.when(r0 == 0)
        def _():
            ext_s[0:8, cs] = halo_ref[q, :, cs].astype(F32)[8:16]

        @pl.when(r0 > 0)
        def _():
            ext_s[0:8, cs] = ext_s[TILE : TILE + 8, cs]

        low_x = xy_ref[q, pl.ds(r0, TILE), cs].astype(BF)

        @pl.when(r0 < L - TILE)
        def _():
            x_ref[q, pl.ds(r0, TILE), cs] = low_x

        @pl.when(r0 == L - TILE)
        def _():
            x_ref[q, L - TILE : L - LAP, cs] = low_x[: TILE - LAP]

        ext_s[8 : 8 + TILE, cs] = low_x.astype(F32)
        conv = rows_ref[4:5, cs] + jnp.zeros((TILE, BW), F32)
        for k in range(CONV):
            conv = conv + ext_s[5 + k : 5 + k + TILE, cs] * rows_ref[k : k + 1, cs]
        low = conv.astype(BF)
        conv_ref[q, pl.ds(r0, TILE), cs] = low
        vals = low.astype(F32)
        gate = dot(low, wd_ref[cs, :]) + rows_ref[5:6, cs]
        inp = dot(low, wi_ref[cs, :]) + rows_ref[6:7, cs]
        log = -jax.nn.sigmoid(gate) * rows_ref[8:9, cs]
        a = jnp.exp(log)
        b = jnp.sqrt(minus_expm1(2.0 * log, a * a)) * jax.nn.sigmoid(inp) * vals
        here = pl.ds(pl.multiple_of(q * L + r0, TILE), TILE)
        put_wide(a_s, here, col, a)
        put_wide(b_s, here, col, b)

    over_tiles(S, L, C, make)

    NC = C // LANE

    def walk(i, carry):
        at = pl.ds(i, 8, stride=SL)
        out = []
        for c, (h, p) in enumerate(carry):
            a = a_s[c, at, :]
            h = a * h + b_s[c, at, :]
            p = a * p
            a_s[c, at, :] = p
            b_s[c, at, :] = h
            out.append((h, p))
        return tuple(out)

    start = tuple((jnp.zeros((8, LANE), F32), jnp.ones((8, LANE), F32)) for _ in range(NC))
    for c, (h, p) in enumerate(lax.fori_loop(0, SL, walk, start, unroll=4)):
        fin_s[c, 0:8, :] = p
        fin_s[c, 8:16, :] = h

    def ship(j, _):
        remote(fin_s, got_s.at[t], send_sem.at[j], recv_sem.at[t], "tok", j).start()
        return 0

    lax.fori_loop(t + 1, T, ship, 0)

    def fold(j, incs):
        remote(fin_s, got_s.at[j], send_sem.at[j], recv_sem.at[j], "tok", t).wait_recv()
        out = []
        for c, inc in enumerate(incs):
            for k in range(half):
                pj = got_s[j, c, pl.ds(k, S, stride=half), :]
                hj = got_s[j, c, pl.ds(8 + k, S, stride=half), :]
                inc = pj * inc + hj
            out.append(inc)
        return tuple(out)

    for c, inc in enumerate(lax.fori_loop(0, t, fold, tuple(jnp.zeros((S, LANE), F32) for _ in range(NC)))):
        for k in range(half):
            inc_ref[c, pl.ds(k, S, stride=half), :] = inc
            if k < half - 1:
                inc = fin_s[c, pl.ds(k, S, stride=half), :] * inc + fin_s[c, pl.ds(8 + k, S, stride=half), :]

    def finish(q, r0, col):
        cs = pl.ds(col, BW)
        row = q * L + r0
        here = pl.ds(pl.multiple_of(row, TILE), TILE)
        st = wide(b_s, here, col) + wide(a_s, here, col) * wide(inc_ref, pl.ds(row // SL, 1), col)
        states_ref[here, cs] = st
        value, _ = gelu_parts(xy_ref[q, pl.ds(r0, TILE), pl.ds(C + col, BW)])
        mixed_ref[here, cs] = (st * value).astype(BF)

    over_tiles(S, L, C, finish)

    def drain(j, _):
        remote(fin_s, got_s.at[t], send_sem.at[j], recv_sem.at[t], "tok", j).wait_send()
        return 0

    lax.fori_loop(t + 1, T, drain, 0)

    @pl.when(t < T - 1)
    def _():
        lap.wait_send()


def recur_backward(
    T, S, L, C, gm_ref, xy_ref, st_ref, conv_ref, x_ref, halo_ref, inc_ref, rows_ref, wd_ref, wi_ref,
    gxy_ref, gwd_ref, gwi_ref, small_ref,
    a_s, g_s, r_s, sg_s, si_s, gc_s, ext_s, pst_s, fin_s, got_s, car_s, lap_send, lap_recv, send_sem, recv_sem,
):
    t = lax.axis_index("tok")
    SL = S * L // 8
    half = 8 // S
    greet("tok", T, t)

    def prepare(q, r0, col):
        cs = pl.ds(col, BW)
        here = pl.ds(pl.multiple_of(q * L + r0, TILE), TILE)
        low = conv_ref[q, pl.ds(r0, TILE), cs]
        sg = jax.nn.sigmoid(dot(low, wd_ref[cs, :]) + rows_ref[5:6, cs])
        sg_s[here, cs] = sg
        si_s[here, cs] = jax.nn.sigmoid(dot(low, wi_ref[cs, :]) + rows_ref[6:7, cs])
        put_wide(a_s, here, col, jnp.exp(-sg * rows_ref[8:9, cs]))
        value, slope = gelu_parts(xy_ref[q, pl.ds(r0, TILE), pl.ds(C + col, BW)])
        gm = gm_ref[here, cs]
        put_wide(g_s, here, col, gm * value)
        gxy_ref[q, pl.ds(r0, TILE), pl.ds(C + col, BW)] = (gm * st_ref[here, cs] * slope).astype(BF)

    over_tiles(S, L, C, prepare)

    NC = C // LANE

    def walk(i, carry):
        at = pl.ds(SL - 1 - i, 8, stride=SL)
        out = []
        for c, (e, r) in enumerate(carry):
            a = a_s[c, at, :]
            adj = g_s[c, at, :] + e
            g_s[c, at, :] = adj
            r_s[c, at, :] = r
            out.append((a * adj, a * r))
        return tuple(out)

    start = tuple((jnp.zeros((8, LANE), F32), jnp.ones((8, LANE), F32)) for _ in range(NC))
    for c, (e, r) in enumerate(lax.fori_loop(0, SL, walk, start, unroll=4)):
        fin_s[c, 0:8, :] = r
        fin_s[c, 8:16, :] = e

    def ship(j, _):
        remote(fin_s, got_s.at[t], send_sem.at[j], recv_sem.at[t], "tok", j).start()
        return 0

    lax.fori_loop(0, t, ship, 0)

    def fold(i, cars):
        j = T - 1 - i
        remote(fin_s, got_s.at[j], send_sem.at[j], recv_sem.at[j], "tok", t).wait_recv()
        out = []
        for c, car in enumerate(cars):
            for k in reversed(range(half)):
                rj = got_s[j, c, pl.ds(k, S, stride=half), :]
                ej = got_s[j, c, pl.ds(8 + k, S, stride=half), :]
                car = rj * car + ej
            out.append(car)
        return tuple(out)

    for c, car in enumerate(lax.fori_loop(0, T - 1 - t, fold, tuple(jnp.zeros((S, LANE), F32) for _ in range(NC)))):
        for k in reversed(range(half)):
            car_s[c, pl.ds(k, S, stride=half), :] = car
            if k > 0:
                car = fin_s[c, pl.ds(k, S, stride=half), :] * car + fin_s[c, pl.ds(8 + k, S, stride=half), :]

    small_ref[...] = jnp.zeros_like(small_ref)
    gwd_ref[...] = jnp.zeros_like(gwd_ref)
    gwi_ref[...] = jnp.zeros_like(gwi_ref)

    def add_row(k, cs, value):
        small_ref[k : k + 1, cs] += jnp.sum(value, axis=0, keepdims=True)

    def chain(q, r0, col):
        cs = pl.ds(col, BW)
        row = q * L + r0
        here = pl.ds(pl.multiple_of(row, TILE), TILE)

        @pl.when(r0 == 0)
        def _():
            pst_s[0:8, cs] = wide(inc_ref, pl.ds(q * half, 1), col) + jnp.zeros((8, BW), F32)

        @pl.when(r0 > 0)
        def _():
            pst_s[0:8, cs] = pst_s[TILE : TILE + 8, cs]

        pst_s[8 : 8 + TILE, cs] = st_ref[here, cs]
        adj = wide(g_s, here, col) + wide(r_s, here, col) * wide(car_s, pl.ds(row // SL, 1), col)
        sg, si, a = sg_s[here, cs], si_s[here, cs], wide(a_s, here, col)
        low = conv_ref[q, pl.ds(r0, TILE), cs]
        vals = low.astype(F32)
        sp = rows_ref[8:9, cs]
        square = a * a
        scale = jnp.sqrt(minus_expm1(-2.0 * sg * sp, square))
        grad_log = adj * pst_s[7 : 7 + TILE, cs] * a - adj * si * vals * square / scale
        grad_gate = (-grad_log * sp * sg * (1.0 - sg)).astype(BF)
        add_row(7, cs, -grad_log * sg)
        grad_inp = (adj * scale * vals * si * (1.0 - si)).astype(BF)
        add_row(5, cs, grad_gate.astype(F32))
        add_row(6, cs, grad_inp.astype(F32))
        gc = (
            adj * scale * si
            + dot(grad_gate, wd_ref[cs, :], ((1,), (1,)))
            + dot(grad_inp, wi_ref[cs, :], ((1,), (1,)))
        )
        gc_s[q, pl.ds(r0, TILE), cs] = gc
        add_row(4, cs, gc)
        gwd_ref[cs, :] += dot(low, grad_gate, ((0,), (0,)))
        gwi_ref[cs, :] += dot(low, grad_inp, ((0,), (0,)))

    over_tiles(S, L, C, chain)
    small_ref[7:8, :] *= 8.0 * rows_ref[9:10, :]

    lap = remote(gc_s.at[:, pl.ds(0, 8), :], gc_s.at[:, pl.ds(L, 8), :], lap_send, lap_recv, "tok", lax.rem(t + T - 1, T))

    @pl.when(t > 0)
    def _():
        lap.start()

    @pl.when(t < T - 1)
    def _():
        lap.wait_recv()

    @pl.when(t == T - 1)
    def _():
        gc_s[:, pl.ds(L, 8), :] = jnp.zeros((S, 8, C), F32)

    def taps(q, r0, col):
        cs = pl.ds(col, BW)

        @pl.when(r0 == 0)
        def _():
            ext_s[0:8, cs] = halo_ref[q, :, cs].astype(F32)[8:16]

        @pl.when(r0 > 0)
        def _():
            ext_s[0:8, cs] = ext_s[TILE : TILE + 8, cs]

        ext_s[8 : 8 + TILE, cs] = x_ref[q, pl.ds(r0, TILE), cs].astype(F32)
        pst_s[0 : TILE + 8, cs] = gc_s[q, pl.ds(r0, TILE + 8), cs]
        gc = pst_s[0:TILE, cs]
        gx = jnp.zeros((TILE, BW), F32)
        for k in range(CONV):
            add_row(k, cs, gc * ext_s[5 + k : 5 + k + TILE, cs])
            gx = gx + pst_s[3 - k : 3 - k + TILE, cs] * rows_ref[k : k + 1, cs]
        gxy_ref[q, pl.ds(r0, TILE), cs] = gx.astype(BF)

    over_tiles(S, L, C, taps)

    def drain(j, _):
        remote(fin_s, got_s.at[t], send_sem.at[j], recv_sem.at[t], "tok", j).wait_send()
        return 0

    lax.fori_loop(0, t, drain, 0)

    @pl.when(t > 0)
    def _():
        lap.wait_send()


VM = pl.BlockSpec(memory_space=pltpu.VMEM)


def shape(dims, kind=F32):
    return jax.ShapeDtypeStruct(dims, kind)


def params(collective_id, mib=58):
    return pltpu.CompilerParams(
        collective_id=collective_id, has_side_effects=True, vmem_limit_bytes=mib * 1024 * 1024
    )


def run_forward(T, branches, rows, wd, wi):
    S, L, C = branches.shape
    C //= 2
    M = S * L
    dma = pltpu.SemaphoreType.DMA
    split = pltpu.VMEM((C // LANE, M, LANE), F32)
    return pl.pallas_call(
        functools.partial(recur_forward, T, S, L, C),
        out_shape=(
            shape((M, C), BF),
            shape((M, C)),
            shape((S, L, C), BF),
            shape((S, L, C), BF),
            shape((S, LAP, C), BF),
            shape((C // LANE, 8, LANE)),
        ),
        in_specs=[VM] * 4,
        out_specs=(VM,) * 6,
        scratch_shapes=[
            split,
            split,
            pltpu.VMEM((TILE + 8, C), F32),
            pltpu.VMEM((C // LANE, 16, LANE), F32),
            pltpu.VMEM((T, C // LANE, 16, LANE), F32),
            dma,
            dma,
            dma((T,)),
            dma((T,)),
        ],
        compiler_params=params(0),
        cost_estimate=pl.CostEstimate(flops=4 * M * C * BW, bytes_accessed=100000000, transcendentals=6 * M * C),
    )(branches, rows, wd, wi)


def run_backward(T, grad_mixed, branches, states, conv, branch_x, halo, inc, rows, wd, wi):
    S, L, C = branch_x.shape
    M = S * L
    dma = pltpu.SemaphoreType.DMA
    big = pltpu.VMEM((M, C), F32)
    split = pltpu.VMEM((C // LANE, M, LANE), F32)
    return pl.pallas_call(
        functools.partial(recur_backward, T, S, L, C),
        out_shape=(shape((S, L, 2 * C), BF), shape((C, BW)), shape((C, BW)), shape((8, C))),
        in_specs=[VM] * 10,
        out_specs=(VM,) * 4,
        scratch_shapes=[split] * 3
        + [big] * 2
        + [
            pltpu.VMEM((S, L + 8, C), F32),
            pltpu.VMEM((TILE + 8, C), F32),
            pltpu.VMEM((TILE + 8, C), F32),
            pltpu.VMEM((C // LANE, 16, LANE), F32),
            pltpu.VMEM((T, C // LANE, 16, LANE), F32),
            pltpu.VMEM((C // LANE, 8, LANE), F32),
            dma,
            dma,
            dma((T,)),
            dma((T,)),
        ],
        compiler_params=params(1),
        cost_estimate=pl.CostEstimate(flops=12 * M * C * BW, bytes_accessed=180000000, transcendentals=6 * M * C),
    )(grad_mixed, branches, states, conv, branch_x, halo, inc, rows, wd, wi)


CHUNKS = 4


def root_scale(v):
    return lax.rsqrt(jnp.mean(v * v, axis=-1, keepdims=True) + eps)


def rms_back(v, gain, grad):
    scale = root_scale(v)
    hat = v * scale
    inner = grad * gain
    return scale * (inner - hat * jnp.mean(inner * hat, axis=-1, keepdims=True)), grad * hat


def flip(me, bit):
    return me + bit - 2 * bit * lax.rem(me // bit, 2)


def plane_sum(kind, L, D, *refs):
    shares = kind in ("first", "second")
    part = refs[0]
    if kind == "first":
        tokens, gain, keep, everyone = refs[1:5]
        rest = refs[5:]
    elif kind == "second":
        resid, gain, cot, weight, keep, gain_grad, everyone = refs[1:8]
        rest = refs[8:]
    elif kind == "third":
        tokens, gain, before, keep = refs[1:5]
        rest = refs[5:]
    else:
        resid, keep = refs[1:3]
        rest = refs[3:]
    one_s, two_s, two_out, one_send, one_recv, two_send, two_recv = rest[:7]
    if shares:
        own_s, all_send, all_recv, own_sem = rest[7:]
    me = lax.axis_index("seq")
    H = L // CHUNKS
    px, py = flip(me, 1), flip(me, 2)
    pd = 3 - me
    barrier = pltpu.get_barrier_semaphore()
    for peer in (px, py):
        pl.semaphore_signal(barrier, inc=1, device_id={"seq": peer}, device_id_type=MESH)
    pl.semaphore_wait(barrier, 2)

    def peers(c):
        return (px, py) if c % 2 == 0 else (py, px)

    def rows(c):
        return pl.ds(c * H, H)

    def one(c, k):
        f, _ = peers(c)
        src = (f, pd)[k]
        return remote(part.at[src, rows(c), :], one_s.at[c, k], one_send.at[c, k], one_recv.at[c, k], "seq", f)

    def two(c):
        return remote(two_out.at[c], two_s.at[c], two_send.at[c], two_recv.at[c], "seq", peers(c)[1])

    def share(c, k):
        f, g = peers(c)
        if k == 2:
            place = everyone.at[f, rows(c), :]
            return remote(place, place, all_send.at[c, k], all_recv.at[c, k], "seq", g)
        place = everyone.at[me, rows(c), :]
        return remote(own_s.at[rows(c), :], place, all_send.at[c, k], all_recv.at[c, k], "seq", (f, g)[k])

    def own(c):
        return pltpu.make_async_copy(own_s.at[rows(c), :], everyone.at[me, rows(c), :], own_sem.at[c])

    def middle(c):
        one(c, 1).wait_recv()
        two_out[c] = (part[peers(c)[1], rows(c), :].astype(F32) + one_s[c, 1].astype(F32)).astype(BF)
        two(c).start()

    def finish(c):
        one(c, 0).wait_recv()
        two(c).wait_recv()
        total = part[me, rows(c), :].astype(F32) + one_s[c, 0].astype(F32) + two_s[c].astype(F32)
        r = rows(c)
        if kind == "first":
            total = tokens[r, :].astype(F32) + total
            keep[r, :] = total
            own_s[r, :] = (total * root_scale(total) * gain[0:1, :]).astype(BF)
        elif kind == "second":
            back, gg = rms_back(resid[r, :], gain[0:1, :], total)
            gg = jnp.sum(gg, axis=0, keepdims=True)
            gain_grad[0:1, :] = gg if c == 0 else gain_grad[0:1, :] + gg
            total = cot[r, :].astype(F32) * weight[0:1, 0:1] + back
            keep[r, :] = total
            own_s[r, :] = total.astype(BF)
        elif kind == "third":
            back, _ = rms_back(tokens[r, :].astype(F32), gain[0:1, :], total)
            keep[r, :] = before[r, :] + back
        else:
            keep[r, :] = (resid[r, :] + total).astype(BF)
        if shares:
            share(c, 0).start()
            share(c, 1).start()
            own(c).start()

    def forward(c):
        share(c, 0).wait_recv()
        share(c, 2).start()

    if kind == "second":
        gain_grad[...] = jnp.zeros_like(gain_grad)
    for c in range(CHUNKS):
        for k in (1, 0):
            one(c, k).start()
    for c in range(CHUNKS):
        middle(c)
        if c > 0:
            finish(c - 1)
        if shares and c > 1:
            forward(c - 2)
    finish(CHUNKS - 1)
    if shares:
        forward(CHUNKS - 2)
        forward(CHUNKS - 1)
    for c in range(CHUNKS):
        for k in (0, 1):
            one(c, k).wait_send()
        two(c).wait_send()
        if shares:
            for k in (1, 2):
                share(c, k).wait_recv()
            for k in (0, 1, 2):
                share(c, k).wait_send()
            own(c).wait()


def run_plane(kind, collective_id, part, *ins):
    S, L, D = part.shape
    H = L // CHUNKS
    dma = pltpu.SemaphoreType.DMA
    shares = kind in ("first", "second")
    outs = [shape((L, D), BF if kind == "out" else F32)]
    specs = [VM]
    if kind == "second":
        outs.append(shape((8, D)))
        specs.append(VM)
    if shares:
        outs.append(shape((S, L, D), BF))
        specs.append(pl.BlockSpec(memory_space=pl.ANY))
    scratch = [
        pltpu.VMEM((CHUNKS, 2, H, D), BF),
        pltpu.VMEM((CHUNKS, H, D), BF),
        pltpu.VMEM((CHUNKS, H, D), BF),
        dma((CHUNKS, 2)),
        dma((CHUNKS, 2)),
        dma((CHUNKS,)),
        dma((CHUNKS,)),
    ]
    if shares:
        scratch += [pltpu.VMEM((L, D), BF), dma((CHUNKS, 3)), dma((CHUNKS, 3)), dma((CHUNKS,))]
    return pl.pallas_call(
        functools.partial(plane_sum, kind, L, D),
        out_shape=tuple(outs),
        in_specs=[VM] * (1 + len(ins)),
        out_specs=tuple(specs),
        scratch_shapes=scratch,
        compiler_params=params(collective_id, 40),
        cost_estimate=pl.CostEstimate(
            flops=40 * L * D, bytes_accessed=(240 if shares else 120) * 1000000, transcendentals=L
        ),
    )(part, *ins)


def plane_swap(modes, *refs):
    n = len(modes)
    ins, outs = refs[:n], refs[n : 2 * n]
    send, recv, own_sem = refs[2 * n :]
    me = lax.axis_index("seq")
    S = lax.axis_size("seq")
    greet("seq", S, me)

    def copy(i, d):
        to = lax.rem(me + d, S)
        src = ins[i] if modes[i] == "all" else ins[i].at[to]
        return remote(src, outs[i].at[me], send.at[i, d], recv.at[i, d], "seq", to)

    def own(i):
        src = ins[i] if modes[i] == "all" else ins[i].at[me]
        return pltpu.make_async_copy(src, outs[i].at[me], own_sem.at[i])

    for i in range(n):
        for d in range(1, S):
            copy(i, d).start()
        own(i).start()
    for i in range(n):
        for d in range(1, S):
            copy(i, d).wait()
        own(i).wait()


def run_swap(S, modes, collective_id, *ins):
    n = len(modes)
    dma = pltpu.SemaphoreType.DMA
    outs = tuple(shape(((S,) if m == "all" else ()) + x.shape, x.dtype) for m, x in zip(modes, ins))
    size = sum(3 * x.size * x.dtype.itemsize // (1 if m == "all" else S) for m, x in zip(modes, ins))
    hbm = pl.BlockSpec(memory_space=pl.ANY)
    return pl.pallas_call(
        functools.partial(plane_swap, modes),
        out_shape=outs,
        in_specs=[hbm] * n,
        out_specs=(hbm,) * n,
        scratch_shapes=[dma((n, S)), dma((n, S)), dma((n,))],
        compiler_params=params(collective_id, 4),
        cost_estimate=pl.CostEstimate(flops=0, bytes_accessed=size * 40, transcendentals=0),
    )(*ins)


def plane_fill(S, T, L, slabs, *refs):
    pack, first, second, gates = refs[:4]
    pack_out, first_out, second_out, gates_out, lent = refs[4:9]
    pack_send, pack_recv, row_send, row_recv, gate_send, gate_recv, lent_send, lent_recv, own_sem = refs[9:]
    me, t = lax.axis_index("seq"), lax.axis_index("tok")
    px, py, pd = flip(me, 1), flip(me, 2), S - 1 - me
    H = L // CHUNKS
    barrier = pltpu.get_barrier_semaphore()
    for peer in (px, py, pd):
        pl.semaphore_signal(barrier, inc=1, device_id={"seq": peer}, device_id_type=MESH)

    @pl.loop(1, T)
    def _(d):
        pl.semaphore_signal(barrier, inc=1, device_id={"tok": lax.rem(t + d, T)}, device_id_type=MESH)

    pl.semaphore_wait(barrier, S - 1 + T - 1)

    def gate(d):
        return remote(gates, gates_out.at[t], gate_send.at[d], gate_recv.at[d], "tok", lax.rem(t + d, T))

    def piece(k):
        to = (pd, px, py)[k]
        return remote(pack.at[to], pack_out.at[me], pack_send.at[k], pack_recv.at[k], "seq", to)

    def row(a, c, k):
        src, out = ((first, first_out), (second, second_out))[a]
        f, g = (px, py) if c % 2 == 0 else (py, px)
        rows = pl.ds(c * H, H)
        sems = row_send.at[a, c, k], row_recv.at[a, c, k], "seq"
        if k == 2:
            place = out.at[f, rows, :]
            return remote(place, place, *sems, g)
        return remote(src.at[rows, :], out.at[me, rows, :], *sems, (f, g)[k])

    mine = [
        pltpu.make_async_copy(pack.at[me], pack_out.at[me], own_sem.at[0]),
        pltpu.make_async_copy(first, first_out.at[me], own_sem.at[1]),
        pltpu.make_async_copy(second, second_out.at[me], own_sem.at[2]),
        pltpu.make_async_copy(gates, gates_out.at[t], own_sem.at[3]),
    ]
    loan = remote(gates_out.at[pl.ds(0, slabs)], lent, lent_send, lent_recv, "seq", px)

    @pl.loop(1, T)
    def _(d):
        gate(d).start()

    for k in range(3):
        piece(k).start()
    for copy in mine:
        copy.start()
    for k in (0, 1):
        for c in range(CHUNKS):
            row(0, c, k).start()
    mine[3].wait()

    @pl.loop(1, T)
    def _(d):
        gate(d).wait_recv()

    @pl.when(lax.rem(me, 2) == 1)
    def _():
        loan.start()

    for c in range(CHUNKS):
        row(0, c, 0).wait_recv()
        row(0, c, 2).start()
    for k in (0, 1):
        for c in range(CHUNKS):
            row(1, c, k).start()
    for c in range(CHUNKS):
        row(1, c, 0).wait_recv()
        row(1, c, 2).start()
    for k in range(3):
        piece(k).wait()
    for a in (0, 1):
        for c in range(CHUNKS):
            row(a, c, 0).wait_send()
            row(a, c, 1).wait()
            row(a, c, 2).wait()
    for copy in mine[:3]:
        copy.wait()

    @pl.loop(1, T)
    def _(d):
        gate(d).wait_send()

    @pl.when(lax.rem(me, 2) == 1)
    def _():
        loan.wait_send()

    @pl.when(lax.rem(me, 2) == 0)
    def _():
        loan.wait_recv()


def run_fill(S, T, slabs, collective_id, pack, first, second, gates):
    L = first.shape[0]
    dma = pltpu.SemaphoreType.DMA
    hbm = pl.BlockSpec(memory_space=pl.ANY)
    return pl.pallas_call(
        functools.partial(plane_fill, S, T, L, slabs),
        out_shape=(
            shape(pack.shape, BF),
            shape((S,) + first.shape, BF),
            shape((S,) + second.shape, BF),
            shape((T,) + gates.shape, BF),
            shape((slabs,) + gates.shape, BF),
        ),
        in_specs=[hbm] * 4,
        out_specs=(hbm,) * 5,
        scratch_shapes=[
            dma((3,)),
            dma((3,)),
            dma((2, CHUNKS, 3)),
            dma((2, CHUNKS, 3)),
            dma((T,)),
            dma((T,)),
            dma,
            dma,
            dma((4,)),
        ],
        compiler_params=params(collective_id, 4),
        cost_estimate=pl.CostEstimate(flops=0, bytes_accessed=320000000, transcendentals=0),
    )(pack, first, second, gates)


def after(value, *others):
    return lax.optimization_barrier((value,) + others)[0]


def body(
    tokens,
    source_ids,
    loss_weights,
    grad_output,
    first_gain,
    input_weight,
    gelu_weight,
    conv_weight,
    conv_bias,
    decay_gate,
    decay_bias,
    input_gate,
    input_bias,
    decay_param,
    output_weight,
    second_gain,
    gate_weight,
    up_weight,
    down_weight,
):
    S, T = lax.axis_size("seq"), lax.axis_size("tok")
    me = lax.axis_index("seq")
    length, D = tokens.shape[1:]
    ds, R = input_weight.shape
    rs = output_weight.shape[0]
    F = gate_weight.shape[1]
    FQ = F // S
    heads = R // BW
    starts = [-(-i * heads // S) for i in range(S + 1)]
    C = max(starts[i + 1] - starts[i] for i in range(S)) * BW
    quarter = R // S
    offs = [starts[i] * BW - i * quarter for i in range(S)] + [0]
    most = max(offs)
    off = sum(jnp.where(me == i, offs[i], 0) for i in range(S))
    own = sum(jnp.where(me == i, (starts[i + 1] - starts[i]) * BW, 0) for i in range(S))

    def cols_for(w):
        parts = [w[:, starts[i] * BW : starts[i + 1] * BW] for i in range(S)]
        return jnp.stack([jnp.pad(p, ((0, 0), (0, C - p.shape[1]))) for p in parts])

    def d_rows(w):
        return lax.all_gather(w, "tok", axis=1, tiled=True).reshape((D, w.shape[-1]))

    def d_scatter(g):
        return lax.psum_scatter(g.reshape(S, T * ds, g.shape[-1]), "tok", scatter_dimension=1, tiled=True)

    def r_align(g):
        g = lax.dynamic_update_slice_in_dim(jnp.zeros((quarter + 2 * most, g.shape[1]), BF), g.astype(BF), off, axis=0)
        back = from_behind(g[quarter : quarter + most], "seq", 1)
        keep = lax.broadcasted_iota(jnp.int32, (quarter, 1), 0) < off
        return jnp.where(keep, jnp.pad(back, ((0, quarter - most), (0, 0))), g[:quarter])

    small = jnp.concatenate(
        [conv_weight, jnp.stack([conv_bias, decay_bias, input_bias, decay_param], axis=1)], axis=1
    )
    small = jnp.pad(small, ((0, 0), (0, SMALL - small.shape[1])))
    gates = jnp.concatenate([decay_gate, input_gate, small], axis=1)
    gains = jnp.pad(jnp.stack([first_gain, second_gain], axis=1), ((0, 0), (0, SMALL - 2)))
    pack_in = jnp.concatenate(
        [cols_for(input_weight), cols_for(gelu_weight), jnp.broadcast_to(gains, (S,) + gains.shape)], axis=2
    )
    (pack_in,) = run_swap(S, ("slice",), 2, pack_in)
    sources = lax.broadcasted_iota(jnp.int32, (1, loss_weights.shape[0]), 1)
    picked = jnp.sum(jnp.where(source_ids[:, None] == sources, loss_weights[None, :], 0.0), axis=1)
    cot_low = (grad_output[0].astype(F32) * picked[:, None]).astype(BF)
    pack_f = jnp.concatenate([w.reshape(ds, S, FQ).swapaxes(0, 1) for w in (gate_weight, up_weight)], axis=2)
    pack_f, everyone, cot_low, gates, lent = run_fill(
        S, T, -(-most // rs), 3, after(pack_f, pack_in), tokens[0], cot_low, gates
    )

    def r_rows(whole, lent):
        lent = lent[:most]
        whole = jnp.concatenate([whole, lent, jnp.zeros_like(lent)], axis=0)
        whole = lax.dynamic_slice_in_dim(whole, off, C, axis=0)
        return jnp.where(lax.broadcasted_iota(jnp.int32, whole.shape, 0) < own, whole, 0)

    output_weight = after(output_weight, pack_in)
    pack_in = d_rows(pack_in)
    weight_xy = pack_in[:, : 2 * C]
    gain_one, gain_two = pack_in[:, 2 * C].astype(F32), pack_in[:, 2 * C + 1].astype(F32)
    gates = r_rows(gates.reshape(quarter, -1), lent.reshape(-1, lent.shape[-1]))
    weight_decay, weight_input = gates[:, :BW], gates[:, BW : 2 * BW]
    rows = gates[:, 2 * BW : 2 * BW + 8].T.astype(F32)
    param = rows[7:8]
    rows = jnp.concatenate(
        [rows, 8.0 * jax.nn.softplus(param), jax.nn.sigmoid(param), jnp.zeros((6, C), F32)], axis=0
    )
    weight_out = gather(output_weight, "tok")
    weight_out = r_rows(weight_out, from_behind(weight_out[:most], "seq", -1))

    pack_f = d_rows(after(pack_f, pack_in))
    weight_gate, weight_up = pack_f[:, :FQ], pack_f[:, FQ:]

    everyone = everyone.astype(F32)
    normed = lax.optimization_barrier(rms_scale(everyone, gain_one).astype(BF))
    branches = forward_product(normed, weight_xy)
    weight_down = gather(after(down_weight, branches), "tok")
    mixed, states, conv_low, branch_x, halo, incoming = run_forward(T, branches, rows, weight_decay, weight_input)
    mixed = mixed.reshape(S, length, C)
    passed = from_behind(mixed[:, :, quarter:], "seq", 1)
    mixed_own = jnp.pad(mixed, ((0, 0), (0, 0), (most, 0)))[:, :, :quarter]
    mixed_own = jnp.where(off > 0, mixed_own, mixed[:, :, :quarter])
    mixed_own = jnp.where(
        lax.broadcasted_iota(jnp.int32, (1, 1, quarter), 2) < off,
        jnp.pad(passed, ((0, 0), (0, 0), (0, quarter - most))),
        mixed_own,
    )
    part = forward_product(mixed, weight_out).astype(BF)
    resid, second_normed = run_plane("first", 4, part, tokens[0], gain_two[None])

    gate_val = forward_product(second_normed, weight_gate)
    up_val = forward_product(second_normed, weight_up)
    hidden = gelu_product(gate_val, up_val).astype(BF)
    grad_down = token_product(hidden, cot_low).astype(BF)
    weight_down = after(weight_down, grad_down)
    grad_down = scatter(grad_down, "tok").astype(F32)

    grad_hidden = back_product(cot_low, weight_down)
    _, hidden_pull = jax.vjp(gelu_product, gate_val, up_val)
    grad_gate_val, grad_up_val = hidden_pull(grad_hidden)
    grad_gate_low, grad_up_low = grad_gate_val.astype(BF), grad_up_val.astype(BF)
    grad_gate_w = token_product(second_normed, grad_gate_low).astype(BF)
    grad_up_w = token_product(second_normed, grad_up_low).astype(BF)
    grad_gate_low, grad_up_low, _, _ = lax.optimization_barrier((grad_gate_low, grad_up_low, grad_gate_w, grad_up_w))
    grad_second = back_product(grad_gate_low, weight_gate) + back_product(grad_up_low, weight_up)
    grad_second = after(grad_second.astype(BF), grad_down)
    grad_gate_w = d_scatter(grad_gate_w)
    grad_up_w = d_scatter(grad_up_w)
    picked = jnp.broadcast_to(picked[None], (8, 128))
    grad_resid, grad_gain_two, resid_low = run_plane(
        "second", 6, grad_second, resid, gain_two[None], grad_output[0], picked
    )
    grad_gain_two = grad_gain_two[0]

    def whole_rows(parts):
        return to_seq(parts).swapaxes(0, 1).reshape(ds, F).astype(F32)

    grad_out_w = token_product(mixed_own, resid_low).astype(BF)
    grad_mixed = back_product(after(resid_low, grad_out_w, grad_gate_w), weight_out)
    grad_out_w = scatter(grad_out_w, "tok").astype(F32)
    grad_xy, grad_decay_w, grad_input_w, smalls = run_backward(
        T, grad_mixed.reshape(S * length, C), branches, states, conv_low, branch_x, halo, incoming, rows,
        weight_decay, weight_input,
    )
    grad_i = token_product(normed, after(grad_xy, grad_up_w)).astype(BF)
    smalls = jnp.pad(smalls.T, ((0, 0), (0, BW - 8)))
    grad_r = r_align(jnp.concatenate([grad_decay_w, grad_input_w, smalls], axis=1))
    grad_normed = back_product(after(grad_xy, grad_i), weight_xy)
    grad_normed = after(grad_normed, grad_out_w)
    hat = everyone * root_scale(everyone)
    gains = jnp.stack([jnp.sum(grad_normed * hat, axis=(0, 1)), grad_gain_two], axis=0).astype(BF)

    block = [p.reshape(T, rs, BW) for p in (grad_r[:, :BW], grad_r[:, BW : 2 * BW], grad_r[:, 2 * BW :])]
    gains = gains.reshape(2, S, T, ds).transpose(2, 0, 1, 3).reshape(T, 2, S * ds)
    tall = 3 * rs + 2 + -(3 * rs + 2) % (S * ds)
    across = tall // (S * ds)
    block = jnp.concatenate(block + [jnp.pad(gains, ((0, 0), (0, tall - 3 * rs - 2), (0, BW - S * ds)))], axis=1)
    block = block.reshape(T, S, ds, across, BW).transpose(1, 0, 2, 3, 4).reshape(D, across * BW)
    grad_i = jnp.concatenate([grad_i, block], axis=1)
    (grad_tokens,) = run_plane("third", 7, grad_normed.astype(BF), tokens[0], gain_one[None], grad_resid)
    part = forward_product(hidden, weight_down).astype(BF)
    (block_out,) = run_plane("out", 5, part, resid)
    grad_i = d_scatter(grad_i)
    block = grad_i[:, :, 2 * C :].reshape(tall, BW).astype(F32)
    grad_r = [block[i * rs : (i + 1) * rs] for i in range(3)]
    gains = block[3 * rs : 3 * rs + 2, : S * ds].reshape(2, S, ds).transpose(1, 2, 0)
    gains = jnp.pad(gains.astype(BF), ((0, 0), (0, 0), (0, SMALL - 2)))
    grad_i = to_seq(jnp.concatenate([grad_i[:, :, : 2 * C], gains], axis=2)).astype(F32)
    gain_grads = jnp.sum(grad_i[:, :, 2 * C : 2 * C + 2], axis=0)

    def columns(at):
        return jnp.concatenate(
            [grad_i[i, :, at : at + (starts[i + 1] - starts[i]) * BW] for i in range(S)], axis=1
        )

    smalls = grad_r[2]
    return (
        block_out[None],
        grad_tokens[None],
        gain_grads[:, 0],
        columns(0),
        columns(C),
        smalls[:, :CONV],
        smalls[:, 4],
        grad_r[0],
        smalls[:, 5],
        grad_r[1],
        smalls[:, 6],
        smalls[:, 7],
        grad_out_w,
        gain_grads[:, 1],
        whole_rows(grad_gate_w),
        whole_rows(grad_up_w),
        grad_down,
    )


def solution(mesh):
    one, two = P(("seq", "tok")), P(("seq", "tok"), None)
    data = P("seq", "tok", None)
    return jax.shard_map(
        body,
        mesh=mesh,
        in_specs=(data, P("seq"), P(), data, one, two, two, two, one, two, one, two, one, one, two, one, two, two, two),
        out_specs=(data, data, one, two, two, two, one, two, one, two, one, one, two, one, two, two, two),
        check_vma=False,
    )
```

```python
import functools

import jax
import jax.numpy as jnp
from jax import lax
from jax.experimental import pallas as pl
from jax.experimental.pallas import tpu as pltpu
from jax.sharding import PartitionSpec as P

BW = 256
CONV = 4
SMALL = 128
BF = jnp.bfloat16
F32 = jnp.float32
eps = 1e-06


def from_behind(block, axis, distance):
    devices = range(lax.axis_size(axis))
    route = [(i - distance, i) for i in devices if i - distance in devices]
    return lax.ppermute(block, axis, route)


def gelu(value):
    return jax.nn.gelu(value, approximate=True)


def rms_scale(value, gain):
    return value * lax.rsqrt(jnp.mean(value * value, axis=-1, keepdims=True) + eps) * gain


def gelu_product(gate_val, up_val):
    return gelu(gate_val) * up_val


def forward_product(left, weight):
    return jnp.dot(left, weight, preferred_element_type=F32)


def back_product(grad, weight):
    return lax.dot_general(grad, weight, (((2,), (1,)), ((), ())), preferred_element_type=F32)


def token_product(left, grad):
    return lax.dot_general(left, grad, (((0, 1), (0, 1)), ((), ())), preferred_element_type=F32)


def to_seq(parts):
    return lax.all_to_all(parts, "seq", split_axis=0, concat_axis=0, tiled=True)


def gather(value, axis):
    return lax.all_gather(value, axis, axis=0, tiled=True)


def scatter(value, axis):
    return lax.psum_scatter(value.astype(BF), axis, scatter_dimension=0, tiled=True)


MESH = pl.DeviceIdType.MESH
TILE = 128
LAP = 16


def greet(axis, count, mine):
    barrier = pltpu.get_barrier_semaphore()
    for d in range(1, count):
        pl.semaphore_signal(
            barrier, inc=1, device_id={axis: lax.rem(mine + d, count)}, device_id_type=MESH
        )
    pl.semaphore_wait(barrier, count - 1)


def remote(src, dst, send, recv, axis, to):
    return pltpu.make_async_remote_copy(
        src_ref=src, dst_ref=dst, send_sem=send, recv_sem=recv, device_id={axis: to}, device_id_type=MESH
    )


CHUNKS = 4


def flip(me, bit):
    return me + bit - 2 * bit * lax.rem(me // bit, 2)


def greet_all(T, mine, peers):
    barrier = pltpu.get_barrier_semaphore()
    for peer in peers:
        pl.semaphore_signal(barrier, inc=1, device_id={"seq": peer}, device_id_type=MESH)
    for d in range(1, T):
        pl.semaphore_signal(barrier, inc=1, device_id={"tok": lax.rem(mine + d, T)}, device_id_type=MESH)
    pl.semaphore_wait(barrier, T - 1 + len(peers))


def gather_rows(L, src, out, send, recv):
    me = lax.axis_index("seq")
    px, py = flip(me, 1), flip(me, 2)
    H = L // CHUNKS

    def copy(c, k):
        f, g = (px, py) if c % 2 == 0 else (py, px)
        rows = pl.ds(c * H, H)
        sems = send.at[c, k], recv.at[c, k], "seq"
        if k == 2:
            place = out.at[f, rows, :]
            return remote(place, place, *sems, g)
        return remote(src.at[rows, :], out.at[me, rows, :], *sems, (f, g)[k])

    def start():
        for k in (0, 1):
            for c in range(CHUNKS):
                copy(c, k).start()

    def forward():
        for c in range(CHUNKS):
            copy(c, 0).wait_recv()
            copy(c, 2).start()

    def drain():
        for c in range(CHUNKS):
            copy(c, 0).wait_send()
            copy(c, 1).wait()
            copy(c, 2).wait()

    return start, forward, drain


def sum_rows(L, part, one_s, two_s, two_out, one_send, one_recv, two_send, two_recv):
    me = lax.axis_index("seq")
    px, py, pd = flip(me, 1), flip(me, 2), 3 - me
    H = L // CHUNKS

    def peers(c):
        return (px, py) if c % 2 == 0 else (py, px)

    def rows(c):
        return pl.ds(c * H, H)

    def one(c, k):
        f, _ = peers(c)
        src = (f, pd)[k]
        return remote(part.at[src, rows(c), :], one_s.at[c, k], one_send.at[c, k], one_recv.at[c, k], "seq", f)

    def two(c):
        return remote(two_out.at[c], two_s.at[c], two_send.at[c], two_recv.at[c], "seq", peers(c)[1])

    def start():
        for c in range(CHUNKS):
            for k in (1, 0):
                one(c, k).start()

    def middle(c):
        one(c, 1).wait_recv()
        two_out[c] = (part[peers(c)[1], rows(c), :].astype(F32) + one_s[c, 1].astype(F32)).astype(BF)
        two(c).start()

    def total(c):
        one(c, 0).wait_recv()
        two(c).wait_recv()
        return part[me, rows(c), :].astype(F32) + one_s[c, 0].astype(F32) + two_s[c].astype(F32)

    def drain():
        for c in range(CHUNKS):
            for k in (0, 1):
                one(c, k).wait_send()
            two(c).wait_send()

    return start, middle, total, drain


def sum_scratch(L, D):
    H = L // CHUNKS
    dma = pltpu.SemaphoreType.DMA
    return [
        pltpu.VMEM((CHUNKS, 2, H, D), BF),
        pltpu.VMEM((CHUNKS, H, D), BF),
        pltpu.VMEM((CHUNKS, H, D), BF),
        dma((CHUNKS, 2)),
        dma((CHUNKS, 2)),
        dma((CHUNKS,)),
        dma((CHUNKS,)),
    ]


def minus_expm1(x, whole):
    series = 1.0 + x * (1.0 / 7)
    for n in (6, 5, 4, 3, 2):
        series = 1.0 + x * (1.0 / n) * series
    return jnp.where(x > -0.5, -x * series, 1.0 - whole)


def gelu_parts(v):
    inner = 0.7978845608028654 * (v + 0.044715 * (v * v * v))
    th = jnp.tanh(inner)
    value = 0.5 * v * (1.0 + th)
    slope = 0.5 * (1.0 + th) + 0.5 * v * (1.0 - th * th) * 0.7978845608028654 * (
        1.0 + 3 * 0.044715 * (v * v)
    )
    return value, slope


def dot(a, b, dims=((1,), (0,))):
    return lax.dot_general(a, b, (dims, ((), ())), preferred_element_type=F32)


LANE = 128


def wide(ref, rows, col):
    return jnp.concatenate([ref[c, rows, :] for c in range(col // LANE, (col + BW) // LANE)], axis=1)


def put_wide(ref, rows, col, value):
    for c in range(BW // LANE):
        ref[col // LANE + c, rows, :] = value[:, c * LANE : (c + 1) * LANE]


def over_tiles(S, L, C, step):
    per = L // TILE

    @pl.loop(0, S * per)
    def _(i):
        for col in range(0, C, BW):
            step(i // per, pl.multiple_of(lax.rem(i, per) * TILE, TILE), col)


def recur_forward(
    T, S, L, C, xy_ref, rows_ref, wd_ref, wi_ref, cot_ref,
    mixed_ref, states_ref, conv_ref, x_ref, halo_ref, inc_ref, cots_ref,
    a_s, b_s, ext_s, fin_s, got_s, halo_send, halo_recv, send_sem, recv_sem, cot_send, cot_recv, own_sem,
):
    t = lax.axis_index("tok")
    SL = S * L // 8
    half = 8 // S
    me = lax.axis_index("seq")
    greet_all(T, t, (flip(me, 1), flip(me, 2)))
    start_cot, forward_cot, drain_cot = gather_rows(L, cot_ref, cots_ref, cot_send, cot_recv)
    own_cot = pltpu.make_async_copy(cot_ref, cots_ref.at[me], own_sem)
    for q in range(S):
        x_ref[q, L - LAP : L, :] = xy_ref[q, L - LAP : L, 0:C].astype(BF)
    lap = remote(x_ref.at[:, pl.ds(L - LAP, LAP), :], halo_ref, halo_send, halo_recv, "tok", lax.rem(t + 1, T))

    @pl.when(t < T - 1)
    def _():
        lap.start()

    start_cot()
    own_cot.start()

    @pl.when(t > 0)
    def _():
        lap.wait_recv()

    @pl.when(t == 0)
    def _():
        halo_ref[...] = jnp.zeros_like(halo_ref)

    def make(q, r0, col):
        cs = pl.ds(col, BW)

        @pl.when(r0 == 0)
        def _():
            ext_s[0:8, cs] = halo_ref[q, :, cs].astype(F32)[8:16]

        @pl.when(r0 > 0)
        def _():
            ext_s[0:8, cs] = ext_s[TILE : TILE + 8, cs]

        low_x = xy_ref[q, pl.ds(r0, TILE), cs].astype(BF)

        @pl.when(r0 < L - TILE)
        def _():
            x_ref[q, pl.ds(r0, TILE), cs] = low_x

        @pl.when(r0 == L - TILE)
        def _():
            x_ref[q, L - TILE : L - LAP, cs] = low_x[: TILE - LAP]

        ext_s[8 : 8 + TILE, cs] = low_x.astype(F32)
        conv = rows_ref[4:5, cs] + jnp.zeros((TILE, BW), F32)
        for k in range(CONV):
            conv = conv + ext_s[5 + k : 5 + k + TILE, cs] * rows_ref[k : k + 1, cs]
        low = conv.astype(BF)
        conv_ref[q, pl.ds(r0, TILE), cs] = low
        vals = low.astype(F32)
        gate = dot(low, wd_ref[cs, :]) + rows_ref[5:6, cs]
        inp = dot(low, wi_ref[cs, :]) + rows_ref[6:7, cs]
        log = -jax.nn.sigmoid(gate) * rows_ref[8:9, cs]
        a = jnp.exp(log)
        b = jnp.sqrt(minus_expm1(2.0 * log, a * a)) * jax.nn.sigmoid(inp) * vals
        here = pl.ds(pl.multiple_of(q * L + r0, TILE), TILE)
        put_wide(a_s, here, col, a)
        put_wide(b_s, here, col, b)

    over_tiles(S, L, C, make)
    forward_cot()

    NC = C // LANE

    def walk(i, carry):
        at = pl.ds(i, 8, stride=SL)
        out = []
        for c, (h, p) in enumerate(carry):
            a = a_s[c, at, :]
            h = a * h + b_s[c, at, :]
            p = a * p
            a_s[c, at, :] = p
            b_s[c, at, :] = h
            out.append((h, p))
        return tuple(out)

    start = tuple((jnp.zeros((8, LANE), F32), jnp.ones((8, LANE), F32)) for _ in range(NC))
    for c, (h, p) in enumerate(lax.fori_loop(0, SL, walk, start, unroll=4)):
        fin_s[c, 0:8, :] = p
        fin_s[c, 8:16, :] = h

    def ship(j, _):
        remote(fin_s, got_s.at[t], send_sem.at[j], recv_sem.at[t], "tok", j).start()
        return 0

    lax.fori_loop(t + 1, T, ship, 0)

    def fold(j, incs):
        remote(fin_s, got_s.at[j], send_sem.at[j], recv_sem.at[j], "tok", t).wait_recv()
        out = []
        for c, inc in enumerate(incs):
            for k in range(half):
                pj = got_s[j, c, pl.ds(k, S, stride=half), :]
                hj = got_s[j, c, pl.ds(8 + k, S, stride=half), :]
                inc = pj * inc + hj
            out.append(inc)
        return tuple(out)

    for c, inc in enumerate(lax.fori_loop(0, t, fold, tuple(jnp.zeros((S, LANE), F32) for _ in range(NC)))):
        for k in range(half):
            inc_ref[c, pl.ds(k, S, stride=half), :] = inc
            if k < half - 1:
                inc = fin_s[c, pl.ds(k, S, stride=half), :] * inc + fin_s[c, pl.ds(8 + k, S, stride=half), :]

    def finish(q, r0, col):
        cs = pl.ds(col, BW)
        row = q * L + r0
        here = pl.ds(pl.multiple_of(row, TILE), TILE)
        st = wide(b_s, here, col) + wide(a_s, here, col) * wide(inc_ref, pl.ds(row // SL, 1), col)
        states_ref[here, cs] = st
        value, _ = gelu_parts(xy_ref[q, pl.ds(r0, TILE), pl.ds(C + col, BW)])
        mixed_ref[here, cs] = (st * value).astype(BF)

    over_tiles(S, L, C, finish)

    def drain(j, _):
        remote(fin_s, got_s.at[t], send_sem.at[j], recv_sem.at[t], "tok", j).wait_send()
        return 0

    lax.fori_loop(t + 1, T, drain, 0)

    @pl.when(t < T - 1)
    def _():
        lap.wait_send()

    drain_cot()
    own_cot.wait()


def recur_backward(
    T, S, L, C, gm_ref, xy_ref, st_ref, conv_ref, x_ref, halo_ref, inc_ref, rows_ref, wd_ref, wi_ref, part_ref, resid_ref,
    gxy_ref, gwd_ref, gwi_ref, small_ref, block_ref,
    a_s, g_s, r_s, sg_s, si_s, gc_s, ext_s, pst_s, fin_s, got_s, car_s, lap_send, lap_recv, send_sem, recv_sem,
    *sum_refs,
):
    t = lax.axis_index("tok")
    SL = S * L // 8
    half = 8 // S
    me = lax.axis_index("seq")
    greet_all(T, t, (flip(me, 1), flip(me, 2)))
    start_sum, middle_sum, total_sum, drain_sum = sum_rows(L, part_ref, *sum_refs)
    start_sum()

    def prepare(q, r0, col):
        cs = pl.ds(col, BW)
        here = pl.ds(pl.multiple_of(q * L + r0, TILE), TILE)
        low = conv_ref[q, pl.ds(r0, TILE), cs]
        sg = jax.nn.sigmoid(dot(low, wd_ref[cs, :]) + rows_ref[5:6, cs])
        sg_s[here, cs] = sg
        si_s[here, cs] = jax.nn.sigmoid(dot(low, wi_ref[cs, :]) + rows_ref[6:7, cs])
        put_wide(a_s, here, col, jnp.exp(-sg * rows_ref[8:9, cs]))
        value, slope = gelu_parts(xy_ref[q, pl.ds(r0, TILE), pl.ds(C + col, BW)])
        gm = gm_ref[here, cs]
        put_wide(g_s, here, col, gm * value)
        gxy_ref[q, pl.ds(r0, TILE), pl.ds(C + col, BW)] = (gm * st_ref[here, cs] * slope).astype(BF)

    over_tiles(S, L, C, prepare)

    NC = C // LANE

    def walk(i, carry):
        at = pl.ds(SL - 1 - i, 8, stride=SL)
        out = []
        for c, (e, r) in enumerate(carry):
            a = a_s[c, at, :]
            adj = g_s[c, at, :] + e
            g_s[c, at, :] = adj
            r_s[c, at, :] = r
            out.append((a * adj, a * r))
        return tuple(out)

    start = tuple((jnp.zeros((8, LANE), F32), jnp.ones((8, LANE), F32)) for _ in range(NC))
    for c, (e, r) in enumerate(lax.fori_loop(0, SL, walk, start, unroll=4)):
        fin_s[c, 0:8, :] = r
        fin_s[c, 8:16, :] = e

    def ship(j, _):
        remote(fin_s, got_s.at[t], send_sem.at[j], recv_sem.at[t], "tok", j).start()
        return 0

    lax.fori_loop(0, t, ship, 0)

    def fold(i, cars):
        j = T - 1 - i
        remote(fin_s, got_s.at[j], send_sem.at[j], recv_sem.at[j], "tok", t).wait_recv()
        out = []
        for c, car in enumerate(cars):
            for k in reversed(range(half)):
                rj = got_s[j, c, pl.ds(k, S, stride=half), :]
                ej = got_s[j, c, pl.ds(8 + k, S, stride=half), :]
                car = rj * car + ej
            out.append(car)
        return tuple(out)

    for c, car in enumerate(lax.fori_loop(0, T - 1 - t, fold, tuple(jnp.zeros((S, LANE), F32) for _ in range(NC)))):
        for k in reversed(range(half)):
            car_s[c, pl.ds(k, S, stride=half), :] = car
            if k > 0:
                car = fin_s[c, pl.ds(k, S, stride=half), :] * car + fin_s[c, pl.ds(8 + k, S, stride=half), :]

    for c in range(CHUNKS):
        middle_sum(c)
    small_ref[...] = jnp.zeros_like(small_ref)
    gwd_ref[...] = jnp.zeros_like(gwd_ref)
    gwi_ref[...] = jnp.zeros_like(gwi_ref)

    def add_row(k, cs, value):
        small_ref[k : k + 1, cs] += jnp.sum(value, axis=0, keepdims=True)

    def chain(q, r0, col):
        cs = pl.ds(col, BW)
        row = q * L + r0
        here = pl.ds(pl.multiple_of(row, TILE), TILE)

        @pl.when(r0 == 0)
        def _():
            pst_s[0:8, cs] = wide(inc_ref, pl.ds(q * half, 1), col) + jnp.zeros((8, BW), F32)

        @pl.when(r0 > 0)
        def _():
            pst_s[0:8, cs] = pst_s[TILE : TILE + 8, cs]

        pst_s[8 : 8 + TILE, cs] = st_ref[here, cs]
        adj = wide(g_s, here, col) + wide(r_s, here, col) * wide(car_s, pl.ds(row // SL, 1), col)
        sg, si, a = sg_s[here, cs], si_s[here, cs], wide(a_s, here, col)
        low = conv_ref[q, pl.ds(r0, TILE), cs]
        vals = low.astype(F32)
        sp = rows_ref[8:9, cs]
        square = a * a
        scale = jnp.sqrt(minus_expm1(-2.0 * sg * sp, square))
        grad_log = adj * pst_s[7 : 7 + TILE, cs] * a - adj * si * vals * square / scale
        grad_gate = (-grad_log * sp * sg * (1.0 - sg)).astype(BF)
        add_row(7, cs, -grad_log * sg)
        grad_inp = (adj * scale * vals * si * (1.0 - si)).astype(BF)
        add_row(5, cs, grad_gate.astype(F32))
        add_row(6, cs, grad_inp.astype(F32))
        gc = (
            adj * scale * si
            + dot(grad_gate, wd_ref[cs, :], ((1,), (1,)))
            + dot(grad_inp, wi_ref[cs, :], ((1,), (1,)))
        )
        gc_s[q, pl.ds(r0, TILE), cs] = gc
        add_row(4, cs, gc)
        gwd_ref[cs, :] += dot(low, grad_gate, ((0,), (0,)))
        gwi_ref[cs, :] += dot(low, grad_inp, ((0,), (0,)))

    over_tiles(S, L, C, chain)
    small_ref[7:8, :] *= 8.0 * rows_ref[9:10, :]

    lap = remote(gc_s.at[:, pl.ds(0, 8), :], gc_s.at[:, pl.ds(L, 8), :], lap_send, lap_recv, "tok", lax.rem(t + T - 1, T))

    @pl.when(t > 0)
    def _():
        lap.start()

    for c in range(CHUNKS):
        rows = pl.ds(c * (L // CHUNKS), L // CHUNKS)
        block_ref[rows, :] = (resid_ref[rows, :] + total_sum(c)).astype(BF)

    @pl.when(t < T - 1)
    def _():
        lap.wait_recv()

    @pl.when(t == T - 1)
    def _():
        gc_s[:, pl.ds(L, 8), :] = jnp.zeros((S, 8, C), F32)

    def taps(q, r0, col):
        cs = pl.ds(col, BW)

        @pl.when(r0 == 0)
        def _():
            ext_s[0:8, cs] = halo_ref[q, :, cs].astype(F32)[8:16]

        @pl.when(r0 > 0)
        def _():
            ext_s[0:8, cs] = ext_s[TILE : TILE + 8, cs]

        ext_s[8 : 8 + TILE, cs] = x_ref[q, pl.ds(r0, TILE), cs].astype(F32)
        pst_s[0 : TILE + 8, cs] = gc_s[q, pl.ds(r0, TILE + 8), cs]
        gc = pst_s[0:TILE, cs]
        gx = jnp.zeros((TILE, BW), F32)
        for k in range(CONV):
            add_row(k, cs, gc * ext_s[5 + k : 5 + k + TILE, cs])
            gx = gx + pst_s[3 - k : 3 - k + TILE, cs] * rows_ref[k : k + 1, cs]
        gxy_ref[q, pl.ds(r0, TILE), cs] = gx.astype(BF)

    over_tiles(S, L, C, taps)

    def drain(j, _):
        remote(fin_s, got_s.at[t], send_sem.at[j], recv_sem.at[t], "tok", j).wait_send()
        return 0

    lax.fori_loop(0, t, drain, 0)

    @pl.when(t > 0)
    def _():
        lap.wait_send()

    drain_sum()


VM = pl.BlockSpec(memory_space=pltpu.VMEM)


def shape(dims, kind=F32):
    return jax.ShapeDtypeStruct(dims, kind)


def params(collective_id, mib=58):
    return pltpu.CompilerParams(
        collective_id=collective_id, has_side_effects=True, vmem_limit_bytes=mib * 1024 * 1024
    )


def run_forward(T, branches, rows, wd, wi, cot):
    S, L, C = branches.shape
    hbm = pl.BlockSpec(memory_space=pl.ANY)
    C //= 2
    M = S * L
    dma = pltpu.SemaphoreType.DMA
    split = pltpu.VMEM((C // LANE, M, LANE), F32)
    return pl.pallas_call(
        functools.partial(recur_forward, T, S, L, C),
        out_shape=(
            shape((M, C), BF),
            shape((M, C)),
            shape((S, L, C), BF),
            shape((S, L, C), BF),
            shape((S, LAP, C), BF),
            shape((C // LANE, 8, LANE)),
            shape((S,) + cot.shape, BF),
        ),
        in_specs=[VM] * 4 + [hbm],
        out_specs=(VM,) * 6 + (hbm,),
        scratch_shapes=[
            split,
            split,
            pltpu.VMEM((TILE + 8, C), F32),
            pltpu.VMEM((C // LANE, 16, LANE), F32),
            pltpu.VMEM((T, C // LANE, 16, LANE), F32),
            dma,
            dma,
            dma((T,)),
            dma((T,)),
            dma((CHUNKS, 3)),
            dma((CHUNKS, 3)),
            dma,
        ],
        compiler_params=params(0),
        cost_estimate=pl.CostEstimate(flops=4 * M * C * BW, bytes_accessed=100000000, transcendentals=6 * M * C),
    )(branches, rows, wd, wi, cot)


def run_backward(T, grad_mixed, branches, states, conv, branch_x, halo, inc, rows, wd, wi, part, resid):
    S, L, C = branch_x.shape
    M = S * L
    dma = pltpu.SemaphoreType.DMA
    big = pltpu.VMEM((M, C), F32)
    split = pltpu.VMEM((C // LANE, M, LANE), F32)
    return pl.pallas_call(
        functools.partial(recur_backward, T, S, L, C),
        out_shape=(
            shape((S, L, 2 * C), BF),
            shape((C, BW)),
            shape((C, BW)),
            shape((8, C)),
            shape(resid.shape, BF),
        ),
        in_specs=[VM] * 12,
        out_specs=(VM,) * 5,
        scratch_shapes=[split] * 3
        + [big] * 2
        + [
            pltpu.VMEM((S, L + 8, C), F32),
            pltpu.VMEM((TILE + 8, C), F32),
            pltpu.VMEM((TILE + 8, C), F32),
            pltpu.VMEM((C // LANE, 16, LANE), F32),
            pltpu.VMEM((T, C // LANE, 16, LANE), F32),
            pltpu.VMEM((C // LANE, 8, LANE), F32),
            dma,
            dma,
            dma((T,)),
            dma((T,)),
        ]
        + sum_scratch(*resid.shape),
        compiler_params=params(1),
        cost_estimate=pl.CostEstimate(flops=12 * M * C * BW, bytes_accessed=180000000, transcendentals=6 * M * C),
    )(grad_mixed, branches, states, conv, branch_x, halo, inc, rows, wd, wi, part, resid)


def root_scale(v):
    return lax.rsqrt(jnp.mean(v * v, axis=-1, keepdims=True) + eps)


def rms_back(v, gain, grad):
    scale = root_scale(v)
    hat = v * scale
    inner = grad * gain
    return scale * (inner - hat * jnp.mean(inner * hat, axis=-1, keepdims=True))


def plane_sum(kind, L, D, *refs):
    shares = kind in ("first", "second")
    part = refs[0]
    if kind == "first":
        tokens, gain, keep, everyone = refs[1:5]
        rest = refs[5:]
    elif kind == "second":
        resid, gain, cot, weight, keep, everyone = refs[1:7]
        rest = refs[7:]
    else:
        tokens, gain, before, keep = refs[1:5]
        rest = refs[5:]
    if shares:
        own_s, all_send, all_recv, own_sem = rest[7:]
    me = lax.axis_index("seq")
    H = L // CHUNKS
    px, py = flip(me, 1), flip(me, 2)
    barrier = pltpu.get_barrier_semaphore()
    for peer in (px, py):
        pl.semaphore_signal(barrier, inc=1, device_id={"seq": peer}, device_id_type=MESH)
    pl.semaphore_wait(barrier, 2)
    start, middle, sums, drain = sum_rows(L, part, *rest[:7])

    def rows(c):
        return pl.ds(c * H, H)

    def share(c, k):
        f, g = (px, py) if c % 2 == 0 else (py, px)
        if k == 2:
            place = everyone.at[f, rows(c), :]
            return remote(place, place, all_send.at[c, k], all_recv.at[c, k], "seq", g)
        place = everyone.at[me, rows(c), :]
        return remote(own_s.at[rows(c), :], place, all_send.at[c, k], all_recv.at[c, k], "seq", (f, g)[k])

    def own(c):
        return pltpu.make_async_copy(own_s.at[rows(c), :], everyone.at[me, rows(c), :], own_sem.at[c])

    def finish(c):
        total = sums(c)
        r = rows(c)
        if kind == "first":
            total = tokens[r, :].astype(F32) + total
            keep[r, :] = total
            own_s[r, :] = (total * root_scale(total) * gain[0:1, :]).astype(BF)
        elif kind == "second":
            back = rms_back(resid[r, :], gain[0:1, :], total)
            total = cot[r, :].astype(F32) * weight[0:1, 0:1] + back
            keep[r, :] = total
            own_s[r, :] = total.astype(BF)
        else:
            back = rms_back(tokens[r, :].astype(F32), gain[0:1, :], total)
            keep[r, :] = before[r, :] + back
        if shares:
            share(c, 0).start()
            share(c, 1).start()
            own(c).start()

    def forward(c):
        share(c, 0).wait_recv()
        share(c, 2).start()

    start()
    for c in range(CHUNKS):
        middle(c)
        if c > 0:
            finish(c - 1)
        if shares and c > 1:
            forward(c - 2)
    finish(CHUNKS - 1)
    if shares:
        forward(CHUNKS - 2)
        forward(CHUNKS - 1)
    drain()
    if shares:
        for c in range(CHUNKS):
            for k in (1, 2):
                share(c, k).wait_recv()
            for k in (0, 1, 2):
                share(c, k).wait_send()
            own(c).wait()


def run_plane(kind, collective_id, part, *ins):
    S, L, D = part.shape
    dma = pltpu.SemaphoreType.DMA
    shares = kind in ("first", "second")
    outs = [shape((L, D))]
    specs = [VM]
    if shares:
        outs.append(shape((S, L, D), BF))
        specs.append(pl.BlockSpec(memory_space=pl.ANY))
    scratch = sum_scratch(L, D)
    if shares:
        scratch += [pltpu.VMEM((L, D), BF), dma((CHUNKS, 3)), dma((CHUNKS, 3)), dma((CHUNKS,))]
    return pl.pallas_call(
        functools.partial(plane_sum, kind, L, D),
        out_shape=tuple(outs),
        in_specs=[VM] * (1 + len(ins)),
        out_specs=tuple(specs),
        scratch_shapes=scratch,
        compiler_params=params(collective_id, 40),
        cost_estimate=pl.CostEstimate(
            flops=40 * L * D, bytes_accessed=(240 if shares else 120) * 1000000, transcendentals=L
        ),
    )(part, *ins)


def plane_swap(modes, *refs):
    n = len(modes)
    ins, outs = refs[:n], refs[n : 2 * n]
    send, recv, own_sem = refs[2 * n :]
    me = lax.axis_index("seq")
    S = lax.axis_size("seq")
    greet("seq", S, me)

    def copy(i, d):
        to = lax.rem(me + d, S)
        src = ins[i] if modes[i] == "all" else ins[i].at[to]
        return remote(src, outs[i].at[me], send.at[i, d], recv.at[i, d], "seq", to)

    def own(i):
        src = ins[i] if modes[i] == "all" else ins[i].at[me]
        return pltpu.make_async_copy(src, outs[i].at[me], own_sem.at[i])

    for i in range(n):
        for d in range(1, S):
            copy(i, d).start()
        own(i).start()
    for i in range(n):
        for d in range(1, S):
            copy(i, d).wait()
        own(i).wait()


def run_swap(S, modes, collective_id, *ins):
    n = len(modes)
    dma = pltpu.SemaphoreType.DMA
    outs = tuple(shape(((S,) if m == "all" else ()) + x.shape, x.dtype) for m, x in zip(modes, ins))
    size = sum(3 * x.size * x.dtype.itemsize // (1 if m == "all" else S) for m, x in zip(modes, ins))
    hbm = pl.BlockSpec(memory_space=pl.ANY)
    return pl.pallas_call(
        functools.partial(plane_swap, modes),
        out_shape=outs,
        in_specs=[hbm] * n,
        out_specs=(hbm,) * n,
        scratch_shapes=[dma((n, S)), dma((n, S)), dma((n,))],
        compiler_params=params(collective_id, 4),
        cost_estimate=pl.CostEstimate(flops=0, bytes_accessed=size * 40, transcendentals=0),
    )(*ins)


def plane_fill(S, T, L, slabs, *refs):
    pack, first, gates, pack_out, first_out, gates_out, lent = refs[:7]
    pack_send, pack_recv, row_send, row_recv, gate_send, gate_recv, relay_send, relay_recv = refs[7:15]
    lent_send, lent_recv, own_sem = refs[15:]
    me, t = lax.axis_index("seq"), lax.axis_index("tok")
    px, py, pd = flip(me, 1), flip(me, 2), S - 1 - me
    barrier = pltpu.get_barrier_semaphore()
    for peer in (px, py, pd):
        pl.semaphore_signal(barrier, inc=1, device_id={"seq": peer}, device_id_type=MESH)

    @pl.loop(1, T // 2)
    def _(d):
        pl.semaphore_signal(barrier, inc=1, device_id={"tok": lax.rem(t + 2 * d, T)}, device_id_type=MESH)

    mate = flip(t, 1)
    pl.semaphore_signal(barrier, inc=1, device_id={"tok": mate}, device_id_type=MESH)
    pl.semaphore_wait(barrier, S - 1 + T // 2)

    def gate(d):
        return remote(gates, gates_out.at[t], gate_send.at[d], gate_recv.at[d], "tok", lax.rem(t + 2 * d, T))

    def relay(d):
        place = gates_out.at[lax.rem(t - 2 * d + T, T)]
        return remote(place, place, relay_send.at[d], relay_recv.at[d], "tok", mate)

    def piece(k):
        to = (pd, px, py)[k]
        return remote(pack.at[to], pack_out.at[me], pack_send.at[k], pack_recv.at[k], "seq", to)

    mine = [
        pltpu.make_async_copy(pack.at[me], pack_out.at[me], own_sem.at[0]),
        pltpu.make_async_copy(first, first_out.at[me], own_sem.at[1]),
        pltpu.make_async_copy(gates, gates_out.at[t], own_sem.at[2]),
    ]
    loan = remote(gates_out.at[pl.ds(0, slabs)], lent, lent_send, lent_recv, "seq", px)
    start, forward, drain = gather_rows(L, first, first_out, row_send, row_recv)

    @pl.loop(1, T // 2)
    def _(d):
        gate(d).start()

    for copy in mine:
        copy.start()
    start()
    for k in range(3):
        piece(k).start()
    mine[2].wait()
    relay(0).start()

    @pl.loop(1, T // 2)
    def _(d):
        gate(d).wait_recv()
        relay(d).start()

    @pl.loop(0, T // 2)
    def _(d):
        relay(d).wait_recv()

    @pl.when(lax.rem(me, 2) == 1)
    def _():
        loan.start()

    forward()
    for k in range(3):
        piece(k).wait()
    drain()
    for copy in mine[:2]:
        copy.wait()

    @pl.loop(1, T // 2)
    def _(d):
        gate(d).wait_send()

    @pl.loop(0, T // 2)
    def _(d):
        relay(d).wait_send()

    @pl.when(lax.rem(me, 2) == 1)
    def _():
        loan.wait_send()

    @pl.when(lax.rem(me, 2) == 0)
    def _():
        loan.wait_recv()


def run_fill(S, T, slabs, collective_id, pack, first, gates):
    L = first.shape[0]
    dma = pltpu.SemaphoreType.DMA
    hbm = pl.BlockSpec(memory_space=pl.ANY)
    return pl.pallas_call(
        functools.partial(plane_fill, S, T, L, slabs),
        out_shape=(
            shape(pack.shape, BF),
            shape((S,) + first.shape, BF),
            shape((T,) + gates.shape, BF),
            shape((slabs,) + gates.shape, BF),
        ),
        in_specs=[hbm] * 3,
        out_specs=(hbm,) * 4,
        scratch_shapes=[dma((3,))] * 2
        + [dma((CHUNKS, 3))] * 2
        + [dma((T // 2,))] * 4
        + [dma, dma, dma((3,))],
        compiler_params=params(collective_id, 4),
        cost_estimate=pl.CostEstimate(flops=0, bytes_accessed=220000000, transcendentals=0),
    )(pack, first, gates)


def after(value, *others):
    return lax.optimization_barrier((value,) + others)[0]


def body(
    tokens,
    source_ids,
    loss_weights,
    grad_output,
    first_gain,
    input_weight,
    gelu_weight,
    conv_weight,
    conv_bias,
    decay_gate,
    decay_bias,
    input_gate,
    input_bias,
    decay_param,
    output_weight,
    second_gain,
    gate_weight,
    up_weight,
    down_weight,
):
    S, T = lax.axis_size("seq"), lax.axis_size("tok")
    me = lax.axis_index("seq")
    length, D = tokens.shape[1:]
    ds, R = input_weight.shape
    rs = output_weight.shape[0]
    F = gate_weight.shape[1]
    FQ = F // S
    heads = R // BW
    starts = [-(-i * heads // S) for i in range(S + 1)]
    C = max(starts[i + 1] - starts[i] for i in range(S)) * BW
    quarter = R // S
    offs = [starts[i] * BW - i * quarter for i in range(S)] + [0]
    most = max(offs)
    off = sum(jnp.where(me == i, offs[i], 0) for i in range(S))
    own = sum(jnp.where(me == i, (starts[i + 1] - starts[i]) * BW, 0) for i in range(S))

    def cols_for(w):
        parts = [w[:, starts[i] * BW : starts[i + 1] * BW] for i in range(S)]
        return jnp.stack([jnp.pad(p, ((0, 0), (0, C - p.shape[1]))) for p in parts])

    def d_rows(w):
        return lax.all_gather(w, "tok", axis=1, tiled=True).reshape((D, w.shape[-1]))

    def d_scatter(g):
        return lax.psum_scatter(g.reshape(S, T * ds, g.shape[-1]), "tok", scatter_dimension=1, tiled=True)

    def r_align(g):
        g = lax.dynamic_update_slice_in_dim(jnp.zeros((quarter + 2 * most, g.shape[1]), BF), g.astype(BF), off, axis=0)
        back = from_behind(g[quarter : quarter + most], "seq", 1)
        keep = lax.broadcasted_iota(jnp.int32, (quarter, 1), 0) < off
        return jnp.where(keep, jnp.pad(back, ((0, quarter - most), (0, 0))), g[:quarter])

    small = jnp.concatenate(
        [conv_weight, jnp.stack([conv_bias, decay_bias, input_bias, decay_param], axis=1)], axis=1
    )
    small = jnp.pad(small, ((0, 0), (0, SMALL - small.shape[1])))
    gates = jnp.concatenate([decay_gate, input_gate, small], axis=1)
    gains = jnp.pad(jnp.stack([first_gain, second_gain], axis=1), ((0, 0), (0, SMALL - 2)))
    pack_in = jnp.concatenate(
        [cols_for(input_weight), cols_for(gelu_weight), jnp.broadcast_to(gains, (S,) + gains.shape)], axis=2
    )
    (pack_in,) = run_swap(S, ("slice",), 2, pack_in)
    sources = lax.broadcasted_iota(jnp.int32, (1, loss_weights.shape[0]), 1)
    picked = jnp.sum(jnp.where(source_ids[:, None] == sources, loss_weights[None, :], 0.0), axis=1)
    cot_low = (grad_output[0].astype(F32) * picked[:, None]).astype(BF)
    pack_f = jnp.concatenate([w.reshape(ds, S, FQ).swapaxes(0, 1) for w in (gate_weight, up_weight)], axis=2)
    weight_out = gather(output_weight, "tok")
    pack_f, everyone, gates, lent = run_fill(
        S, T, -(-most // rs), 3, after(pack_f, pack_in, weight_out), tokens[0], gates
    )

    def r_rows(whole, lent):
        lent = lent[:most]
        whole = jnp.concatenate([whole, lent, jnp.zeros_like(lent)], axis=0)
        whole = lax.dynamic_slice_in_dim(whole, off, C, axis=0)
        return jnp.where(lax.broadcasted_iota(jnp.int32, whole.shape, 0) < own, whole, 0)

    pack_in = d_rows(pack_in)
    weight_xy = pack_in[:, : 2 * C]
    gain_one, gain_two = pack_in[:, 2 * C].astype(F32), pack_in[:, 2 * C + 1].astype(F32)
    gates = r_rows(gates.reshape(quarter, -1), lent.reshape(-1, lent.shape[-1]))
    weight_decay, weight_input = gates[:, :BW], gates[:, BW : 2 * BW]
    rows = gates[:, 2 * BW : 2 * BW + 8].T.astype(F32)
    param = rows[7:8]
    rows = jnp.concatenate(
        [rows, 8.0 * jax.nn.softplus(param), jax.nn.sigmoid(param), jnp.zeros((6, C), F32)], axis=0
    )
    weight_out = r_rows(weight_out, from_behind(weight_out[:most], "seq", -1))

    pack_f = d_rows(after(pack_f, pack_in))
    weight_gate, weight_up = pack_f[:, :FQ], pack_f[:, FQ:]

    everyone = everyone.astype(F32)
    normed = lax.optimization_barrier(rms_scale(everyone, gain_one).astype(BF))
    branches = forward_product(normed, weight_xy)
    weight_down = gather(after(down_weight, branches), "tok")
    mixed, states, conv_low, branch_x, halo, incoming, cot_low = run_forward(
        T, branches, rows, weight_decay, weight_input, cot_low
    )
    mixed = mixed.reshape(S, length, C)
    passed = from_behind(mixed[:, :, quarter:], "seq", 1)
    mixed_own = jnp.pad(mixed, ((0, 0), (0, 0), (most, 0)))[:, :, :quarter]
    mixed_own = jnp.where(off > 0, mixed_own, mixed[:, :, :quarter])
    mixed_own = jnp.where(
        lax.broadcasted_iota(jnp.int32, (1, 1, quarter), 2) < off,
        jnp.pad(passed, ((0, 0), (0, 0), (0, quarter - most))),
        mixed_own,
    )
    part = forward_product(mixed, weight_out).astype(BF)
    resid, second_normed = run_plane("first", 4, part, tokens[0], gain_two[None])

    gate_val = forward_product(second_normed, weight_gate)
    up_val = forward_product(second_normed, weight_up)
    hidden = gelu_product(gate_val, up_val).astype(BF)
    grad_down = token_product(hidden, cot_low).astype(BF)
    weight_down = after(weight_down, grad_down)
    grad_down = scatter(grad_down, "tok").astype(F32)

    grad_hidden = back_product(cot_low, weight_down)
    _, hidden_pull = jax.vjp(gelu_product, gate_val, up_val)
    grad_gate_val, grad_up_val = hidden_pull(grad_hidden)
    grad_gate_up = jnp.concatenate([grad_gate_val.astype(BF), grad_up_val.astype(BF)], axis=2)
    grad_pack = token_product(second_normed, grad_gate_up).astype(BF)
    grad_second = back_product(after(grad_gate_up, grad_pack), pack_f)
    grad_second = after(grad_second.astype(BF), grad_down)
    grad_pack = d_scatter(grad_pack)
    picked = jnp.broadcast_to(picked[None], (8, 128))
    grad_resid, resid_low = run_plane(
        "second", 6, grad_second, resid, gain_two[None], grad_output[0], picked
    )

    grad_out_w = token_product(mixed_own, resid_low).astype(BF)
    grad_mixed = back_product(after(resid_low, grad_out_w), weight_out)
    grad_out_w = scatter(grad_out_w, "tok").astype(F32)
    part = forward_product(hidden, weight_down).astype(BF)
    grad_xy, grad_decay_w, grad_input_w, smalls, block_out = run_backward(
        T, grad_mixed.reshape(S * length, C), branches, states, conv_low, branch_x, halo, incoming, rows,
        weight_decay, weight_input, part, resid,
    )
    grad_i = token_product(normed, after(grad_xy, grad_pack)).astype(BF)
    smalls = jnp.pad(smalls.T, ((0, 0), (0, BW - 8)))
    grad_r = r_align(after(jnp.concatenate([grad_decay_w, grad_input_w, smalls], axis=1), grad_i))
    grad_normed = back_product(after(grad_xy, grad_i), weight_xy)
    grad_normed = after(grad_normed, grad_out_w)

    grad_i = to_seq(d_scatter(grad_i)).astype(F32)
    (grad_tokens,) = run_plane("third", 7, grad_normed.astype(BF), tokens[0], gain_one[None], grad_resid)
    grad_r = scatter(grad_r, "tok").astype(F32)
    grad_pack = to_seq(grad_pack).swapaxes(0, 1).astype(F32)
    grad_gate_w = grad_pack[:, :, :FQ].reshape(ds, F)
    grad_up_w = grad_pack[:, :, FQ:].reshape(ds, F)

    def columns(at):
        return jnp.concatenate(
            [grad_i[i, :, at : at + (starts[i + 1] - starts[i]) * BW] for i in range(S)], axis=1
        )

    grad_in_w, grad_gelu_w = columns(0), columns(C)

    def gain_grad(gain, *pairs):
        return sum(jnp.sum(w.astype(F32) * g, axis=1) for w, g in pairs) / gain.astype(F32)

    smalls = grad_r[:, 2 * BW :]
    return (
        block_out[None],
        grad_tokens[None],
        gain_grad(first_gain, (input_weight, grad_in_w), (gelu_weight, grad_gelu_w)),
        grad_in_w,
        grad_gelu_w,
        smalls[:, :CONV],
        smalls[:, 4],
        grad_r[:, :BW],
        smalls[:, 5],
        grad_r[:, BW : 2 * BW],
        smalls[:, 6],
        smalls[:, 7],
        grad_out_w,
        gain_grad(second_gain, (gate_weight, grad_gate_w), (up_weight, grad_up_w)),
        grad_gate_w,
        grad_up_w,
        grad_down,
    )


def solution(mesh):
    one, two = P(("seq", "tok")), P(("seq", "tok"), None)
    data = P("seq", "tok", None)
    return jax.shard_map(
        body,
        mesh=mesh,
        in_specs=(data, P("seq"), P(), data, one, two, two, two, one, two, one, two, one, one, two, one, two, two, two),
        out_specs=(data, data, one, two, two, two, one, two, one, two, one, one, two, one, two, two, two),
        check_vma=False,
    )
```

```python
import functools

import jax
import jax.numpy as jnp
from jax import lax
from jax.experimental import pallas as pl
from jax.experimental.pallas import tpu as pltpu
from jax.sharding import PartitionSpec as P

BW = 256
CONV = 4
SMALL = 128
BF = jnp.bfloat16
F32 = jnp.float32
eps = 1e-06


def from_behind(block, axis, distance):
    devices = range(lax.axis_size(axis))
    route = [(i - distance, i) for i in devices if i - distance in devices]
    return lax.ppermute(block, axis, route)


def gelu(value):
    return jax.nn.gelu(value, approximate=True)


def rms_scale(value, gain):
    return value * lax.rsqrt(jnp.mean(value * value, axis=-1, keepdims=True) + eps) * gain


def gelu_product(gate_val, up_val):
    return gelu(gate_val) * up_val


def forward_product(left, weight):
    return jnp.dot(left, weight, preferred_element_type=F32)


def back_product(grad, weight):
    return lax.dot_general(grad, weight, (((2,), (1,)), ((), ())), preferred_element_type=F32)


def token_product(left, grad):
    return lax.dot_general(left, grad, (((0, 1), (0, 1)), ((), ())), preferred_element_type=F32)


def to_seq(parts):
    return lax.all_to_all(parts, "seq", split_axis=0, concat_axis=0, tiled=True)


def gather(value, axis):
    return lax.all_gather(value, axis, axis=0, tiled=True)


def scatter(value, axis):
    return lax.psum_scatter(value.astype(BF), axis, scatter_dimension=0, tiled=True)


MESH = pl.DeviceIdType.MESH
TILE = 128
LAP = 16


def greet(axis, count, mine):
    barrier = pltpu.get_barrier_semaphore()
    for d in range(1, count):
        pl.semaphore_signal(
            barrier, inc=1, device_id={axis: lax.rem(mine + d, count)}, device_id_type=MESH
        )
    pl.semaphore_wait(barrier, count - 1)


def remote(src, dst, send, recv, axis, to):
    return pltpu.make_async_remote_copy(
        src_ref=src, dst_ref=dst, send_sem=send, recv_sem=recv, device_id={axis: to}, device_id_type=MESH
    )


CHUNKS = 4


def flip(me, bit):
    return me + bit - 2 * bit * lax.rem(me // bit, 2)


def greet_all(T, mine, peers):
    barrier = pltpu.get_barrier_semaphore()
    for peer in peers:
        pl.semaphore_signal(barrier, inc=1, device_id={"seq": peer}, device_id_type=MESH)
    for d in range(1, T):
        pl.semaphore_signal(barrier, inc=1, device_id={"tok": lax.rem(mine + d, T)}, device_id_type=MESH)
    pl.semaphore_wait(barrier, T - 1 + len(peers))


def gather_rows(L, src, out, send, recv):
    me = lax.axis_index("seq")
    px, py = flip(me, 1), flip(me, 2)
    H = L // CHUNKS

    def copy(c, k):
        f, g = (px, py) if c % 2 == 0 else (py, px)
        rows = pl.ds(c * H, H)
        sems = send.at[c, k], recv.at[c, k], "seq"
        if k == 2:
            place = out.at[f, rows, :]
            return remote(place, place, *sems, g)
        return remote(src.at[rows, :], out.at[me, rows, :], *sems, (f, g)[k])

    def start():
        for k in (0, 1):
            for c in range(CHUNKS):
                copy(c, k).start()

    def forward():
        for c in range(CHUNKS):
            copy(c, 0).wait_recv()
            copy(c, 2).start()

    def drain():
        for c in range(CHUNKS):
            copy(c, 0).wait_send()
            copy(c, 1).wait()
            copy(c, 2).wait()

    return start, forward, drain


def sum_rows(L, part, one_s, two_s, two_out, one_send, one_recv, two_send, two_recv):
    me = lax.axis_index("seq")
    px, py, pd = flip(me, 1), flip(me, 2), 3 - me
    H = L // CHUNKS

    def peers(c):
        return (px, py) if c % 2 == 0 else (py, px)

    def rows(c):
        return pl.ds(c * H, H)

    def one(c, k):
        f, _ = peers(c)
        src = (f, pd)[k]
        return remote(part.at[src, rows(c), :], one_s.at[c, k], one_send.at[c, k], one_recv.at[c, k], "seq", f)

    def two(c):
        return remote(two_out.at[c], two_s.at[c], two_send.at[c], two_recv.at[c], "seq", peers(c)[1])

    def start():
        for c in range(CHUNKS):
            for k in (1, 0):
                one(c, k).start()

    def middle(c):
        one(c, 1).wait_recv()
        two_out[c] = (part[peers(c)[1], rows(c), :].astype(F32) + one_s[c, 1].astype(F32)).astype(BF)
        two(c).start()

    def total(c):
        one(c, 0).wait_recv()
        two(c).wait_recv()
        return part[me, rows(c), :].astype(F32) + one_s[c, 0].astype(F32) + two_s[c].astype(F32)

    def drain():
        for c in range(CHUNKS):
            for k in (0, 1):
                one(c, k).wait_send()
            two(c).wait_send()

    return start, middle, total, drain


def sum_scratch(L, D):
    H = L // CHUNKS
    dma = pltpu.SemaphoreType.DMA
    return [
        pltpu.VMEM((CHUNKS, 2, H, D), BF),
        pltpu.VMEM((CHUNKS, H, D), BF),
        pltpu.VMEM((CHUNKS, H, D), BF),
        dma((CHUNKS, 2)),
        dma((CHUNKS, 2)),
        dma((CHUNKS,)),
        dma((CHUNKS,)),
    ]


def minus_expm1(x, whole):
    series = 1.0 + x * (1.0 / 7)
    for n in (6, 5, 4, 3, 2):
        series = 1.0 + x * (1.0 / n) * series
    return jnp.where(x > -0.5, -x * series, 1.0 - whole)


def gelu_parts(v):
    inner = 0.7978845608028654 * (v + 0.044715 * (v * v * v))
    th = jnp.tanh(inner)
    value = 0.5 * v * (1.0 + th)
    slope = 0.5 * (1.0 + th) + 0.5 * v * (1.0 - th * th) * 0.7978845608028654 * (
        1.0 + 3 * 0.044715 * (v * v)
    )
    return value, slope


def dot(a, b, dims=((1,), (0,))):
    return lax.dot_general(a, b, (dims, ((), ())), preferred_element_type=F32)


LANE = 128


def wide(ref, rows, col):
    return jnp.concatenate([ref[c, rows, :] for c in range(col // LANE, (col + BW) // LANE)], axis=1)


def put_wide(ref, rows, col, value):
    for c in range(BW // LANE):
        ref[col // LANE + c, rows, :] = value[:, c * LANE : (c + 1) * LANE]


def over_tiles(S, L, C, step):
    per = L // TILE

    @pl.loop(0, S * per)
    def _(i):
        for col in range(0, C, BW):
            step(i // per, pl.multiple_of(lax.rem(i, per) * TILE, TILE), col)


def recur_forward(
    T, S, L, C, xy_ref, rows_ref, wd_ref, wi_ref, cot_ref,
    mixed_ref, own_ref, states_ref, conv_ref, x_ref, halo_ref, inc_ref, cots_ref,
    a_s, b_s, ext_s, fin_s, got_s, halo_send, halo_recv, send_sem, recv_sem, cot_send, cot_recv, own_sem,
    pass_send, pass_recv,
):
    t = lax.axis_index("tok")
    SL = S * L // 8
    half = 8 // S
    me = lax.axis_index("seq")
    greet_all(T, t, (flip(me, 1), flip(me, 2)))
    start_cot, forward_cot, drain_cot = gather_rows(L, cot_ref, cots_ref, cot_send, cot_recv)
    own_cot = pltpu.make_async_copy(cot_ref, cots_ref.at[me], own_sem)
    for q in range(S):
        x_ref[q, L - LAP : L, :] = xy_ref[q, L - LAP : L, 0:C].astype(BF)
    lap = remote(x_ref.at[:, pl.ds(L - LAP, LAP), :], halo_ref, halo_send, halo_recv, "tok", lax.rem(t + 1, T))

    @pl.when(t < T - 1)
    def _():
        lap.start()

    start_cot()
    own_cot.start()

    @pl.when(t > 0)
    def _():
        lap.wait_recv()

    @pl.when(t == 0)
    def _():
        halo_ref[...] = jnp.zeros_like(halo_ref)

    def make(q, r0, col):
        cs = pl.ds(col, BW)

        @pl.when(r0 == 0)
        def _():
            ext_s[0:8, cs] = halo_ref[q, :, cs].astype(F32)[8:16]

        @pl.when(r0 > 0)
        def _():
            ext_s[0:8, cs] = ext_s[TILE : TILE + 8, cs]

        low_x = xy_ref[q, pl.ds(r0, TILE), cs].astype(BF)

        @pl.when(r0 < L - TILE)
        def _():
            x_ref[q, pl.ds(r0, TILE), cs] = low_x

        @pl.when(r0 == L - TILE)
        def _():
            x_ref[q, L - TILE : L - LAP, cs] = low_x[: TILE - LAP]

        ext_s[8 : 8 + TILE, cs] = low_x.astype(F32)
        conv = rows_ref[4:5, cs] + jnp.zeros((TILE, BW), F32)
        for k in range(CONV):
            conv = conv + ext_s[5 + k : 5 + k + TILE, cs] * rows_ref[k : k + 1, cs]
        low = conv.astype(BF)
        conv_ref[q, pl.ds(r0, TILE), cs] = low
        vals = low.astype(F32)
        gate = dot(low, wd_ref[cs, :]) + rows_ref[5:6, cs]
        inp = dot(low, wi_ref[cs, :]) + rows_ref[6:7, cs]
        log = -jax.nn.sigmoid(gate) * rows_ref[8:9, cs]
        a = jnp.exp(log)
        b = jnp.sqrt(minus_expm1(2.0 * log, a * a)) * jax.nn.sigmoid(inp) * vals
        here = pl.ds(pl.multiple_of(q * L + r0, TILE), TILE)
        put_wide(a_s, here, col, a)
        put_wide(b_s, here, col, b)

    over_tiles(S, L, C, make)
    forward_cot()

    NC = C // LANE

    def walk(i, carry):
        at = pl.ds(i, 8, stride=SL)
        out = []
        for c, (h, p) in enumerate(carry):
            a = a_s[c, at, :]
            h = a * h + b_s[c, at, :]
            p = a * p
            a_s[c, at, :] = p
            b_s[c, at, :] = h
            out.append((h, p))
        return tuple(out)

    start = tuple((jnp.zeros((8, LANE), F32), jnp.ones((8, LANE), F32)) for _ in range(NC))
    for c, (h, p) in enumerate(lax.fori_loop(0, SL, walk, start, unroll=4)):
        fin_s[c, 0:8, :] = p
        fin_s[c, 8:16, :] = h

    def ship(j, _):
        remote(fin_s, got_s.at[t], send_sem.at[j], recv_sem.at[t], "tok", j).start()
        return 0

    lax.fori_loop(t + 1, T, ship, 0)

    def fold(j, incs):
        remote(fin_s, got_s.at[j], send_sem.at[j], recv_sem.at[j], "tok", t).wait_recv()
        out = []
        for c, inc in enumerate(incs):
            for k in range(half):
                pj = got_s[j, c, pl.ds(k, S, stride=half), :]
                hj = got_s[j, c, pl.ds(8 + k, S, stride=half), :]
                inc = pj * inc + hj
            out.append(inc)
        return tuple(out)

    for c, inc in enumerate(lax.fori_loop(0, t, fold, tuple(jnp.zeros((S, LANE), F32) for _ in range(NC)))):
        for k in range(half):
            inc_ref[c, pl.ds(k, S, stride=half), :] = inc
            if k < half - 1:
                inc = fin_s[c, pl.ds(k, S, stride=half), :] * inc + fin_s[c, pl.ds(8 + k, S, stride=half), :]

    def finish(q, r0, col):
        cs = pl.ds(col, BW)
        row = q * L + r0
        here = pl.ds(pl.multiple_of(row, TILE), TILE)
        st = wide(b_s, here, col) + wide(a_s, here, col) * wide(inc_ref, pl.ds(row // SL, 1), col)
        states_ref[here, cs] = st
        value, _ = gelu_parts(xy_ref[q, pl.ds(r0, TILE), pl.ds(C + col, BW)])
        mixed_ref[here, cs] = (st * value).astype(BF)

    over_tiles(S, L, C, finish)

    def drain(j, _):
        remote(fin_s, got_s.at[t], send_sem.at[j], recv_sem.at[t], "tok", j).wait_send()
        return 0

    lax.fori_loop(t + 1, T, drain, 0)
    kept = own_ref.shape[1]
    more = C - kept
    handed = remote(
        mixed_ref.at[:, pl.ds(kept, more)], own_ref.at[:, pl.ds(0, more)], pass_send, pass_recv, "seq", flip(me, 1)
    )

    @pl.when(lax.rem(me, 2) == 0)
    def _():
        handed.start()
        own_ref[...] = mixed_ref[:, 0:kept]
        handed.wait_send()

    @pl.when(lax.rem(me, 2) == 1)
    def _():
        own_ref[:, more:kept] = mixed_ref[:, 0 : kept - more]
        handed.wait_recv()

    @pl.when(t < T - 1)
    def _():
        lap.wait_send()

    drain_cot()
    own_cot.wait()


def recur_backward(
    T, S, L, C, gm_ref, xy_ref, st_ref, conv_ref, x_ref, halo_ref, inc_ref, rows_ref, wd_ref, wi_ref, part_ref,
    gxy_ref, gwd_ref, gwi_ref, small_ref, block_ref,
    a_s, g_s, r_s, sg_s, si_s, gc_s, ext_s, pst_s, fin_s, got_s, car_s, lap_send, lap_recv, send_sem, recv_sem,
    y_s, y_sem, *sum_refs,
):
    t = lax.axis_index("tok")
    SL = S * L // 8
    half = 8 // S
    me = lax.axis_index("seq")
    greet_all(T, t, (flip(me, 1), flip(me, 2)))
    load = pltpu.make_async_copy(xy_ref.at[:, :, pl.ds(C, C)], y_s, y_sem)
    load.start()
    start_sum, middle_sum, total_sum, drain_sum = sum_rows(L, part_ref, *sum_refs)
    start_sum()
    load.wait()

    def prepare(q, r0, col):
        cs = pl.ds(col, BW)
        here = pl.ds(pl.multiple_of(q * L + r0, TILE), TILE)
        low = conv_ref[q, pl.ds(r0, TILE), cs]
        sg = jax.nn.sigmoid(dot(low, wd_ref[cs, :]) + rows_ref[5:6, cs])
        sg_s[here, cs] = sg
        si_s[here, cs] = jax.nn.sigmoid(dot(low, wi_ref[cs, :]) + rows_ref[6:7, cs])
        put_wide(a_s, here, col, jnp.exp(-sg * rows_ref[8:9, cs]))
        value, slope = gelu_parts(y_s[q, pl.ds(r0, TILE), cs])
        gm = gm_ref[here, cs]
        put_wide(g_s, here, col, gm * value)
        gxy_ref[q, pl.ds(r0, TILE), pl.ds(C + col, BW)] = (gm * st_ref[here, cs] * slope).astype(BF)

    over_tiles(S, L, C, prepare)

    NC = C // LANE

    def walk(i, carry):
        at = pl.ds(SL - 1 - i, 8, stride=SL)
        out = []
        for c, (e, r) in enumerate(carry):
            a = a_s[c, at, :]
            adj = g_s[c, at, :] + e
            g_s[c, at, :] = adj
            r_s[c, at, :] = r
            out.append((a * adj, a * r))
        return tuple(out)

    start = tuple((jnp.zeros((8, LANE), F32), jnp.ones((8, LANE), F32)) for _ in range(NC))
    for c, (e, r) in enumerate(lax.fori_loop(0, SL, walk, start, unroll=4)):
        fin_s[c, 0:8, :] = r
        fin_s[c, 8:16, :] = e

    def ship(j, _):
        remote(fin_s, got_s.at[t], send_sem.at[j], recv_sem.at[t], "tok", j).start()
        return 0

    lax.fori_loop(0, t, ship, 0)

    def fold(i, cars):
        j = T - 1 - i
        remote(fin_s, got_s.at[j], send_sem.at[j], recv_sem.at[j], "tok", t).wait_recv()
        out = []
        for c, car in enumerate(cars):
            for k in reversed(range(half)):
                rj = got_s[j, c, pl.ds(k, S, stride=half), :]
                ej = got_s[j, c, pl.ds(8 + k, S, stride=half), :]
                car = rj * car + ej
            out.append(car)
        return tuple(out)

    for c, car in enumerate(lax.fori_loop(0, T - 1 - t, fold, tuple(jnp.zeros((S, LANE), F32) for _ in range(NC)))):
        for k in reversed(range(half)):
            car_s[c, pl.ds(k, S, stride=half), :] = car
            if k > 0:
                car = fin_s[c, pl.ds(k, S, stride=half), :] * car + fin_s[c, pl.ds(8 + k, S, stride=half), :]

    for c in range(CHUNKS):
        middle_sum(c)
    small_ref[...] = jnp.zeros_like(small_ref)
    gwd_ref[...] = jnp.zeros_like(gwd_ref)
    gwi_ref[...] = jnp.zeros_like(gwi_ref)

    def add_row(k, cs, value):
        small_ref[k : k + 1, cs] += jnp.sum(value, axis=0, keepdims=True)

    def chain(q, r0, col):
        cs = pl.ds(col, BW)
        row = q * L + r0
        here = pl.ds(pl.multiple_of(row, TILE), TILE)

        @pl.when(r0 == 0)
        def _():
            pst_s[0:8, cs] = wide(inc_ref, pl.ds(q * half, 1), col) + jnp.zeros((8, BW), F32)

        @pl.when(r0 > 0)
        def _():
            pst_s[0:8, cs] = pst_s[TILE : TILE + 8, cs]

        pst_s[8 : 8 + TILE, cs] = st_ref[here, cs]
        adj = wide(g_s, here, col) + wide(r_s, here, col) * wide(car_s, pl.ds(row // SL, 1), col)
        sg, si, a = sg_s[here, cs], si_s[here, cs], wide(a_s, here, col)
        low = conv_ref[q, pl.ds(r0, TILE), cs]
        vals = low.astype(F32)
        sp = rows_ref[8:9, cs]
        square = a * a
        scale = jnp.sqrt(minus_expm1(-2.0 * sg * sp, square))
        grad_log = adj * pst_s[7 : 7 + TILE, cs] * a - adj * si * vals * square / scale
        grad_gate = (-grad_log * sp * sg * (1.0 - sg)).astype(BF)
        add_row(7, cs, -grad_log * sg)
        grad_inp = (adj * scale * vals * si * (1.0 - si)).astype(BF)
        add_row(5, cs, grad_gate.astype(F32))
        add_row(6, cs, grad_inp.astype(F32))
        gc = (
            adj * scale * si
            + dot(grad_gate, wd_ref[cs, :], ((1,), (1,)))
            + dot(grad_inp, wi_ref[cs, :], ((1,), (1,)))
        )
        gc_s[q, pl.ds(r0, TILE), cs] = gc
        add_row(4, cs, gc)
        gwd_ref[cs, :] += dot(low, grad_gate, ((0,), (0,)))
        gwi_ref[cs, :] += dot(low, grad_inp, ((0,), (0,)))

    over_tiles(S, L, C, chain)
    small_ref[7:8, :] *= 8.0 * rows_ref[9:10, :]

    lap = remote(gc_s.at[:, pl.ds(0, 8), :], gc_s.at[:, pl.ds(L, 8), :], lap_send, lap_recv, "tok", lax.rem(t + T - 1, T))

    @pl.when(t > 0)
    def _():
        lap.start()

    for c in range(CHUNKS):
        rows = pl.ds(c * (L // CHUNKS), L // CHUNKS)
        block_ref[rows, :] = total_sum(c)

    @pl.when(t < T - 1)
    def _():
        lap.wait_recv()

    @pl.when(t == T - 1)
    def _():
        gc_s[:, pl.ds(L, 8), :] = jnp.zeros((S, 8, C), F32)

    def taps(q, r0, col):
        cs = pl.ds(col, BW)

        @pl.when(r0 == 0)
        def _():
            ext_s[0:8, cs] = halo_ref[q, :, cs].astype(F32)[8:16]

        @pl.when(r0 > 0)
        def _():
            ext_s[0:8, cs] = ext_s[TILE : TILE + 8, cs]

        ext_s[8 : 8 + TILE, cs] = x_ref[q, pl.ds(r0, TILE), cs].astype(F32)
        pst_s[0 : TILE + 8, cs] = gc_s[q, pl.ds(r0, TILE + 8), cs]
        gc = pst_s[0:TILE, cs]
        gx = jnp.zeros((TILE, BW), F32)
        for k in range(CONV):
            add_row(k, cs, gc * ext_s[5 + k : 5 + k + TILE, cs])
            gx = gx + pst_s[3 - k : 3 - k + TILE, cs] * rows_ref[k : k + 1, cs]
        gxy_ref[q, pl.ds(r0, TILE), cs] = gx.astype(BF)

    over_tiles(S, L, C, taps)

    def drain(j, _):
        remote(fin_s, got_s.at[t], send_sem.at[j], recv_sem.at[t], "tok", j).wait_send()
        return 0

    lax.fori_loop(0, t, drain, 0)

    @pl.when(t > 0)
    def _():
        lap.wait_send()

    drain_sum()


VM = pl.BlockSpec(memory_space=pltpu.VMEM)


def shape(dims, kind=F32):
    return jax.ShapeDtypeStruct(dims, kind)


def params(collective_id, mib=58):
    return pltpu.CompilerParams(
        collective_id=collective_id, has_side_effects=True, vmem_limit_bytes=mib * 1024 * 1024
    )


def run_forward(T, quarter, branches, rows, wd, wi, cot):
    S, L, C = branches.shape
    hbm = pl.BlockSpec(memory_space=pl.ANY)
    C //= 2
    M = S * L
    dma = pltpu.SemaphoreType.DMA
    split = pltpu.VMEM((C // LANE, M, LANE), F32)
    return pl.pallas_call(
        functools.partial(recur_forward, T, S, L, C),
        out_shape=(
            shape((M, C), BF),
            shape((M, quarter), BF),
            shape((M, C)),
            shape((S, L, C), BF),
            shape((S, L, C), BF),
            shape((S, LAP, C), BF),
            shape((C // LANE, 8, LANE)),
            shape((S,) + cot.shape, BF),
        ),
        in_specs=[VM] * 4 + [hbm],
        out_specs=(VM,) * 7 + (hbm,),
        scratch_shapes=[
            split,
            split,
            pltpu.VMEM((TILE + 8, C), F32),
            pltpu.VMEM((C // LANE, 16, LANE), F32),
            pltpu.VMEM((T, C // LANE, 16, LANE), F32),
            dma,
            dma,
            dma((T,)),
            dma((T,)),
            dma((CHUNKS, 3)),
            dma((CHUNKS, 3)),
            dma,
            dma,
            dma,
        ],
        compiler_params=params(0),
        cost_estimate=pl.CostEstimate(flops=4 * M * C * BW, bytes_accessed=100000000, transcendentals=6 * M * C),
    )(branches, rows, wd, wi, cot)


def run_backward(T, grad_mixed, branches, states, conv, branch_x, halo, inc, rows, wd, wi, part):
    S, L, C = branch_x.shape
    M = S * L
    dma = pltpu.SemaphoreType.DMA
    big = pltpu.VMEM((M, C), F32)
    split = pltpu.VMEM((C // LANE, M, LANE), F32)
    return pl.pallas_call(
        functools.partial(recur_backward, T, S, L, C),
        out_shape=(
            shape((S, L, 2 * C), BF),
            shape((C, BW)),
            shape((C, BW)),
            shape((8, C)),
            shape(part.shape[1:]),
        ),
        in_specs=[VM, pl.BlockSpec(memory_space=pl.ANY)] + [VM] * 9,
        out_specs=(VM,) * 5,
        scratch_shapes=[split] * 3
        + [big] * 2
        + [
            pltpu.VMEM((S, L + 8, C), F32),
            pltpu.VMEM((TILE + 8, C), F32),
            pltpu.VMEM((TILE + 8, C), F32),
            pltpu.VMEM((C // LANE, 16, LANE), F32),
            pltpu.VMEM((T, C // LANE, 16, LANE), F32),
            pltpu.VMEM((C // LANE, 8, LANE), F32),
            dma,
            dma,
            dma((T,)),
            dma((T,)),
        ]
        + [pltpu.VMEM((S, L, C), F32), dma]
        + sum_scratch(*part.shape[1:]),
        compiler_params=params(1),
        cost_estimate=pl.CostEstimate(flops=12 * M * C * BW, bytes_accessed=40000000, transcendentals=0),
    )(grad_mixed, branches, states, conv, branch_x, halo, inc, rows, wd, wi, part)


def root_scale(v):
    return lax.rsqrt(jnp.mean(v * v, axis=-1, keepdims=True) + eps)


def rms_back(v, gain, grad):
    scale = root_scale(v)
    hat = v * scale
    inner = grad * gain
    return scale * (inner - hat * jnp.mean(inner * hat, axis=-1, keepdims=True))


def plane_sum(kind, L, D, *refs):
    shares = kind in ("first", "second")
    part = refs[0]
    if kind == "first":
        tokens, gain, keep, everyone = refs[1:5]
        rest = refs[5:]
    elif kind == "second":
        resid, gain, cot, weight, keep, everyone = refs[1:7]
        rest = refs[7:]
    else:
        tokens, gain, gates, keep, gates_sum = refs[1:6]
        rest = refs[6:]
        pair_s, pair_out, far_s, pair_send, pair_recv, far_send, far_recv = rest[7:]
    if shares:
        own_s, all_send, all_recv, own_sem = rest[7:]
    me = lax.axis_index("seq")
    H = L // CHUNKS
    px, py = flip(me, 1), flip(me, 2)
    barrier = pltpu.get_barrier_semaphore()
    for peer in (px, py):
        pl.semaphore_signal(barrier, inc=1, device_id={"seq": peer}, device_id_type=MESH)
    if kind == "third":
        t, T = lax.axis_index("tok"), gates.shape[0]
        pairs, spot, side = T // 2, t // 2, lax.rem(t, 2)
        pl.semaphore_signal(barrier, inc=1, device_id={"tok": flip(t, 1)}, device_id_type=MESH)

        @pl.loop(1, pairs)
        def _(d):
            pl.semaphore_signal(barrier, inc=1, device_id={"tok": lax.rem(t + 2 * d, T)}, device_id_type=MESH)

        pl.semaphore_wait(barrier, 2 + pairs)

        def near(k):
            return remote(gates.at[2 * k + 1 - side], pair_s.at[k], pair_send.at[k], pair_recv.at[k], "tok", flip(t, 1))

        def far(d):
            k = lax.rem(spot + d, pairs)
            return remote(pair_out.at[k], far_s.at[spot], far_send.at[d], far_recv.at[d], "tok", 2 * k + side)

        @pl.loop(0, pairs)
        def _(k):
            near(k).start()

    else:
        pl.semaphore_wait(barrier, 2)
    start, middle, sums, drain = sum_rows(L, part, *rest[:7])

    def rows(c):
        return pl.ds(c * H, H)

    def share(c, k):
        f, g = (px, py) if c % 2 == 0 else (py, px)
        if k == 2:
            place = everyone.at[f, rows(c), :]
            return remote(place, place, all_send.at[c, k], all_recv.at[c, k], "seq", g)
        place = everyone.at[me, rows(c), :]
        return remote(own_s.at[rows(c), :], place, all_send.at[c, k], all_recv.at[c, k], "seq", (f, g)[k])

    def own(c):
        return pltpu.make_async_copy(own_s.at[rows(c), :], everyone.at[me, rows(c), :], own_sem.at[c])

    def finish(c):
        total = sums(c)
        r = rows(c)
        if kind == "first":
            total = tokens[r, :].astype(F32) + total
            keep[r, :] = total
            own_s[r, :] = (total * root_scale(total) * gain[0:1, :]).astype(BF)
        elif kind == "second":
            back = rms_back(resid[r, :], gain[0:1, :], total)
            total = cot[r, :].astype(F32) * weight[0:1, 0:1] + back
            keep[r, :] = total
            own_s[r, :] = total.astype(BF)
        else:
            back = rms_back(tokens[r, :].astype(F32), gain[0:1, :], total)
            keep[r, :] = back
        if shares:
            share(c, 0).start()
            share(c, 1).start()
            own(c).start()

    def forward(c):
        share(c, 0).wait_recv()
        share(c, 2).start()

    start()
    for c in range(CHUNKS):
        middle(c)
        if kind == "third" and c == 0:

            @pl.loop(0, pairs)
            def _(k):
                near(k).wait()
                pair_out[k] = (gates[2 * k + side].astype(F32) + pair_s[k].astype(F32)).astype(BF)

            @pl.loop(1, pairs)
            def _(d):
                far(d).start()

        if c > 0:
            finish(c - 1)
        if shares and c > 1:
            forward(c - 2)
    finish(CHUNKS - 1)
    if shares:
        forward(CHUNKS - 2)
        forward(CHUNKS - 1)
    drain()
    if kind == "third":
        gates_sum[...] = gates[t].astype(F32) + pair_s[spot].astype(F32)

        @pl.loop(1, pairs)
        def _(d):
            far(d).wait()
            gates_sum[...] += far_s[lax.rem(spot - d + pairs, pairs)].astype(F32)

    if shares:
        for c in range(CHUNKS):
            for k in (1, 2):
                share(c, k).wait_recv()
            for k in (0, 1, 2):
                share(c, k).wait_send()
            own(c).wait()


def run_plane(kind, collective_id, part, *ins):
    S, L, D = part.shape
    dma = pltpu.SemaphoreType.DMA
    shares = kind in ("first", "second")
    outs = [shape((L, D))]
    specs = [VM]
    if shares:
        outs.append(shape((S, L, D), BF))
        specs.append(pl.BlockSpec(memory_space=pl.ANY))
    scratch = sum_scratch(L, D)
    if kind == "third":
        T, *slab = ins[-1].shape
        outs.append(shape(tuple(slab)))
        specs.append(VM)
        scratch += [pltpu.VMEM((T // 2, *slab), BF)] * 3 + [dma((T // 2,))] * 4
    if shares:
        scratch += [pltpu.VMEM((L, D), BF), dma((CHUNKS, 3)), dma((CHUNKS, 3)), dma((CHUNKS,))]
    return pl.pallas_call(
        functools.partial(plane_sum, kind, L, D),
        out_shape=tuple(outs),
        in_specs=[VM] * (1 + len(ins)),
        out_specs=tuple(specs),
        scratch_shapes=scratch,
        compiler_params=params(collective_id, 40),
        cost_estimate=pl.CostEstimate(
            flops=40 * L * D, bytes_accessed=20000000, transcendentals=L
        ),
    )(part, *ins)


def plane_swap(modes, *refs):
    n = len(modes)
    ins, outs = refs[:n], refs[n : 2 * n]
    send, recv, own_sem = refs[2 * n :]
    me = lax.axis_index("seq")
    S = lax.axis_size("seq")
    greet("seq", S, me)

    def copy(i, d):
        to = lax.rem(me + d, S)
        src = ins[i] if modes[i] == "all" else ins[i].at[to]
        return remote(src, outs[i].at[me], send.at[i, d], recv.at[i, d], "seq", to)

    def own(i):
        src = ins[i] if modes[i] == "all" else ins[i].at[me]
        return pltpu.make_async_copy(src, outs[i].at[me], own_sem.at[i])

    for i in range(n):
        for d in range(1, S):
            copy(i, d).start()
        own(i).start()
    for i in range(n):
        for d in range(1, S):
            copy(i, d).wait()
        own(i).wait()


def run_swap(S, modes, collective_id, *ins):
    n = len(modes)
    dma = pltpu.SemaphoreType.DMA
    outs = tuple(shape(((S,) if m == "all" else ()) + x.shape, x.dtype) for m, x in zip(modes, ins))
    size = sum(3 * x.size * x.dtype.itemsize // (1 if m == "all" else S) for m, x in zip(modes, ins))
    hbm = pl.BlockSpec(memory_space=pl.ANY)
    return pl.pallas_call(
        functools.partial(plane_swap, modes),
        out_shape=outs,
        in_specs=[hbm] * n,
        out_specs=(hbm,) * n,
        scratch_shapes=[dma((n, S)), dma((n, S)), dma((n,))],
        compiler_params=params(collective_id, 4),
        cost_estimate=pl.CostEstimate(flops=0, bytes_accessed=size * 40, transcendentals=0),
    )(*ins)


def plane_fill(S, T, slabs, *refs):
    pack, gates, pack_out, gates_out, lent = refs[:5]
    pack_send, pack_recv, gate_send, gate_recv, relay_send, relay_recv, lent_send, lent_recv, own_sem = refs[5:]
    me, t = lax.axis_index("seq"), lax.axis_index("tok")
    px, py, pd = flip(me, 1), flip(me, 2), S - 1 - me
    barrier = pltpu.get_barrier_semaphore()
    for peer in (px, py, pd):
        pl.semaphore_signal(barrier, inc=1, device_id={"seq": peer}, device_id_type=MESH)

    @pl.loop(1, T // 2)
    def _(d):
        pl.semaphore_signal(barrier, inc=1, device_id={"tok": lax.rem(t + 2 * d, T)}, device_id_type=MESH)

    mate = flip(t, 1)
    pl.semaphore_signal(barrier, inc=1, device_id={"tok": mate}, device_id_type=MESH)
    pl.semaphore_wait(barrier, S - 1 + T // 2)

    def gate(d):
        return remote(gates, gates_out.at[t], gate_send.at[d], gate_recv.at[d], "tok", lax.rem(t + 2 * d, T))

    def relay(d):
        place = gates_out.at[lax.rem(t - 2 * d + T, T)]
        return remote(place, place, relay_send.at[d], relay_recv.at[d], "tok", mate)

    def piece(k):
        to = (pd, px, py)[k]
        return remote(pack.at[to], pack_out.at[me], pack_send.at[k], pack_recv.at[k], "seq", to)

    mine = [
        pltpu.make_async_copy(pack.at[me], pack_out.at[me], own_sem.at[0]),
        pltpu.make_async_copy(gates, gates_out.at[t], own_sem.at[1]),
    ]
    loan = remote(gates_out.at[pl.ds(0, slabs)], lent, lent_send, lent_recv, "seq", px)

    @pl.loop(1, T // 2)
    def _(d):
        gate(d).start()

    for copy in mine:
        copy.start()
    for k in range(3):
        piece(k).start()
    mine[1].wait()
    relay(0).start()

    @pl.loop(1, T // 2)
    def _(d):
        gate(d).wait_recv()
        relay(d).start()

    @pl.loop(0, T // 2)
    def _(d):
        relay(d).wait_recv()

    @pl.when(lax.rem(me, 2) == 1)
    def _():
        loan.start()

    for k in range(3):
        piece(k).wait()
    mine[0].wait()

    @pl.loop(1, T // 2)
    def _(d):
        gate(d).wait_send()

    @pl.loop(0, T // 2)
    def _(d):
        relay(d).wait_send()

    @pl.when(lax.rem(me, 2) == 1)
    def _():
        loan.wait_send()

    @pl.when(lax.rem(me, 2) == 0)
    def _():
        loan.wait_recv()


def run_fill(S, T, slabs, collective_id, pack, gates):
    dma = pltpu.SemaphoreType.DMA
    hbm = pl.BlockSpec(memory_space=pl.ANY)
    return pl.pallas_call(
        functools.partial(plane_fill, S, T, slabs),
        out_shape=(
            shape(pack.shape, BF),
            shape((T,) + gates.shape, BF),
            shape((slabs,) + gates.shape, BF),
        ),
        in_specs=[hbm] * 2,
        out_specs=(hbm,) * 3,
        scratch_shapes=[dma((3,))] * 2 + [dma((T // 2,))] * 4 + [dma, dma, dma((2,))],
        compiler_params=params(collective_id, 4),
        cost_estimate=pl.CostEstimate(flops=0, bytes_accessed=80000000, transcendentals=0),
    )(pack, gates)


def plane_rows(S, L, first, out, send, recv, own_sem):
    me = lax.axis_index("seq")
    barrier = pltpu.get_barrier_semaphore()
    for bit in (1, 2):
        pl.semaphore_signal(barrier, inc=1, device_id={"seq": flip(me, bit)}, device_id_type=MESH)
    pl.semaphore_wait(barrier, 2)
    start, forward, drain = gather_rows(L, first, out, send, recv)
    own = pltpu.make_async_copy(first, out.at[me], own_sem)
    start()
    own.start()
    forward()
    drain()
    own.wait()


def run_rows(S, collective_id, first):
    dma = pltpu.SemaphoreType.DMA
    hbm = pl.BlockSpec(memory_space=pl.ANY)
    return pl.pallas_call(
        functools.partial(plane_rows, S, first.shape[0]),
        out_shape=shape((S,) + first.shape, BF),
        in_specs=[hbm],
        out_specs=hbm,
        scratch_shapes=[dma((CHUNKS, 3)), dma((CHUNKS, 3)), dma],
        compiler_params=params(collective_id, 4),
        cost_estimate=pl.CostEstimate(flops=0, bytes_accessed=140000000, transcendentals=0),
    )(first)


def after(value, *others):
    return lax.optimization_barrier((value,) + others)[0]


def body(
    tokens,
    source_ids,
    loss_weights,
    grad_output,
    first_gain,
    input_weight,
    gelu_weight,
    conv_weight,
    conv_bias,
    decay_gate,
    decay_bias,
    input_gate,
    input_bias,
    decay_param,
    output_weight,
    second_gain,
    gate_weight,
    up_weight,
    down_weight,
):
    S, T = lax.axis_size("seq"), lax.axis_size("tok")
    me = lax.axis_index("seq")
    length, D = tokens.shape[1:]
    ds, R = input_weight.shape
    rs = output_weight.shape[0]
    F = gate_weight.shape[1]
    FQ = F // S
    heads = R // BW
    starts = [-(-i * heads // S) for i in range(S + 1)]
    C = max(starts[i + 1] - starts[i] for i in range(S)) * BW
    quarter = R // S
    offs = [starts[i] * BW - i * quarter for i in range(S)] + [0]
    most = max(offs)
    off = sum(jnp.where(me == i, offs[i], 0) for i in range(S))
    own = sum(jnp.where(me == i, (starts[i + 1] - starts[i]) * BW, 0) for i in range(S))

    def cols_for(w):
        parts = [w[:, starts[i] * BW : starts[i + 1] * BW] for i in range(S)]
        return jnp.stack([jnp.pad(p, ((0, 0), (0, C - p.shape[1]))) for p in parts])

    def d_rows(w):
        return lax.all_gather(w, "tok", axis=1, tiled=True).reshape((D, w.shape[-1]))

    def d_scatter(g):
        return lax.psum_scatter(g.reshape(S, T * ds, g.shape[-1]), "tok", scatter_dimension=1, tiled=True)

    def r_align(g):
        g = lax.dynamic_update_slice_in_dim(jnp.zeros((quarter + 2 * most, g.shape[1]), BF), g.astype(BF), off, axis=0)
        back = from_behind(g[quarter : quarter + most], "seq", 1)
        keep = lax.broadcasted_iota(jnp.int32, (quarter, 1), 0) < off
        return jnp.where(keep, jnp.pad(back, ((0, quarter - most), (0, 0))), g[:quarter])

    small = jnp.concatenate(
        [conv_weight, jnp.stack([conv_bias, decay_bias, input_bias, decay_param], axis=1)], axis=1
    )
    gains = jnp.pad(jnp.stack([first_gain, second_gain], axis=1), ((0, 0), (0, SMALL - 2)))
    pack_in = jnp.concatenate([cols_for(input_weight), cols_for(gelu_weight)], axis=2)
    pack_in, gains = run_swap(S, ("slice", "all"), 2, pack_in, gains)
    gains = jnp.pad(gains[:, :, :2].transpose(1, 0, 2).reshape(ds, 2 * S), ((0, rs - ds), (0, 0)))
    small = jnp.concatenate([small, gains], axis=1)
    small = jnp.pad(small, ((0, 0), (0, SMALL - small.shape[1])))
    gates = jnp.concatenate([decay_gate, input_gate, small], axis=1)
    sources = lax.broadcasted_iota(jnp.int32, (1, loss_weights.shape[0]), 1)
    picked = jnp.sum(jnp.where(source_ids[:, None] == sources, loss_weights[None, :], 0.0), axis=1)
    cot_low = (grad_output[0].astype(F32) * picked[:, None]).astype(BF)
    pack_f = jnp.concatenate([w.reshape(ds, S, FQ).swapaxes(0, 1) for w in (gate_weight, up_weight)], axis=2)
    weight_out = gather(output_weight, "tok")
    pack_f, gates, lent = run_fill(S, T, -(-most // rs), 3, after(pack_f, pack_in), gates)
    everyone = run_rows(S, 8, after(tokens[0], pack_f, weight_out))

    def r_rows(whole, lent):
        lent = lent[:most]
        whole = jnp.concatenate([whole, lent, jnp.zeros_like(lent)], axis=0)
        whole = lax.dynamic_slice_in_dim(whole, off, C, axis=0)
        return jnp.where(lax.broadcasted_iota(jnp.int32, whole.shape, 0) < own, whole, 0)

    pack_in = d_rows(pack_in)
    weight_xy = pack_in[:, : 2 * C]
    gains = gates[:, :ds, 2 * BW + 8 : 2 * BW + 8 + 2 * S].reshape(T, ds, S, 2).transpose(3, 2, 0, 1)
    gain_one, gain_two = gains.reshape(2, D).astype(F32)
    gates = r_rows(gates.reshape(quarter, -1), lent.reshape(-1, lent.shape[-1]))
    weight_decay, weight_input = gates[:, :BW], gates[:, BW : 2 * BW]
    rows = gates[:, 2 * BW : 2 * BW + 8].T.astype(F32)
    param = rows[7:8]
    rows = jnp.concatenate(
        [rows, 8.0 * jax.nn.softplus(param), jax.nn.sigmoid(param), jnp.zeros((6, C), F32)], axis=0
    )
    weight_out = r_rows(weight_out, from_behind(weight_out[:most], "seq", -1))

    everyone = everyone.astype(F32)
    normed = lax.optimization_barrier(rms_scale(everyone, gain_one).astype(BF))
    ready = (pack_f, normed, rows, weight_decay, weight_input, weight_out)
    pack_f, normed, rows, weight_decay, weight_input, weight_out = lax.optimization_barrier(ready)
    pack_f, weight_xy = lax.optimization_barrier((pack_f, weight_xy))
    pack_f = d_rows(pack_f)
    weight_gate, weight_up = pack_f[:, :FQ], pack_f[:, FQ:]
    branches = forward_product(normed, weight_xy)
    weight_down = gather(after(down_weight, branches), "tok")
    mixed, mixed_own, states, conv_low, branch_x, halo, incoming, cot_low = run_forward(
        T, quarter, branches, rows, weight_decay, weight_input, cot_low
    )
    mixed, mixed_own = mixed.reshape(S, length, C), mixed_own.reshape(S, length, quarter)
    part = forward_product(mixed, weight_out).astype(BF)
    resid, second_normed = run_plane("first", 4, part, tokens[0], gain_two[None])

    gate_val = forward_product(second_normed, weight_gate)
    up_val = forward_product(second_normed, weight_up)
    hidden = gelu_product(gate_val, up_val).astype(BF)
    grad_down = token_product(hidden, cot_low).astype(BF)
    weight_down = after(weight_down, grad_down)
    grad_down = scatter(grad_down, "tok")

    grad_hidden = back_product(cot_low, weight_down)
    _, hidden_pull = jax.vjp(gelu_product, gate_val, up_val)
    grad_gate_val, grad_up_val = hidden_pull(grad_hidden)
    grad_gate_up = jnp.concatenate([grad_gate_val.astype(BF), grad_up_val.astype(BF)], axis=2)
    grad_pack = token_product(second_normed, grad_gate_up).astype(BF)
    grad_second = back_product(after(grad_gate_up, grad_pack), pack_f)
    grad_second = grad_second.astype(BF)
    grad_pack = d_scatter(grad_pack)
    picked = jnp.broadcast_to(picked[None], (8, 128))
    grad_resid, resid_low = run_plane(
        "second", 6, grad_second, resid, gain_two[None], grad_output[0], picked
    )

    grad_out_w = token_product(mixed_own, after(resid_low, grad_down)).astype(BF)
    grad_mixed = back_product(after(resid_low, grad_out_w), weight_out)
    grad_out_w = scatter(grad_out_w, "tok")
    part = forward_product(hidden, weight_down).astype(BF)
    grad_xy, grad_decay_w, grad_input_w, smalls, block_out = run_backward(
        T, grad_mixed.reshape(S * length, C), branches, states, conv_low, branch_x, halo, incoming, rows,
        weight_decay, weight_input, part,
    )
    block_out = (resid + block_out).astype(BF)
    grad_i = token_product(normed, after(grad_xy, grad_pack)).astype(BF)
    smalls = jnp.pad(smalls.T, ((0, 0), (0, SMALL - 8)))
    grad_r = r_align(after(jnp.concatenate([grad_decay_w, grad_input_w, smalls], axis=1), grad_i))
    grad_normed = back_product(after(grad_xy, grad_i), weight_xy)
    grad_normed = after(grad_normed, grad_out_w)

    grad_i = d_scatter(grad_i)
    grad_tokens, grad_r = run_plane(
        "third", 7, grad_normed.astype(BF), tokens[0], gain_one[None], grad_r.reshape(T, rs, -1)
    )
    grad_tokens = grad_resid + grad_tokens
    grad_pack = to_seq(grad_pack).swapaxes(0, 1).astype(F32)
    grad_gate_w = grad_pack[:, :, :FQ].reshape(ds, F)
    grad_up_w = grad_pack[:, :, FQ:].reshape(ds, F)
    grad_down, grad_out_w = grad_down.astype(F32), grad_out_w.astype(F32)

    def gain_grad(gain, *pairs):
        return sum(jnp.sum(w.astype(F32) * g, axis=1) for w, g in pairs) / gain.astype(F32)

    grad_gain_two = gain_grad(second_gain, (gate_weight, grad_gate_w), (up_weight, grad_up_w))
    early = (block_out, grad_tokens, grad_r, grad_down, grad_out_w, grad_gate_w, grad_up_w, grad_gain_two)
    grad_i, *early = lax.optimization_barrier((grad_i,) + early)
    block_out, grad_tokens, grad_r, grad_down, grad_out_w, grad_gate_w, grad_up_w, grad_gain_two = early
    grad_i = to_seq(grad_i).astype(F32)

    def columns(at):
        return jnp.concatenate(
            [grad_i[i, :, at : at + (starts[i + 1] - starts[i]) * BW] for i in range(S)], axis=1
        )

    grad_in_w, grad_gelu_w = columns(0), columns(C)

    smalls = grad_r[:, 2 * BW :]
    return (
        block_out[None],
        grad_tokens[None],
        gain_grad(first_gain, (input_weight, grad_in_w), (gelu_weight, grad_gelu_w)),
        grad_in_w,
        grad_gelu_w,
        smalls[:, :CONV],
        smalls[:, 4],
        grad_r[:, :BW],
        smalls[:, 5],
        grad_r[:, BW : 2 * BW],
        smalls[:, 6],
        smalls[:, 7],
        grad_out_w,
        grad_gain_two,
        grad_gate_w,
        grad_up_w,
        grad_down,
    )


def solution(mesh):
    one, two = P(("seq", "tok")), P(("seq", "tok"), None)
    data = P("seq", "tok", None)
    return jax.shard_map(
        body,
        mesh=mesh,
        in_specs=(data, P("seq"), P(), data, one, two, two, two, one, two, one, two, one, one, two, one, two, two, two),
        out_specs=(data, data, one, two, two, two, one, two, one, two, one, one, two, one, two, two, two),
        check_vma=False,
    )
```

```python
import functools

import jax
import jax.numpy as jnp
from jax import lax
from jax.experimental import pallas as pl
from jax.experimental.pallas import tpu as pltpu
from jax.sharding import PartitionSpec as P

BW = 256
CONV = 4
SMALL = 128
BF = jnp.bfloat16
F32 = jnp.float32
eps = 1e-06


def from_behind(block, axis, distance):
    devices = range(lax.axis_size(axis))
    route = [(i - distance, i) for i in devices if i - distance in devices]
    return lax.ppermute(block, axis, route)


def gelu(value):
    return jax.nn.gelu(value, approximate=True)


def rms_scale(value, gain):
    return value * lax.rsqrt(jnp.mean(value * value, axis=-1, keepdims=True) + eps) * gain


def gelu_product(gate_val, up_val):
    return gelu(gate_val) * up_val


def forward_product(left, weight):
    return jnp.dot(left, weight, preferred_element_type=F32)


def back_product(grad, weight):
    return lax.dot_general(grad, weight, (((2,), (1,)), ((), ())), preferred_element_type=F32)


def token_product(left, grad):
    return lax.dot_general(left, grad, (((0, 1), (0, 1)), ((), ())), preferred_element_type=F32)


def to_seq(parts):
    return lax.all_to_all(parts, "seq", split_axis=0, concat_axis=0, tiled=True)


def gather(value, axis):
    return lax.all_gather(value, axis, axis=0, tiled=True)


def scatter(value, axis):
    return lax.psum_scatter(value.astype(BF), axis, scatter_dimension=0, tiled=True)


MESH = pl.DeviceIdType.MESH
TILE = 128
LAP = 16


def greet(axis, count, mine):
    barrier = pltpu.get_barrier_semaphore()
    for d in range(1, count):
        pl.semaphore_signal(
            barrier, inc=1, device_id={axis: lax.rem(mine + d, count)}, device_id_type=MESH
        )
    pl.semaphore_wait(barrier, count - 1)


def remote(src, dst, send, recv, axis, to):
    return pltpu.make_async_remote_copy(
        src_ref=src, dst_ref=dst, send_sem=send, recv_sem=recv, device_id={axis: to}, device_id_type=MESH
    )


CHUNKS = 4


def flip(me, bit):
    return me + bit - 2 * bit * lax.rem(me // bit, 2)


def greet_all(T, mine, peers):
    barrier = pltpu.get_barrier_semaphore()
    for peer in peers:
        pl.semaphore_signal(barrier, inc=1, device_id={"seq": peer}, device_id_type=MESH)
    for d in range(1, T):
        pl.semaphore_signal(barrier, inc=1, device_id={"tok": lax.rem(mine + d, T)}, device_id_type=MESH)
    pl.semaphore_wait(barrier, T - 1 + len(peers))


def gather_rows(L, src, out, send, recv):
    me = lax.axis_index("seq")
    px, py = flip(me, 1), flip(me, 2)
    H = L // CHUNKS

    def copy(c, k):
        f, g = (px, py) if c % 2 == 0 else (py, px)
        rows = pl.ds(c * H, H)
        sems = send.at[c, k], recv.at[c, k], "seq"
        if k == 2:
            place = out.at[f, rows, :]
            return remote(place, place, *sems, g)
        return remote(src.at[rows, :], out.at[me, rows, :], *sems, (f, g)[k])

    def start():
        for k in (0, 1):
            for c in range(CHUNKS):
                copy(c, k).start()

    def forward():
        for c in range(CHUNKS):
            copy(c, 0).wait_recv()
            copy(c, 2).start()

    def drain():
        for c in range(CHUNKS):
            copy(c, 0).wait_send()
            copy(c, 1).wait()
            copy(c, 2).wait()

    return start, forward, drain


def sum_rows(L, part, one_s, two_s, two_out, one_send, one_recv, two_send, two_recv):
    me = lax.axis_index("seq")
    px, py, pd = flip(me, 1), flip(me, 2), 3 - me
    H = L // CHUNKS

    def peers(c):
        return (px, py) if c % 2 == 0 else (py, px)

    def rows(c):
        return pl.ds(c * H, H)

    def one(c, k):
        f, _ = peers(c)
        src = (f, pd)[k]
        return remote(part.at[src, rows(c), :], one_s.at[c, k], one_send.at[c, k], one_recv.at[c, k], "seq", f)

    def two(c):
        return remote(two_out.at[c], two_s.at[c], two_send.at[c], two_recv.at[c], "seq", peers(c)[1])

    def start():
        for c in range(CHUNKS):
            for k in (1, 0):
                one(c, k).start()

    def middle(c):
        one(c, 1).wait_recv()
        two_out[c] = (part[peers(c)[1], rows(c), :].astype(F32) + one_s[c, 1].astype(F32)).astype(BF)
        two(c).start()

    def total(c):
        one(c, 0).wait_recv()
        two(c).wait_recv()
        return part[me, rows(c), :].astype(F32) + one_s[c, 0].astype(F32) + two_s[c].astype(F32)

    def drain():
        for c in range(CHUNKS):
            for k in (0, 1):
                one(c, k).wait_send()
            two(c).wait_send()

    return start, middle, total, drain


def sum_scratch(L, D):
    H = L // CHUNKS
    dma = pltpu.SemaphoreType.DMA
    return [
        pltpu.VMEM((CHUNKS, 2, H, D), BF),
        pltpu.VMEM((CHUNKS, H, D), BF),
        pltpu.VMEM((CHUNKS, H, D), BF),
        dma((CHUNKS, 2)),
        dma((CHUNKS, 2)),
        dma((CHUNKS,)),
        dma((CHUNKS,)),
    ]


def minus_expm1(x, whole):
    series = 1.0 + x * (1.0 / 7)
    for n in (6, 5, 4, 3, 2):
        series = 1.0 + x * (1.0 / n) * series
    return jnp.where(x > -0.5, -x * series, 1.0 - whole)


def gelu_parts(v):
    inner = 0.7978845608028654 * (v + 0.044715 * (v * v * v))
    th = jnp.tanh(inner)
    value = 0.5 * v * (1.0 + th)
    slope = 0.5 * (1.0 + th) + 0.5 * v * (1.0 - th * th) * 0.7978845608028654 * (
        1.0 + 3 * 0.044715 * (v * v)
    )
    return value, slope


def dot(a, b, dims=((1,), (0,))):
    return lax.dot_general(a, b, (dims, ((), ())), preferred_element_type=F32)


LANE = 128


def wide(ref, rows, col):
    return jnp.concatenate([ref[c, rows, :] for c in range(col // LANE, (col + BW) // LANE)], axis=1)


def put_wide(ref, rows, col, value):
    for c in range(BW // LANE):
        ref[col // LANE + c, rows, :] = value[:, c * LANE : (c + 1) * LANE]


def over_tiles(S, L, C, step, first=0):
    per = L // TILE

    @pl.loop(0, S * per)
    def _(i):
        for col in range(first, C, BW):
            step(i // per, pl.multiple_of(lax.rem(i, per) * TILE, TILE), col)


def recur_forward(
    T, S, L, C, xy_ref, rows_ref, wd_ref, wi_ref, cot_ref,
    mixed_ref, own_ref, states_ref, conv_ref, x_ref, halo_ref, inc_ref, cots_ref,
    a_s, b_s, ext_s, fin_s, got_s, halo_send, halo_recv, send_sem, recv_sem, cot_send, cot_recv, own_sem,
    pass_send, pass_recv,
):
    t = lax.axis_index("tok")
    SL = S * L // 8
    half = 8 // S
    me = lax.axis_index("seq")
    greet_all(T, t, (flip(me, 1), flip(me, 2)))
    start_cot, forward_cot, drain_cot = gather_rows(L, cot_ref, cots_ref, cot_send, cot_recv)
    own_cot = pltpu.make_async_copy(cot_ref, cots_ref.at[me], own_sem)
    for q in range(S):
        x_ref[q, L - LAP : L, :] = xy_ref[q, L - LAP : L, 0:C].astype(BF)
    lap = remote(x_ref.at[:, pl.ds(L - LAP, LAP), :], halo_ref, halo_send, halo_recv, "tok", lax.rem(t + 1, T))

    @pl.when(t < T - 1)
    def _():
        lap.start()

    start_cot()
    own_cot.start()

    @pl.when(t > 0)
    def _():
        lap.wait_recv()

    @pl.when(t == 0)
    def _():
        halo_ref[...] = jnp.zeros_like(halo_ref)

    def make(q, r0, col):
        cs = pl.ds(col, BW)

        @pl.when(r0 == 0)
        def _():
            ext_s[0:8, cs] = halo_ref[q, :, cs].astype(F32)[8:16]

        @pl.when(r0 > 0)
        def _():
            ext_s[0:8, cs] = ext_s[TILE : TILE + 8, cs]

        low_x = xy_ref[q, pl.ds(r0, TILE), cs].astype(BF)

        @pl.when(r0 < L - TILE)
        def _():
            x_ref[q, pl.ds(r0, TILE), cs] = low_x

        @pl.when(r0 == L - TILE)
        def _():
            x_ref[q, L - TILE : L - LAP, cs] = low_x[: TILE - LAP]

        ext_s[8 : 8 + TILE, cs] = low_x.astype(F32)
        conv = rows_ref[4:5, cs] + jnp.zeros((TILE, BW), F32)
        for k in range(CONV):
            conv = conv + ext_s[5 + k : 5 + k + TILE, cs] * rows_ref[k : k + 1, cs]
        low = conv.astype(BF)
        conv_ref[q, pl.ds(r0, TILE), cs] = low
        vals = low.astype(F32)
        gate = dot(low, wd_ref[cs, :]) + rows_ref[5:6, cs]
        inp = dot(low, wi_ref[cs, :]) + rows_ref[6:7, cs]
        log = -jax.nn.sigmoid(gate) * rows_ref[8:9, cs]
        a = jnp.exp(log)
        b = jnp.sqrt(minus_expm1(2.0 * log, a * a)) * jax.nn.sigmoid(inp) * vals
        here = pl.ds(pl.multiple_of(q * L + r0, TILE), TILE)
        put_wide(a_s, here, col, a)
        put_wide(b_s, here, col, b)

    over_tiles(S, L, C, make)
    forward_cot()

    NC = C // LANE

    def walk(i, carry):
        at = pl.ds(i, 8, stride=SL)
        out = []
        for c, (h, p) in enumerate(carry):
            a = a_s[c, at, :]
            h = a * h + b_s[c, at, :]
            p = a * p
            a_s[c, at, :] = p
            b_s[c, at, :] = h
            out.append((h, p))
        return tuple(out)

    start = tuple((jnp.zeros((8, LANE), F32), jnp.ones((8, LANE), F32)) for _ in range(NC))
    for c, (h, p) in enumerate(lax.fori_loop(0, SL, walk, start, unroll=4)):
        fin_s[c, 0:8, :] = p
        fin_s[c, 8:16, :] = h

    def ship(j, _):
        remote(fin_s, got_s.at[t], send_sem.at[j], recv_sem.at[t], "tok", j).start()
        return 0

    lax.fori_loop(t + 1, T, ship, 0)

    def fold(j, incs):
        remote(fin_s, got_s.at[j], send_sem.at[j], recv_sem.at[j], "tok", t).wait_recv()
        out = []
        for c, inc in enumerate(incs):
            for k in range(half):
                pj = got_s[j, c, pl.ds(k, S, stride=half), :]
                hj = got_s[j, c, pl.ds(8 + k, S, stride=half), :]
                inc = pj * inc + hj
            out.append(inc)
        return tuple(out)

    for c, inc in enumerate(lax.fori_loop(0, t, fold, tuple(jnp.zeros((S, LANE), F32) for _ in range(NC)))):
        for k in range(half):
            inc_ref[c, pl.ds(k, S, stride=half), :] = inc
            if k < half - 1:
                inc = fin_s[c, pl.ds(k, S, stride=half), :] * inc + fin_s[c, pl.ds(8 + k, S, stride=half), :]

    def finish(q, r0, col):
        cs = pl.ds(col, BW)
        row = q * L + r0
        here = pl.ds(pl.multiple_of(row, TILE), TILE)
        st = wide(b_s, here, col) + wide(a_s, here, col) * wide(inc_ref, pl.ds(row // SL, 1), col)
        states_ref[here, cs] = st
        value, _ = gelu_parts(xy_ref[q, pl.ds(r0, TILE), pl.ds(C + col, BW)])
        mixed_ref[here, cs] = (st * value).astype(BF)

    kept = own_ref.shape[1]
    more = C - kept
    handed = remote(
        mixed_ref.at[:, pl.ds(kept, more)], own_ref.at[:, pl.ds(0, more)], pass_send, pass_recv, "seq", flip(me, 1)
    )
    over_tiles(S, L, C, finish, C - BW)

    @pl.when(lax.rem(me, 2) == 0)
    def _():
        handed.start()

    over_tiles(S, L, C - BW, finish)

    def drain(j, _):
        remote(fin_s, got_s.at[t], send_sem.at[j], recv_sem.at[t], "tok", j).wait_send()
        return 0

    lax.fori_loop(t + 1, T, drain, 0)

    @pl.when(lax.rem(me, 2) == 0)
    def _():
        own_ref[...] = mixed_ref[:, 0:kept]
        handed.wait_send()

    @pl.when(lax.rem(me, 2) == 1)
    def _():
        own_ref[:, more:kept] = mixed_ref[:, 0 : kept - more]
        handed.wait_recv()

    @pl.when(t < T - 1)
    def _():
        lap.wait_send()

    drain_cot()
    own_cot.wait()


def recur_backward(
    T, S, L, C, gm_ref, xy_ref, st_ref, conv_ref, x_ref, halo_ref, inc_ref, rows_ref, wd_ref, wi_ref, part_ref,
    gxy_ref, gwd_ref, gwi_ref, small_ref, block_ref,
    a_s, g_s, r_s, sg_s, si_s, gc_s, ext_s, pst_s, fin_s, got_s, car_s, lap_send, lap_recv, send_sem, recv_sem,
    y_s, y_sem, *sum_refs,
):
    t = lax.axis_index("tok")
    SL = S * L // 8
    half = 8 // S
    me = lax.axis_index("seq")
    greet_all(T, t, (flip(me, 1), flip(me, 2)))
    load = pltpu.make_async_copy(xy_ref.at[:, :, pl.ds(C, C)], y_s, y_sem)
    load.start()
    start_sum, middle_sum, total_sum, drain_sum = sum_rows(L, part_ref, *sum_refs)
    start_sum()
    load.wait()

    def prepare(q, r0, col):
        cs = pl.ds(col, BW)
        here = pl.ds(pl.multiple_of(q * L + r0, TILE), TILE)
        low = conv_ref[q, pl.ds(r0, TILE), cs]
        sg = jax.nn.sigmoid(dot(low, wd_ref[cs, :]) + rows_ref[5:6, cs])
        sg_s[here, cs] = sg
        si_s[here, cs] = jax.nn.sigmoid(dot(low, wi_ref[cs, :]) + rows_ref[6:7, cs])
        put_wide(a_s, here, col, jnp.exp(-sg * rows_ref[8:9, cs]))
        value, slope = gelu_parts(y_s[q, pl.ds(r0, TILE), cs])
        gm = gm_ref[here, cs]
        put_wide(g_s, here, col, gm * value)
        gxy_ref[q, pl.ds(r0, TILE), pl.ds(C + col, BW)] = (gm * st_ref[here, cs] * slope).astype(BF)

    over_tiles(S, L, C, prepare)

    NC = C // LANE

    def walk(i, carry):
        at = pl.ds(SL - 1 - i, 8, stride=SL)
        out = []
        for c, (e, r) in enumerate(carry):
            a = a_s[c, at, :]
            adj = g_s[c, at, :] + e
            g_s[c, at, :] = adj
            r_s[c, at, :] = r
            out.append((a * adj, a * r))
        return tuple(out)

    start = tuple((jnp.zeros((8, LANE), F32), jnp.ones((8, LANE), F32)) for _ in range(NC))
    for c, (e, r) in enumerate(lax.fori_loop(0, SL, walk, start, unroll=4)):
        fin_s[c, 0:8, :] = r
        fin_s[c, 8:16, :] = e

    def ship(j, _):
        remote(fin_s, got_s.at[t], send_sem.at[j], recv_sem.at[t], "tok", j).start()
        return 0

    lax.fori_loop(0, t, ship, 0)

    def fold(i, cars):
        j = T - 1 - i
        remote(fin_s, got_s.at[j], send_sem.at[j], recv_sem.at[j], "tok", t).wait_recv()
        out = []
        for c, car in enumerate(cars):
            for k in reversed(range(half)):
                rj = got_s[j, c, pl.ds(k, S, stride=half), :]
                ej = got_s[j, c, pl.ds(8 + k, S, stride=half), :]
                car = rj * car + ej
            out.append(car)
        return tuple(out)

    for c, car in enumerate(lax.fori_loop(0, T - 1 - t, fold, tuple(jnp.zeros((S, LANE), F32) for _ in range(NC)))):
        for k in reversed(range(half)):
            car_s[c, pl.ds(k, S, stride=half), :] = car
            if k > 0:
                car = fin_s[c, pl.ds(k, S, stride=half), :] * car + fin_s[c, pl.ds(8 + k, S, stride=half), :]

    for c in range(CHUNKS):
        middle_sum(c)
    small_ref[...] = jnp.zeros_like(small_ref)
    gwd_ref[...] = jnp.zeros_like(gwd_ref)
    gwi_ref[...] = jnp.zeros_like(gwi_ref)

    def add_row(k, cs, value):
        small_ref[k : k + 1, cs] += jnp.sum(value, axis=0, keepdims=True)

    def chain(q, r0, col):
        cs = pl.ds(col, BW)
        row = q * L + r0
        here = pl.ds(pl.multiple_of(row, TILE), TILE)

        @pl.when(r0 == 0)
        def _():
            pst_s[0:8, cs] = wide(inc_ref, pl.ds(q * half, 1), col) + jnp.zeros((8, BW), F32)

        @pl.when(r0 > 0)
        def _():
            pst_s[0:8, cs] = pst_s[TILE : TILE + 8, cs]

        pst_s[8 : 8 + TILE, cs] = st_ref[here, cs]
        adj = wide(g_s, here, col) + wide(r_s, here, col) * wide(car_s, pl.ds(row // SL, 1), col)
        sg, si, a = sg_s[here, cs], si_s[here, cs], wide(a_s, here, col)
        low = conv_ref[q, pl.ds(r0, TILE), cs]
        vals = low.astype(F32)
        sp = rows_ref[8:9, cs]
        square = a * a
        scale = jnp.sqrt(minus_expm1(-2.0 * sg * sp, square))
        grad_log = adj * pst_s[7 : 7 + TILE, cs] * a - adj * si * vals * square / scale
        grad_gate = (-grad_log * sp * sg * (1.0 - sg)).astype(BF)
        add_row(7, cs, -grad_log * sg)
        grad_inp = (adj * scale * vals * si * (1.0 - si)).astype(BF)
        add_row(5, cs, grad_gate.astype(F32))
        add_row(6, cs, grad_inp.astype(F32))
        gc = (
            adj * scale * si
            + dot(grad_gate, wd_ref[cs, :], ((1,), (1,)))
            + dot(grad_inp, wi_ref[cs, :], ((1,), (1,)))
        )
        gc_s[q, pl.ds(r0, TILE), cs] = gc
        add_row(4, cs, gc)
        gwd_ref[cs, :] += dot(low, grad_gate, ((0,), (0,)))
        gwi_ref[cs, :] += dot(low, grad_inp, ((0,), (0,)))

    over_tiles(S, L, C, chain)
    small_ref[7:8, :] *= 8.0 * rows_ref[9:10, :]

    lap = remote(gc_s.at[:, pl.ds(0, 8), :], gc_s.at[:, pl.ds(L, 8), :], lap_send, lap_recv, "tok", lax.rem(t + T - 1, T))

    @pl.when(t > 0)
    def _():
        lap.start()

    for c in range(CHUNKS):
        rows = pl.ds(c * (L // CHUNKS), L // CHUNKS)
        block_ref[rows, :] = total_sum(c)

    @pl.when(t < T - 1)
    def _():
        lap.wait_recv()

    @pl.when(t == T - 1)
    def _():
        gc_s[:, pl.ds(L, 8), :] = jnp.zeros((S, 8, C), F32)

    def taps(q, r0, col):
        cs = pl.ds(col, BW)

        @pl.when(r0 == 0)
        def _():
            ext_s[0:8, cs] = halo_ref[q, :, cs].astype(F32)[8:16]

        @pl.when(r0 > 0)
        def _():
            ext_s[0:8, cs] = ext_s[TILE : TILE + 8, cs]

        ext_s[8 : 8 + TILE, cs] = x_ref[q, pl.ds(r0, TILE), cs].astype(F32)
        pst_s[0 : TILE + 8, cs] = gc_s[q, pl.ds(r0, TILE + 8), cs]
        gc = pst_s[0:TILE, cs]
        gx = jnp.zeros((TILE, BW), F32)
        for k in range(CONV):
            add_row(k, cs, gc * ext_s[5 + k : 5 + k + TILE, cs])
            gx = gx + pst_s[3 - k : 3 - k + TILE, cs] * rows_ref[k : k + 1, cs]
        gxy_ref[q, pl.ds(r0, TILE), cs] = gx.astype(BF)

    over_tiles(S, L, C, taps)

    def drain(j, _):
        remote(fin_s, got_s.at[t], send_sem.at[j], recv_sem.at[t], "tok", j).wait_send()
        return 0

    lax.fori_loop(0, t, drain, 0)

    @pl.when(t > 0)
    def _():
        lap.wait_send()

    drain_sum()


VM = pl.BlockSpec(memory_space=pltpu.VMEM)


def shape(dims, kind=F32):
    return jax.ShapeDtypeStruct(dims, kind)


def params(collective_id, mib=58):
    return pltpu.CompilerParams(
        collective_id=collective_id, has_side_effects=True, vmem_limit_bytes=mib * 1024 * 1024
    )


def run_forward(T, quarter, branches, rows, wd, wi, cot):
    S, L, C = branches.shape
    hbm = pl.BlockSpec(memory_space=pl.ANY)
    C //= 2
    M = S * L
    dma = pltpu.SemaphoreType.DMA
    split = pltpu.VMEM((C // LANE, M, LANE), F32)
    return pl.pallas_call(
        functools.partial(recur_forward, T, S, L, C),
        out_shape=(
            shape((M, C), BF),
            shape((M, quarter), BF),
            shape((M, C)),
            shape((S, L, C), BF),
            shape((S, L, C), BF),
            shape((S, LAP, C), BF),
            shape((C // LANE, 8, LANE)),
            shape((S,) + cot.shape, BF),
        ),
        in_specs=[VM] * 4 + [hbm],
        out_specs=(VM,) * 7 + (hbm,),
        scratch_shapes=[
            split,
            split,
            pltpu.VMEM((TILE + 8, C), F32),
            pltpu.VMEM((C // LANE, 16, LANE), F32),
            pltpu.VMEM((T, C // LANE, 16, LANE), F32),
            dma,
            dma,
            dma((T,)),
            dma((T,)),
            dma((CHUNKS, 3)),
            dma((CHUNKS, 3)),
            dma,
            dma,
            dma,
        ],
        compiler_params=params(0),
        cost_estimate=pl.CostEstimate(flops=4 * M * C * BW, bytes_accessed=100000000, transcendentals=6 * M * C),
    )(branches, rows, wd, wi, cot)


def run_backward(T, grad_mixed, branches, states, conv, branch_x, halo, inc, rows, wd, wi, part):
    S, L, C = branch_x.shape
    M = S * L
    dma = pltpu.SemaphoreType.DMA
    big = pltpu.VMEM((M, C), F32)
    split = pltpu.VMEM((C // LANE, M, LANE), F32)
    return pl.pallas_call(
        functools.partial(recur_backward, T, S, L, C),
        out_shape=(
            shape((S, L, 2 * C), BF),
            shape((C, BW)),
            shape((C, BW)),
            shape((8, C)),
            shape(part.shape[1:]),
        ),
        in_specs=[VM, pl.BlockSpec(memory_space=pl.ANY)] + [VM] * 9,
        out_specs=(VM,) * 5,
        scratch_shapes=[split] * 3
        + [big] * 2
        + [
            pltpu.VMEM((S, L + 8, C), F32),
            pltpu.VMEM((TILE + 8, C), F32),
            pltpu.VMEM((TILE + 8, C), F32),
            pltpu.VMEM((C // LANE, 16, LANE), F32),
            pltpu.VMEM((T, C // LANE, 16, LANE), F32),
            pltpu.VMEM((C // LANE, 8, LANE), F32),
            dma,
            dma,
            dma((T,)),
            dma((T,)),
        ]
        + [pltpu.VMEM((S, L, C), F32), dma]
        + sum_scratch(*part.shape[1:]),
        compiler_params=params(1),
        cost_estimate=pl.CostEstimate(flops=12 * M * C * BW, bytes_accessed=40000000, transcendentals=0),
    )(grad_mixed, branches, states, conv, branch_x, halo, inc, rows, wd, wi, part)


def root_scale(v):
    return lax.rsqrt(jnp.mean(v * v, axis=-1, keepdims=True) + eps)


def rms_back(v, gain, grad):
    scale = root_scale(v)
    hat = v * scale
    inner = grad * gain
    return scale * (inner - hat * jnp.mean(inner * hat, axis=-1, keepdims=True))


def plane_sum(kind, L, D, *refs):
    shares = kind in ("first", "second")
    part = refs[0]
    if kind == "first":
        tokens, gain, keep, everyone = refs[1:5]
        rest = refs[5:]
    elif kind == "second":
        resid, gain, cot, weight, keep, everyone = refs[1:7]
        rest = refs[7:]
    else:
        tokens, gain, gates, keep, gates_sum = refs[1:6]
        rest = refs[6:]
        pair_s, pair_out, far_s, pair_send, pair_recv, far_send, far_recv = rest[7:]
    if shares:
        own_s, all_send, all_recv, own_sem = rest[7:]
    me = lax.axis_index("seq")
    H = L // CHUNKS
    px, py = flip(me, 1), flip(me, 2)
    barrier = pltpu.get_barrier_semaphore()
    for peer in (px, py):
        pl.semaphore_signal(barrier, inc=1, device_id={"seq": peer}, device_id_type=MESH)
    if kind == "third":
        t, T = lax.axis_index("tok"), gates.shape[0]
        pairs, spot, side = T // 2, t // 2, lax.rem(t, 2)
        pl.semaphore_signal(barrier, inc=1, device_id={"tok": flip(t, 1)}, device_id_type=MESH)

        @pl.loop(1, pairs)
        def _(d):
            pl.semaphore_signal(barrier, inc=1, device_id={"tok": lax.rem(t + 2 * d, T)}, device_id_type=MESH)

        pl.semaphore_wait(barrier, 2 + pairs)

        def near(k):
            return remote(gates.at[2 * k + 1 - side], pair_s.at[k], pair_send.at[k], pair_recv.at[k], "tok", flip(t, 1))

        def far(d):
            k = lax.rem(spot + d, pairs)
            return remote(pair_out.at[k], far_s.at[spot], far_send.at[d], far_recv.at[d], "tok", 2 * k + side)

        @pl.loop(0, pairs)
        def _(k):
            near(k).start()

    else:
        pl.semaphore_wait(barrier, 2)
    start, middle, sums, drain = sum_rows(L, part, *rest[:7])

    def rows(c):
        return pl.ds(c * H, H)

    def share(c, k):
        f, g = (px, py) if c % 2 == 0 else (py, px)
        if k == 2:
            place = everyone.at[f, rows(c), :]
            return remote(place, place, all_send.at[c, k], all_recv.at[c, k], "seq", g)
        place = everyone.at[me, rows(c), :]
        return remote(own_s.at[rows(c), :], place, all_send.at[c, k], all_recv.at[c, k], "seq", (f, g)[k])

    def own(c):
        return pltpu.make_async_copy(own_s.at[rows(c), :], everyone.at[me, rows(c), :], own_sem.at[c])

    def finish(c):
        total = sums(c)
        r = rows(c)
        if kind == "first":
            total = tokens[r, :].astype(F32) + total
            keep[r, :] = total
            own_s[r, :] = (total * root_scale(total) * gain[0:1, :]).astype(BF)
        elif kind == "second":
            back = rms_back(resid[r, :], gain[0:1, :], total)
            total = cot[r, :].astype(F32) * weight[0:1, 0:1] + back
            keep[r, :] = total
            own_s[r, :] = total.astype(BF)
        else:
            back = rms_back(tokens[r, :].astype(F32), gain[0:1, :], total)
            keep[r, :] = back
        if shares:
            share(c, 0).start()
            share(c, 1).start()
            own(c).start()

    def forward(c):
        share(c, 0).wait_recv()
        share(c, 2).start()

    start()
    for c in range(CHUNKS):
        middle(c)
        if kind == "third" and c == 0:

            @pl.loop(0, pairs)
            def _(k):
                near(k).wait()
                pair_out[k] = (gates[2 * k + side].astype(F32) + pair_s[k].astype(F32)).astype(BF)

            @pl.loop(1, pairs)
            def _(d):
                far(d).start()

        if c > 0:
            finish(c - 1)
        if shares and c > 1:
            forward(c - 2)
    finish(CHUNKS - 1)
    if shares:
        forward(CHUNKS - 2)
        forward(CHUNKS - 1)
    drain()
    if kind == "third":
        gates_sum[...] = gates[t].astype(F32) + pair_s[spot].astype(F32)

        @pl.loop(1, pairs)
        def _(d):
            far(d).wait()
            gates_sum[...] += far_s[lax.rem(spot - d + pairs, pairs)].astype(F32)

    if shares:
        for c in range(CHUNKS):
            for k in (1, 2):
                share(c, k).wait_recv()
            for k in (0, 1, 2):
                share(c, k).wait_send()
            own(c).wait()


def run_plane(kind, collective_id, part, *ins):
    S, L, D = part.shape
    dma = pltpu.SemaphoreType.DMA
    shares = kind in ("first", "second")
    outs = [shape((L, D))]
    specs = [VM]
    if shares:
        outs.append(shape((S, L, D), BF))
        specs.append(pl.BlockSpec(memory_space=pl.ANY))
    scratch = sum_scratch(L, D)
    if kind == "third":
        T, *slab = ins[-1].shape
        outs.append(shape(tuple(slab)))
        specs.append(VM)
        scratch += [pltpu.VMEM((T // 2, *slab), BF)] * 3 + [dma((T // 2,))] * 4
    if shares:
        scratch += [pltpu.VMEM((L, D), BF), dma((CHUNKS, 3)), dma((CHUNKS, 3)), dma((CHUNKS,))]
    return pl.pallas_call(
        functools.partial(plane_sum, kind, L, D),
        out_shape=tuple(outs),
        in_specs=[VM] * (1 + len(ins)),
        out_specs=tuple(specs),
        scratch_shapes=scratch,
        compiler_params=params(collective_id, 40),
        cost_estimate=pl.CostEstimate(
            flops=40 * L * D, bytes_accessed=20000000, transcendentals=L
        ),
    )(part, *ins)


def plane_swap(modes, *refs):
    n = len(modes)
    ins, outs = refs[:n], refs[n : 2 * n]
    send, recv, own_sem = refs[2 * n :]
    me = lax.axis_index("seq")
    S = lax.axis_size("seq")
    greet("seq", S, me)

    def copy(i, d):
        to = lax.rem(me + d, S)
        src = ins[i] if modes[i] == "all" else ins[i].at[to]
        return remote(src, outs[i].at[me], send.at[i, d], recv.at[i, d], "seq", to)

    def own(i):
        src = ins[i] if modes[i] == "all" else ins[i].at[me]
        return pltpu.make_async_copy(src, outs[i].at[me], own_sem.at[i])

    for i in range(n):
        for d in range(1, S):
            copy(i, d).start()
        own(i).start()
    for i in range(n):
        for d in range(1, S):
            copy(i, d).wait()
        own(i).wait()


def run_swap(S, modes, collective_id, *ins):
    n = len(modes)
    dma = pltpu.SemaphoreType.DMA
    outs = tuple(shape(((S,) if m == "all" else ()) + x.shape, x.dtype) for m, x in zip(modes, ins))
    size = sum(3 * x.size * x.dtype.itemsize // (1 if m == "all" else S) for m, x in zip(modes, ins))
    hbm = pl.BlockSpec(memory_space=pl.ANY)
    return pl.pallas_call(
        functools.partial(plane_swap, modes),
        out_shape=outs,
        in_specs=[hbm] * n,
        out_specs=(hbm,) * n,
        scratch_shapes=[dma((n, S)), dma((n, S)), dma((n,))],
        compiler_params=params(collective_id, 4),
        cost_estimate=pl.CostEstimate(flops=0, bytes_accessed=size * 40, transcendentals=0),
    )(*ins)


def plane_fill(S, T, slabs, *refs):
    pack, gates, pack_out, gates_out, lent = refs[:5]
    pack_send, pack_recv, gate_send, gate_recv, relay_send, relay_recv, lent_send, lent_recv, own_sem = refs[5:]
    me, t = lax.axis_index("seq"), lax.axis_index("tok")
    px, py, pd = flip(me, 1), flip(me, 2), S - 1 - me
    barrier = pltpu.get_barrier_semaphore()
    for peer in (px, py, pd):
        pl.semaphore_signal(barrier, inc=1, device_id={"seq": peer}, device_id_type=MESH)

    @pl.loop(1, T // 2)
    def _(d):
        pl.semaphore_signal(barrier, inc=1, device_id={"tok": lax.rem(t + 2 * d, T)}, device_id_type=MESH)

    mate = flip(t, 1)
    pl.semaphore_signal(barrier, inc=1, device_id={"tok": mate}, device_id_type=MESH)
    pl.semaphore_wait(barrier, S - 1 + T // 2)

    def gate(d):
        return remote(gates, gates_out.at[t], gate_send.at[d], gate_recv.at[d], "tok", lax.rem(t + 2 * d, T))

    def relay(d):
        place = gates_out.at[lax.rem(t - 2 * d + T, T)]
        return remote(place, place, relay_send.at[d], relay_recv.at[d], "tok", mate)

    def piece(k):
        to = (pd, px, py)[k]
        return remote(pack.at[to], pack_out.at[me], pack_send.at[k], pack_recv.at[k], "seq", to)

    mine = [
        pltpu.make_async_copy(pack.at[me], pack_out.at[me], own_sem.at[0]),
        pltpu.make_async_copy(gates, gates_out.at[t], own_sem.at[1]),
    ]
    loan = remote(gates_out.at[pl.ds(0, slabs)], lent, lent_send, lent_recv, "seq", px)

    @pl.loop(1, T // 2)
    def _(d):
        gate(d).start()

    for copy in mine:
        copy.start()
    for k in range(3):
        piece(k).start()
    mine[1].wait()
    relay(0).start()

    @pl.loop(1, T // 2)
    def _(d):
        gate(d).wait_recv()
        relay(d).start()

    @pl.loop(0, T // 2)
    def _(d):
        relay(d).wait_recv()

    @pl.when(lax.rem(me, 2) == 1)
    def _():
        loan.start()

    for k in range(3):
        piece(k).wait()
    mine[0].wait()

    @pl.loop(1, T // 2)
    def _(d):
        gate(d).wait_send()

    @pl.loop(0, T // 2)
    def _(d):
        relay(d).wait_send()

    @pl.when(lax.rem(me, 2) == 1)
    def _():
        loan.wait_send()

    @pl.when(lax.rem(me, 2) == 0)
    def _():
        loan.wait_recv()


def run_fill(S, T, slabs, collective_id, pack, gates):
    dma = pltpu.SemaphoreType.DMA
    hbm = pl.BlockSpec(memory_space=pl.ANY)
    return pl.pallas_call(
        functools.partial(plane_fill, S, T, slabs),
        out_shape=(
            shape(pack.shape, BF),
            shape((T,) + gates.shape, BF),
            shape((slabs,) + gates.shape, BF),
        ),
        in_specs=[hbm] * 2,
        out_specs=(hbm,) * 3,
        scratch_shapes=[dma((3,))] * 2 + [dma((T // 2,))] * 4 + [dma, dma, dma((2,))],
        compiler_params=params(collective_id, 4),
        cost_estimate=pl.CostEstimate(flops=0, bytes_accessed=80000000, transcendentals=0),
    )(pack, gates)


def plane_rows(S, L, first, out, send, recv, own_sem):
    me = lax.axis_index("seq")
    barrier = pltpu.get_barrier_semaphore()
    for bit in (1, 2):
        pl.semaphore_signal(barrier, inc=1, device_id={"seq": flip(me, bit)}, device_id_type=MESH)
    pl.semaphore_wait(barrier, 2)
    start, forward, drain = gather_rows(L, first, out, send, recv)
    own = pltpu.make_async_copy(first, out.at[me], own_sem)
    start()
    own.start()
    forward()
    drain()
    own.wait()


def run_rows(S, collective_id, first):
    dma = pltpu.SemaphoreType.DMA
    hbm = pl.BlockSpec(memory_space=pl.ANY)
    return pl.pallas_call(
        functools.partial(plane_rows, S, first.shape[0]),
        out_shape=shape((S,) + first.shape, BF),
        in_specs=[hbm],
        out_specs=hbm,
        scratch_shapes=[dma((CHUNKS, 3)), dma((CHUNKS, 3)), dma],
        compiler_params=params(collective_id, 4),
        cost_estimate=pl.CostEstimate(flops=0, bytes_accessed=140000000, transcendentals=0),
    )(first)


def after(value, *others):
    return lax.optimization_barrier((value,) + others)[0]


def body(
    tokens,
    source_ids,
    loss_weights,
    grad_output,
    first_gain,
    input_weight,
    gelu_weight,
    conv_weight,
    conv_bias,
    decay_gate,
    decay_bias,
    input_gate,
    input_bias,
    decay_param,
    output_weight,
    second_gain,
    gate_weight,
    up_weight,
    down_weight,
):
    S, T = lax.axis_size("seq"), lax.axis_size("tok")
    me = lax.axis_index("seq")
    length, D = tokens.shape[1:]
    ds, R = input_weight.shape
    rs = output_weight.shape[0]
    F = gate_weight.shape[1]
    FQ = F // S
    heads = R // BW
    starts = [-(-i * heads // S) for i in range(S + 1)]
    C = max(starts[i + 1] - starts[i] for i in range(S)) * BW
    quarter = R // S
    offs = [starts[i] * BW - i * quarter for i in range(S)] + [0]
    most = max(offs)
    off = sum(jnp.where(me == i, offs[i], 0) for i in range(S))
    own = sum(jnp.where(me == i, (starts[i + 1] - starts[i]) * BW, 0) for i in range(S))

    def cols_for(w):
        parts = [w[:, starts[i] * BW : starts[i + 1] * BW] for i in range(S)]
        return jnp.stack([jnp.pad(p, ((0, 0), (0, C - p.shape[1]))) for p in parts])

    def d_rows(w):
        return lax.all_gather(w, "tok", axis=1, tiled=True).reshape((D, w.shape[-1]))

    def d_scatter(g):
        return lax.psum_scatter(g.reshape(S, T * ds, g.shape[-1]), "tok", scatter_dimension=1, tiled=True)

    def r_align(g):
        g = lax.dynamic_update_slice_in_dim(jnp.zeros((quarter + 2 * most, g.shape[1]), BF), g.astype(BF), off, axis=0)
        back = from_behind(g[quarter : quarter + most], "seq", 1)
        keep = lax.broadcasted_iota(jnp.int32, (quarter, 1), 0) < off
        return jnp.where(keep, jnp.pad(back, ((0, quarter - most), (0, 0))), g[:quarter])

    small = jnp.concatenate(
        [conv_weight, jnp.stack([conv_bias, decay_bias, input_bias, decay_param], axis=1)], axis=1
    )
    gains = jnp.pad(jnp.stack([first_gain, second_gain], axis=1), ((0, 0), (0, SMALL - 2)))
    pack_in = jnp.concatenate([cols_for(input_weight), cols_for(gelu_weight)], axis=2)
    pack_in, gains = run_swap(S, ("slice", "all"), 2, pack_in, gains)
    gains = jnp.pad(gains[:, :, :2].transpose(1, 0, 2).reshape(ds, 2 * S), ((0, rs - ds), (0, 0)))
    small = jnp.concatenate([small, gains], axis=1)
    small = jnp.pad(small, ((0, 0), (0, SMALL - small.shape[1])))
    gates = jnp.concatenate([decay_gate, input_gate, small], axis=1)
    sources = lax.broadcasted_iota(jnp.int32, (1, loss_weights.shape[0]), 1)
    picked = jnp.sum(jnp.where(source_ids[:, None] == sources, loss_weights[None, :], 0.0), axis=1)
    cot_low = (grad_output[0].astype(F32) * picked[:, None]).astype(BF)
    pack_f = jnp.concatenate([w.reshape(ds, S, FQ).swapaxes(0, 1) for w in (gate_weight, up_weight)], axis=2)
    weight_out = gather(output_weight, "tok")
    pack_f, gates, lent = run_fill(S, T, -(-most // rs), 3, after(pack_f, pack_in), gates)
    everyone = run_rows(S, 8, after(tokens[0], pack_f, weight_out))

    def r_rows(whole, lent):
        lent = lent[:most]
        whole = jnp.concatenate([whole, lent, jnp.zeros_like(lent)], axis=0)
        whole = lax.dynamic_slice_in_dim(whole, off, C, axis=0)
        return jnp.where(lax.broadcasted_iota(jnp.int32, whole.shape, 0) < own, whole, 0)

    pack_in = d_rows(pack_in)
    weight_xy = pack_in[:, : 2 * C]
    gains = gates[:, :ds, 2 * BW + 8 : 2 * BW + 8 + 2 * S].reshape(T, ds, S, 2).transpose(3, 2, 0, 1)
    gain_one, gain_two = gains.reshape(2, D).astype(F32)
    gates = r_rows(gates.reshape(quarter, -1), lent.reshape(-1, lent.shape[-1]))
    weight_decay, weight_input = gates[:, :BW], gates[:, BW : 2 * BW]
    rows = gates[:, 2 * BW : 2 * BW + 8].T.astype(F32)
    param = rows[7:8]
    rows = jnp.concatenate(
        [rows, 8.0 * jax.nn.softplus(param), jax.nn.sigmoid(param), jnp.zeros((6, C), F32)], axis=0
    )
    weight_out = r_rows(weight_out, from_behind(weight_out[:most], "seq", -1))

    everyone = everyone.astype(F32)
    normed = lax.optimization_barrier(rms_scale(everyone, gain_one).astype(BF))
    ready = (pack_f, normed, rows, weight_decay, weight_input, weight_out)
    pack_f, normed, rows, weight_decay, weight_input, weight_out = lax.optimization_barrier(ready)
    pack_f, weight_xy = lax.optimization_barrier((pack_f, weight_xy))
    pack_f = d_rows(pack_f)
    weight_gate, weight_up = pack_f[:, :FQ], pack_f[:, FQ:]
    branches = forward_product(normed, weight_xy)
    weight_down = gather(after(down_weight, branches), "tok")
    mixed, mixed_own, states, conv_low, branch_x, halo, incoming, cot_low = run_forward(
        T, quarter, branches, rows, weight_decay, weight_input, cot_low
    )
    mixed, mixed_own = mixed.reshape(S, length, C), mixed_own.reshape(S, length, quarter)
    part = forward_product(mixed, weight_out).astype(BF)
    resid, second_normed = run_plane("first", 4, part, tokens[0], gain_two[None])

    gate_val = forward_product(second_normed, weight_gate)
    up_val = forward_product(second_normed, weight_up)
    hidden = gelu_product(gate_val, up_val).astype(BF)
    grad_down = token_product(hidden, cot_low).astype(BF)
    weight_down = after(weight_down, grad_down)
    grad_down = scatter(grad_down, "tok")

    grad_hidden = back_product(cot_low, weight_down)
    _, hidden_pull = jax.vjp(gelu_product, gate_val, up_val)
    grad_gate_val, grad_up_val = hidden_pull(grad_hidden)
    grad_gate_up = jnp.concatenate([grad_gate_val.astype(BF), grad_up_val.astype(BF)], axis=2)
    grad_pack = token_product(second_normed, grad_gate_up).astype(BF)
    grad_second = back_product(after(grad_gate_up, grad_pack), pack_f)
    grad_second = grad_second.astype(BF)
    grad_pack = d_scatter(grad_pack)
    picked = jnp.broadcast_to(picked[None], (8, 128))
    grad_resid, resid_low = run_plane(
        "second", 6, grad_second, resid, gain_two[None], grad_output[0], picked
    )

    grad_out_w = token_product(mixed_own, after(resid_low, grad_down)).astype(BF)
    grad_mixed = back_product(after(resid_low, grad_out_w), weight_out)
    grad_out_w = scatter(grad_out_w, "tok")
    part = forward_product(hidden, weight_down).astype(BF)
    grad_xy, grad_decay_w, grad_input_w, smalls, block_out = run_backward(
        T, grad_mixed.reshape(S * length, C), branches, states, conv_low, branch_x, halo, incoming, rows,
        weight_decay, weight_input, part,
    )
    block_out = (resid + block_out).astype(BF)
    grad_i = token_product(normed, after(grad_xy, grad_pack)).astype(BF)
    smalls = jnp.pad(smalls.T, ((0, 0), (0, SMALL - 8)))
    grad_r = r_align(after(jnp.concatenate([grad_decay_w, grad_input_w, smalls], axis=1), grad_i))
    grad_normed = back_product(after(grad_xy, grad_i), weight_xy)
    grad_normed = after(grad_normed, grad_out_w)

    grad_i = d_scatter(grad_i)
    grad_tokens, grad_r = run_plane(
        "third", 7, grad_normed.astype(BF), tokens[0], gain_one[None], grad_r.reshape(T, rs, -1)
    )
    grad_tokens = grad_resid + grad_tokens
    grad_pack = to_seq(grad_pack).swapaxes(0, 1).astype(F32)
    grad_gate_w = grad_pack[:, :, :FQ].reshape(ds, F)
    grad_up_w = grad_pack[:, :, FQ:].reshape(ds, F)
    grad_down, grad_out_w = grad_down.astype(F32), grad_out_w.astype(F32)

    def gain_grad(gain, *pairs):
        return sum(jnp.sum(w.astype(F32) * g, axis=1) for w, g in pairs) / gain.astype(F32)

    grad_gain_two = gain_grad(second_gain, (gate_weight, grad_gate_w), (up_weight, grad_up_w))
    early = (block_out, grad_tokens, grad_r, grad_down, grad_out_w, grad_gate_w, grad_up_w, grad_gain_two)
    grad_i, *early = lax.optimization_barrier((grad_i,) + early)
    block_out, grad_tokens, grad_r, grad_down, grad_out_w, grad_gate_w, grad_up_w, grad_gain_two = early
    grad_i = to_seq(grad_i).astype(F32)

    def columns(at):
        return jnp.concatenate(
            [grad_i[i, :, at : at + (starts[i + 1] - starts[i]) * BW] for i in range(S)], axis=1
        )

    grad_in_w, grad_gelu_w = columns(0), columns(C)

    smalls = grad_r[:, 2 * BW :]
    return (
        block_out[None],
        grad_tokens[None],
        gain_grad(first_gain, (input_weight, grad_in_w), (gelu_weight, grad_gelu_w)),
        grad_in_w,
        grad_gelu_w,
        smalls[:, :CONV],
        smalls[:, 4],
        grad_r[:, :BW],
        smalls[:, 5],
        grad_r[:, BW : 2 * BW],
        smalls[:, 6],
        smalls[:, 7],
        grad_out_w,
        grad_gain_two,
        grad_gate_w,
        grad_up_w,
        grad_down,
    )


def solution(mesh):
    one, two = P(("seq", "tok")), P(("seq", "tok"), None)
    data = P("seq", "tok", None)
    return jax.shard_map(
        body,
        mesh=mesh,
        in_specs=(data, P("seq"), P(), data, one, two, two, two, one, two, one, two, one, one, two, one, two, two, two),
        out_specs=(data, data, one, two, two, two, one, two, one, two, one, one, two, one, two, two, two),
        check_vma=False,
    )
```
